128 devices in a mesh: dp: 16 (over y, x_hi, core), tensor: 8 (over z, x_lo).
Axes of the slice: x: 4 (x_hi: 2, x_lo: 2; x = x_hi * 2 + x_lo), y: 4, z: 4, core: 2. Of those that a mesh axis runs over, the one named last changes fastest.
Arguments:
- hidden_in: bfloat16 [16, 1024, 2048], P('dp', 'tensor'), may hold values from -6 to 6
- segment_ids: int32 [16, 1024], P('dp'), may hold values from 0 to 2, as said below
- attention_gain: bfloat16 [2048], replicated, may hold values from 0.5 to 2
- mlp_gain: bfloat16 [2048], replicated, may hold values from 0.5 to 2
- query_base: bfloat16 [2048, 2048], P(None, 'tensor'), may hold values from -0.125 to 0.125
- query_left: float32 [2048, 16], replicated, may hold values from -0.125 to 0.125
- query_right: float32 [16, 2048], P(None, 'tensor'), may hold values from -0.3 to 0.3
- query_magnitude: float32 [2048], P('tensor'), may hold values from 0.5 to 2
- key_base: bfloat16 [2048, 2048], P(None, 'tensor'), may hold values from -0.125 to 0.125
- key_left: float32 [2048, 16], replicated, may hold values from -0.125 to 0.125
- key_right: float32 [16, 2048], P(None, 'tensor'), may hold values from -0.3 to 0.3
- key_magnitude: float32 [2048], P('tensor'), may hold values from 0.5 to 2
- value_base: bfloat16 [2048, 2048], P(None, 'tensor'), may hold values from -0.125 to 0.125
- value_left: float32 [2048, 16], replicated, may hold values from -0.125 to 0.125
- value_right: float32 [16, 2048], P(None, 'tensor'), may hold values from -0.3 to 0.3
- value_magnitude: float32 [2048], P('tensor'), may hold values from 0.5 to 2
- output_base: bfloat16 [2048, 2048], P('tensor'), may hold values from -0.125 to 0.125
- output_left: float32 [2048, 16], P('tensor'), may hold values from -0.125 to 0.125
- output_right: float32 [16, 2048], replicated, may hold values from -0.3 to 0.3
- output_magnitude: float32 [2048], replicated, may hold values from 3 to 12
- gate_base: bfloat16 [2048, 5632], P(None, 'tensor'), may hold values from -0.125 to 0.125
- gate_left: float32 [2048, 16], replicated, may hold values from -0.125 to 0.125
- gate_right: float32 [16, 5632], P(None, 'tensor'), may hold values from -0.3 to 0.3
- gate_magnitude: float32 [5632], P('tensor'), may hold values from 0.5 to 2
- up_base: bfloat16 [2048, 5632], P(None, 'tensor'), may hold values from -0.125 to 0.125
- up_left: float32 [2048, 16], replicated, may hold values from -0.125 to 0.125
- up_right: float32 [16, 5632], P(None, 'tensor'), may hold values from -0.3 to 0.3
- up_magnitude: float32 [5632], P('tensor'), may hold values from 0.5 to 2
- down_base: bfloat16 [5632, 2048], P('tensor'), may hold values from -0.078125 to 0.078125
- down_left: float32 [5632, 16], P('tensor'), may hold values from -0.078125 to 0.078125
- down_right: float32 [16, 2048], replicated, may hold values from -0.3 to 0.3
- down_magnitude: float32 [2048], replicated, may hold values from 1 to 4
- cotangent: bfloat16 [16, 1024, 2048], P('dp', 'tensor'), may hold values from -6 to 6
Outputs:
- layer_out: bfloat16 [16, 1024, 2048], P('dp', 'tensor')
- input_grad: float32 [16, 1024, 2048], P('dp', 'tensor')
- query_left_grad: float32 [2048, 16], replicated
- query_right_grad: float32 [16, 2048], P(None, 'tensor')
- query_magnitude_grad: float32 [2048], P('tensor')
- key_left_grad: float32 [2048, 16], replicated
- key_right_grad: float32 [16, 2048], P(None, 'tensor')
- key_magnitude_grad: float32 [2048], P('tensor')
- value_left_grad: float32 [2048, 16], replicated
- value_right_grad: float32 [16, 2048], P(None, 'tensor')
- value_magnitude_grad: float32 [2048], P('tensor')
- output_left_grad: float32 [2048, 16], P('tensor')
- output_right_grad: float32 [16, 2048], replicated
- output_magnitude_grad: float32 [2048], replicated
- gate_left_grad: float32 [2048, 16], replicated
- gate_right_grad: float32 [16, 5632], P(None, 'tensor')
- gate_magnitude_grad: float32 [5632], P('tensor')
- up_left_grad: float32 [2048, 16], replicated
- up_right_grad: float32 [16, 5632], P(None, 'tensor')
- up_magnitude_grad: float32 [5632], P('tensor')
- down_left_grad: float32 [5632, 16], P('tensor')
- down_right_grad: float32 [16, 2048], replicated
- down_magnitude_grad: float32 [2048], replicated
The draws below stay inside these ranges and needn't reach their ends.
Inputs may be any that keep to these rules, and one draw needn't show every extreme that they name: `segment_ids`: each row holds three documents numbered 0, 1, 2 in order; document 1 begins within the first 128 positions, after position 0, and ends within the last 128 positions, before the last one.
All inputs are finite; a program needn't handle non-finite values.
Results may differ from the reference program's by a relative error of at most 0.03.
Values may be sent and summed in bfloat16 or wider, within the bound.
No kernel may reach another device: no remote copies, remote signals or barrier semaphores. Data moves between devices by JAX's collectives and lax.ppermute only.
A program may use at most 256 MiB of HBM per device.

```python
import math
import jax
import jax.numpy as jnp
from jax import lax

D = 2048
HEADS = 16
HEAD_DIM = 128
FF = 5632
RANK = 16
ALPHA = 32
SEQ = 1024
SEQ_LOC = 128
ROWS = 16


def draw_segment_ids(key, part):
    key = jax.random.fold_in(key, 11)
    first_key, last_key = jax.random.split(key)
    opening = jax.random.randint(first_key, (ROWS, 1), 1, SEQ_LOC)
    closing = jax.random.randint(last_key, (ROWS, 1), SEQ - SEQ_LOC + 1, SEQ)
    index = jnp.arange(SEQ, dtype=jnp.int32)[None, :]
    return (index >= opening).astype(jnp.int32) + (index >= closing).astype(jnp.int32)


def levels(own_key, dims, cuts, smallest, high):
    level = 1.0
    for axis_at, parts in cuts:
        steps = jax.random.uniform(jax.random.fold_in(jax.random.fold_in(own_key, 6), axis_at), (parts,), jnp.float32, smallest / len(cuts), high / len(cuts))
        level = level * jnp.repeat(jnp.exp(steps), dims[axis_at] // parts).reshape((-1,) + (1,) * (len(dims) - 1 - axis_at))
    return level


def gaussian(stream_key, shape, scale, most, cuts=(), held_as=jnp.bfloat16):
    values = jax.random.normal(stream_key, shape, jnp.float32) * scale
    if len(cuts) > 0:
        values = levels(stream_key, shape, cuts, -0.22, 0.18) * values
    return jnp.clip(values, min=-most, max=most).astype(held_as)


def setup_inputs(seed: int = 0) -> dict:
    seeds = jax.random.split(jax.random.key(seed), 34)
    hidden_in = gaussian(seeds[0], (ROWS, SEQ, D), 1.0, 6.0, ((0, 16), (1, 8)))
    segment_ids = draw_segment_ids(jax.random.fold_in(seeds[33], 71), 0)
    attention_gain = jnp.clip(jnp.exp(jax.random.uniform(seeds[2], (D,), jnp.float32, math.log(0.5), math.log(2.0))), 0.5, 2.0).astype(jnp.bfloat16)
    mlp_gain = jnp.clip(jnp.exp(jax.random.uniform(seeds[3], (D,), jnp.float32, math.log(0.5), math.log(2.0))), 0.5, 2.0).astype(jnp.bfloat16)
    query_base = gaussian(seeds[4], (D, D), D ** -0.5, 0.125, ((1, 8),))
    query_left = gaussian(seeds[5], (D, RANK), D ** -0.5, 0.125, (), jnp.float32)
    query_right = gaussian(seeds[6], (RANK, D), 0.05, 0.3, ((1, 8),), jnp.float32)
    query_magnitude = jnp.clip(jnp.exp(math.log(2.0) - 1.3862944 * jax.random.uniform(seeds[7], (D,), jnp.float32) ** levels(seeds[7], (D,), ((0, 8),), -0.2, 0.2)), 0.5, 2.0)
    key_base = gaussian(seeds[8], (D, D), D ** -0.5, 0.125, ((1, 8),))
    key_left = gaussian(seeds[9], (D, RANK), D ** -0.5, 0.125, (), jnp.float32)
    key_right = gaussian(seeds[10], (RANK, D), 0.05, 0.3, ((1, 8),), jnp.float32)
    key_magnitude = jnp.clip(jnp.exp(math.log(2.0) - 1.3862944 * jax.random.uniform(seeds[11], (D,), jnp.float32) ** levels(seeds[11], (D,), ((0, 8),), -0.2, 0.2)), 0.5, 2.0)
    value_base = gaussian(seeds[12], (D, D), D ** -0.5, 0.125, ((1, 8),))
    value_left = gaussian(seeds[13], (D, RANK), D ** -0.5, 0.125, (), jnp.float32)
    value_right = gaussian(seeds[14], (RANK, D), 0.05, 0.3, ((1, 8),), jnp.float32)
    value_magnitude = jnp.clip(jnp.exp(math.log(2.0) - 1.3862944 * jax.random.uniform(seeds[15], (D,), jnp.float32) ** levels(seeds[15], (D,), ((0, 8),), -0.2, 0.2)), 0.5, 2.0)
    output_base = gaussian(seeds[16], (D, D), D ** -0.5, 0.125, ((0, 8),))
    output_left = gaussian(seeds[17], (D, RANK), D ** -0.5, 0.125, ((0, 8),), jnp.float32)
    output_right = gaussian(seeds[18], (RANK, D), 0.05, 0.3, (), jnp.float32)
    output_magnitude = jnp.clip(jnp.exp(jax.random.uniform(seeds[19], (D,), jnp.float32, math.log(3.0), math.log(12.0))), 3.0, 12.0)
    gate_base = gaussian(seeds[20], (D, FF), D ** -0.5, 0.125, ((1, 8),))
    gate_left = gaussian(seeds[21], (D, RANK), D ** -0.5, 0.125, (), jnp.float32)
    gate_right = gaussian(seeds[22], (RANK, FF), 0.05, 0.3, ((1, 8),), jnp.float32)
    gate_magnitude = jnp.clip(jnp.exp(math.log(2.0) - 1.3862944 * jax.random.uniform(seeds[23], (FF,), jnp.float32) ** levels(seeds[23], (FF,), ((0, 8),), -0.2, 0.2)), 0.5, 2.0)
    up_base = gaussian(seeds[24], (D, FF), D ** -0.5, 0.125, ((1, 8),))
    up_left = gaussian(seeds[25], (D, RANK), D ** -0.5, 0.125, (), jnp.float32)
    up_right = gaussian(seeds[26], (RANK, FF), 0.05, 0.3, ((1, 8),), jnp.float32)
    up_magnitude = jnp.clip(jnp.exp(math.log(2.0) - 1.3862944 * jax.random.uniform(seeds[27], (FF,), jnp.float32) ** levels(seeds[27], (FF,), ((0, 8),), -0.2, 0.2)), 0.5, 2.0)
    down_base = gaussian(seeds[28], (FF, D), FF ** -0.5, 0.078125, ((0, 8),))
    down_left = gaussian(seeds[29], (FF, RANK), FF ** -0.5, 0.078125, ((0, 8),), jnp.float32)
    down_right = gaussian(seeds[30], (RANK, D), 0.05, 0.3, (), jnp.float32)
    down_magnitude = jnp.clip(jnp.exp(jax.random.uniform(seeds[31], (D,), jnp.float32, math.log(1.0), math.log(4.0))), 1.0, 4.0)
    cotangent = gaussian(seeds[32], (ROWS, SEQ, D), 1.0, 6.0, ((0, 16), (1, 8)))
    return {"hidden_in": hidden_in, "segment_ids": segment_ids, "attention_gain": attention_gain, "mlp_gain": mlp_gain, "query_base": query_base, "query_left": query_left, "query_right": query_right, "query_magnitude": query_magnitude, "key_base": key_base, "key_left": key_left, "key_right": key_right, "key_magnitude": key_magnitude, "value_base": value_base, "value_left": value_left, "value_right": value_right, "value_magnitude": value_magnitude, "output_base": output_base, "output_left": output_left, "output_right": output_right, "output_magnitude": output_magnitude, "gate_base": gate_base, "gate_left": gate_left, "gate_right": gate_right, "gate_magnitude": gate_magnitude, "up_base": up_base, "up_left": up_left, "up_right": up_right, "up_magnitude": up_magnitude, "down_base": down_base, "down_left": down_left, "down_right": down_right, "down_magnitude": down_magnitude, "cotangent": cotangent}


EPSILON = 1e-05
MASKED_SCORE = -1e+30
HIGHEST_PRECISION = lax.Precision.HIGHEST

@jax.custom_vjp
def low(v):
    return lax.optimization_barrier(v.astype(jnp.bfloat16)).astype(jnp.float32)

@jax.custom_vjp
def low_back(v):
    return v

def low_keep(v):
    return (low(v), None)

def low_pass(kept, grad):
    return (grad,)

def back_keep(v):
    return (v, None)

def back_low(kept, grad):
    return (low(grad),)
low.defvjp(low_keep, low_pass)
low_back.defvjp(back_keep, back_low)

def precise(left_side, right_side):
    return jnp.dot(left_side, right_side, precision=HIGHEST_PRECISION)

def adapted(inputs, base, adapter):
    left, right, magnitude = adapter
    factor = ALPHA / RANK
    weight = base + factor * precise(left, right)
    column_norm = jnp.sqrt(lax.optimization_barrier(jnp.sum(weight * weight, axis=0)))
    raw = precise(inputs, base) + factor * precise(precise(inputs, left), right)
    return low_back(raw) * (magnitude / column_norm)

def normalize(values, gain):
    return values * lax.rsqrt(lax.optimization_barrier(jnp.mean(values * values, axis=-1, keepdims=True)) + EPSILON) * gain

def rotate_half(values):
    middle = values.shape[-1] // 2
    return jnp.concatenate([-values[..., middle:], values[..., :middle]], axis=-1)

def rotary_tables(segments):
    length = segments.shape[0]
    index = jnp.arange(length, dtype=jnp.int32)
    change = jnp.concatenate([jnp.ones((1,), dtype=bool), segments[1:] != segments[:-1]])
    starts = lax.cummax(jnp.where(change, index, 0), axis=0)
    positions = (index - starts).astype(jnp.float32)
    frequency = 10000.0 ** (-jnp.arange(0, HEAD_DIM, 2, dtype=jnp.float32) / HEAD_DIM)
    angles = positions[:, None] * frequency[None, :]
    cosine = jnp.concatenate([jnp.cos(angles), jnp.cos(angles)], axis=-1)[:, None, :]
    sine_table = jnp.concatenate([jnp.sin(angles), jnp.sin(angles)], axis=-1)[:, None, :]
    return (cosine, sine_table)

def layer_row(resid, segments, frozen, trained):
    attention_gain, mlp_gain, query_base, key_base, value_base, output_base, gate_base, up_base, down_base = frozen
    query, key_params, value_params, output, gate, upward, downward = trained
    length = resid.shape[0]
    cosine, sine_table = rotary_tables(segments)
    normed = low(normalize(resid, attention_gain))
    queries = adapted(normed, query_base, query).reshape(length, HEADS, HEAD_DIM)
    keys = adapted(normed, key_base, key_params).reshape(length, HEADS, HEAD_DIM)
    values = low(adapted(normed, value_base, value_params).reshape(length, HEADS, HEAD_DIM))
    queries = low(queries * cosine + rotate_half(queries) * sine_table)
    keys = low(keys * cosine + rotate_half(keys) * sine_table)
    index = jnp.arange(length, dtype=jnp.int32)
    allowed = (segments[:, None] == segments[None, :]) & (index[None, :] <= index[:, None])
    scores = low_back(jnp.einsum('qhd,khd->hqk', queries, keys, precision=HIGHEST_PRECISION)) * HEAD_DIM ** (-0.5)
    scores = jnp.where(allowed[None], scores, MASKED_SCORE)
    largest = lax.optimization_barrier(jnp.max(scores, axis=-1, keepdims=True))
    weights = jnp.exp(scores - largest)
    probabilities = weights / lax.optimization_barrier(jnp.sum(weights, axis=-1, keepdims=True))
    attended = jnp.einsum('hqk,khd->qhd', low(probabilities), values, precision=HIGHEST_PRECISION)
    attended = low(low_back(attended)).reshape(length, HEADS * HEAD_DIM)
    resid_two = resid + adapted(attended, output_base, output)
    normed_two = low(normalize(resid_two, mlp_gain))
    gate_value = adapted(normed_two, gate_base, gate)
    up_value = adapted(normed_two, up_base, upward)
    activated = low(jax.nn.silu(gate_value) * up_value)
    return resid_two + adapted(activated, down_base, downward)

def reference(hidden_in, segment_ids, attention_gain, mlp_gain, query_base, query_left, query_right, query_magnitude, key_base, key_left, key_right, key_magnitude, value_base, value_left, value_right, value_magnitude, output_base, output_left, output_right, output_magnitude, gate_base, gate_left, gate_right, gate_magnitude, up_base, up_left, up_right, up_magnitude, down_base, down_left, down_right, down_magnitude, cotangent):
    frozen = (attention_gain.astype(jnp.float32), mlp_gain.astype(jnp.float32), query_base.astype(jnp.float32), key_base.astype(jnp.float32), value_base.astype(jnp.float32), output_base.astype(jnp.float32), gate_base.astype(jnp.float32), up_base.astype(jnp.float32), down_base.astype(jnp.float32))
    trained = ((query_left, query_right, query_magnitude), (key_left, key_right, key_magnitude), (value_left, value_right, value_magnitude), (output_left, output_right, output_magnitude), (gate_left, gate_right, gate_magnitude), (up_left, up_right, up_magnitude), (down_left, down_right, down_magnitude))
    zeros = jax.tree.map(jnp.zeros_like, trained)

    def one_row(totals, row_inputs):
        resid, segments, row_cotangent = row_inputs

        def layer_of(resid_in, params):
            return layer_row(resid_in, segments, frozen, params)
        result, pullback = jax.vjp(layer_of, resid.astype(jnp.float32), trained)
        grad_resid, grad_trained = pullback(row_cotangent.astype(jnp.float32))
        return (jax.tree.map(jnp.add, totals, grad_trained), (result.astype(jnp.bfloat16), grad_resid))
    totals, outputs = lax.scan(one_row, zeros, (hidden_in, segment_ids, cotangent))
    layer_out, input_grad = outputs
    return (layer_out, input_grad, totals[0][0], totals[0][1], totals[0][2], totals[1][0], totals[1][1], totals[1][2], totals[2][0], totals[2][1], totals[2][2], totals[3][0], totals[3][1], totals[3][2], totals[4][0], totals[4][1], totals[4][2], totals[5][0], totals[5][1], totals[5][2], totals[6][0], totals[6][1], totals[6][2])
```

```python
import jax
import jax.numpy as jnp
from jax import lax
from jax.experimental import pallas as pl
from jax.experimental.pallas import tpu as pltpu
from jax.sharding import Mesh
from jax.sharding import PartitionSpec as P

HEAD_DIM = 128
RANK = 16
ALPHA = 32
FACTOR = ALPHA / RANK
EPSILON = 1e-05
MASKED_SCORE = -1e30
DP = ("y", "xh", "core")
TENSOR = ("z", "xl")
ALL = DP + TENSOR
BF16 = jnp.bfloat16
F32 = jnp.float32

SWAP = ((0, 1), (1, 0))
UP = tuple((i, (i + 1) % 4) for i in range(4))
DOWN = tuple((i, (i + 3) % 4) for i in range(4))
SLOTS = ((0, 0), (0, 1), (-1, 0), (1, 0), (-1, 1), (1, 1), (2, 0), (2, 1))
SLOT_AT = ((0, 1), (3, 5), (6, 7), (2, 4))


def z_up(array):
    return lax.ppermute(array, "z", UP)


def z_down(array):
    return lax.ppermute(array, "z", DOWN)


def x_swap(array):
    return lax.ppermute(array, "xl", SWAP)


def core_swap(array):
    return lax.ppermute(array, "core", SWAP)


def from_x_neighbour(array):
    pairs = []
    for x in range(4):
        for core in range(2):
            source = (x ^ 1) if core else (x + 3 if x % 2 == 0 else x + 1) % 4
            pairs.append(
                ((source // 2) * 4 + core * 2 + source % 2, (x // 2) * 4 + core * 2 + x % 2)
            )
    return lax.ppermute(array, ("xh", "core", "xl"), tuple(pairs))


def gather_row(own):
    other = x_swap(own)
    below, above = z_up(own), z_down(own)
    other_below, other_above = z_up(other), z_down(other)
    far = z_up(below)
    other_far = z_down(other_above)
    return [own, other, below, above, other_below, other_above, far, other_far]


def add(*terms):
    total = terms[0].astype(F32)
    for term in terms[1:]:
        total = total + term.astype(F32)
    return total


def scatter_row(parts):
    far = z_up(parts[6])
    other_far = z_down(parts[7])
    from_above = z_down(parts[2])
    other_from_below = z_up(parts[5])
    from_below = z_up(add(parts[3], far).astype(BF16))
    other_from_above = z_down(add(parts[4], other_far).astype(BF16))
    across = x_swap(add(parts[1], other_from_below, other_from_above).astype(BF16))
    return add(parts[0], from_below, from_above, across)


def gather_z(own):
    half = own.shape[0] // 2
    below, above = z_up(own), z_down(own)
    far_low = z_up(below[:half])
    far_high = z_down(above[half:])
    return jnp.concatenate([own, below, above, far_low, far_high], axis=0)


def scatter_z(total, rows):
    half = rows // 2
    own, below, above, far = (total[i * rows : (i + 1) * rows] for i in range(4))
    low = z_up(far[:half])
    high = z_down(far[half:])
    above_sum = jnp.concatenate([add(above[:half], low).astype(BF16), above[half:]], axis=0)
    below_sum = jnp.concatenate([below[:half], add(below[half:], high).astype(BF16)], axis=0)
    return add(own, z_up(above_sum), z_down(below_sum))


def all_to_all(array, axes):
    return lax.all_to_all(array, axes, 0, 0, tiled=True)


def of_everyone(array, axes):
    count = lax.axis_size(axes)
    return all_to_all(jnp.broadcast_to(array[None], (count, *array.shape)), axes)


def summed(arrays, axes):
    count = lax.axis_size(axes)
    flat = jnp.concatenate([a.astype(BF16).reshape(-1) for a in arrays])
    size = flat.shape[0]
    step = count * 128
    padded = (size + step - 1) // step * step
    flat = jnp.pad(flat, (0, padded - size)).reshape(count, padded // step, 128)
    part = all_to_all(flat, axes).astype(F32).sum(axis=0).astype(BF16)
    whole = of_everyone(part, axes).reshape(-1).astype(F32)
    sums, at = [], 0
    for a in arrays:
        sums.append(whole[at : at + a.size].reshape(a.shape))
        at += a.size
    return sums


def dot(left, right):
    return jnp.dot(left.astype(BF16), right.astype(BF16), preferred_element_type=F32)


def dot_nt(left, right):
    return lax.dot_general(
        left.astype(BF16), right.astype(BF16), (((1,), (1,)), ((), ())), preferred_element_type=F32
    )


def dot_tn(left, right):
    return lax.dot_general(
        left.astype(BF16), right.astype(BF16), (((0,), (0,)), ((), ())), preferred_element_type=F32
    )


def rms_forward(resid, gain):
    inverse = lax.rsqrt(jnp.mean(resid * resid, axis=-1, keepdims=True) + EPSILON)
    normal = resid * inverse
    return normal, inverse, (normal * gain.astype(F32)).astype(BF16)


def rms_backward(grad_normed, normal, inverse, gain):
    scaled = grad_normed * gain.astype(F32)
    return inverse * (scaled - normal * jnp.mean(scaled * normal, axis=-1, keepdims=True))


def rotate_half(values):
    middle = values.shape[-1] // 2
    return jnp.concatenate([-values[..., middle:], values[..., :middle]], axis=-1)


def adapted_weight(base, left, right):
    weight = base.astype(F32) + FACTOR * dot(left, right)
    return weight.astype(BF16), jnp.sum(weight * weight, axis=0)


VMEM = pl.BlockSpec(memory_space=pltpu.VMEM)
SMEM = pl.BlockSpec(memory_space=pltpu.SMEM)
QUERY_ROWS = 256
SCORE_SCALE = HEAD_DIM ** (-0.5)


def masked_scores(query, key, first_row, seg_rows, seg_cols):
    scores = lax.dot_general(
        query, key, (((1,), (1,)), ((), ())), preferred_element_type=F32
    ) * SCORE_SCALE
    row = first_row + lax.broadcasted_iota(jnp.int32, scores.shape, 0)
    column = lax.broadcasted_iota(jnp.int32, scores.shape, 1)
    allowed = (seg_rows == seg_cols) & (column <= row)
    return jnp.where(allowed, scores, MASKED_SCORE)


def attend_kernel(slot_ref, seg_row_ref, seg_col_ref, qkv_ref, out_ref, log_ref, held):
    length = held.shape[0]
    width = out_ref.shape[1]
    for block in range(length // 128):
        held[block * 128 : (block + 1) * 128, :] = qkv_ref[slot_ref[block]]
    for head in range(width // HEAD_DIM):
        at = slice(head * HEAD_DIM, (head + 1) * HEAD_DIM)
        key_at = slice(width + head * HEAD_DIM, width + (head + 1) * HEAD_DIM)
        value_at = slice(2 * width + head * HEAD_DIM, 2 * width + (head + 1) * HEAD_DIM)
        for first in range(0, length, QUERY_ROWS):
            last = first + QUERY_ROWS
            scores = masked_scores(
                held[first:last, at],
                held[:last, key_at],
                first,
                seg_row_ref[first:last, :],
                seg_col_ref[:, :last],
            )
            largest = jnp.max(scores, axis=-1, keepdims=True)
            weights = jnp.exp(scores - largest)
            totals = jnp.sum(weights, axis=-1, keepdims=True)
            probs = (weights * (1.0 / totals)).astype(BF16)
            out = jnp.dot(probs, held[:last, value_at], preferred_element_type=F32)
            out_ref[first:last, at] = out.astype(BF16)
            log_ref[first:last, at] = jnp.broadcast_to(
                largest + jnp.log(totals), (QUERY_ROWS, HEAD_DIM)
            )


def attend(slots, seg_rows, seg_cols, qkv):
    blocks, rows, width = qkv.shape
    length = blocks * rows
    return pl.pallas_call(
        attend_kernel,
        out_shape=(
            jax.ShapeDtypeStruct((length, width // 3), BF16),
            jax.ShapeDtypeStruct((length, width // 3), F32),
        ),
        in_specs=[SMEM, VMEM, VMEM, VMEM],
        out_specs=(VMEM, VMEM),
        scratch_shapes=[pltpu.VMEM((length, width), BF16)],
        compiler_params=pltpu.CompilerParams(vmem_limit_bytes=48 * 1024 * 1024),
        name="attend",
    )(slots, seg_rows, seg_cols, qkv)


def attend_back_kernel(
    slot_ref, seg_row_ref, seg_col_ref, qkv_ref, log_ref, grad_ref, out_ref, held, total
):
    length = held.shape[0]
    width = grad_ref.shape[1]
    for block in range(length // 128):
        held[block * 128 : (block + 1) * 128, :] = qkv_ref[slot_ref[block]]
    for head in range(width // HEAD_DIM):
        at = slice(head * HEAD_DIM, (head + 1) * HEAD_DIM)
        key_at = slice(width + head * HEAD_DIM, width + (head + 1) * HEAD_DIM)
        value_at = slice(2 * width + head * HEAD_DIM, 2 * width + (head + 1) * HEAD_DIM)
        for first in reversed(range(0, length, QUERY_ROWS)):
            last = first + QUERY_ROWS
            query = held[first:last, at]
            key = held[:last, key_at]
            scores = masked_scores(
                query, key, first, seg_row_ref[first:last, :], seg_col_ref[:, :last]
            )
            probs = jnp.exp(scores - log_ref[first:last, head * HEAD_DIM : head * HEAD_DIM + 1])
            grad = grad_ref[first:last, at]
            grad_probs = lax.dot_general(
                grad, held[:last, value_at], (((1,), (1,)), ((), ())), preferred_element_type=F32
            )
            inner = jnp.sum(grad_probs * probs, axis=-1, keepdims=True)
            grad_scores = (probs * (grad_probs - inner) * SCORE_SCALE).astype(BF16)
            total[first:last, at] = jnp.dot(grad_scores, key, preferred_element_type=F32)
            grad_key = lax.dot_general(
                grad_scores, query, (((0,), (0,)), ((), ())), preferred_element_type=F32
            )
            grad_value = lax.dot_general(
                probs.astype(BF16), grad, (((0,), (0,)), ((), ())), preferred_element_type=F32
            )
            if last == length:
                total[:, key_at] = grad_key
                total[:, value_at] = grad_value
            else:
                total[:last, key_at] += grad_key
                total[:last, value_at] += grad_value
    for block in range(length // 128):
        out_ref[slot_ref[block]] = total[block * 128 : (block + 1) * 128, :]


def attend_back(slots, seg_rows, seg_cols, qkv, logs, grad):
    blocks, rows, width = qkv.shape
    length = blocks * rows
    return pl.pallas_call(
        attend_back_kernel,
        out_shape=jax.ShapeDtypeStruct(qkv.shape, F32),
        in_specs=[SMEM, VMEM, VMEM, VMEM, VMEM, VMEM],
        out_specs=VMEM,
        scratch_shapes=[pltpu.VMEM((length, width), BF16), pltpu.VMEM((length, width), F32)],
        compiler_params=pltpu.CompilerParams(vmem_limit_bytes=48 * 1024 * 1024),
        name="attend_back",
    )(slots, seg_rows, seg_cols, qkv, logs, grad)


def on_device(
    hidden_in,
    segment_ids,
    attention_gain,
    mlp_gain,
    query_base,
    query_left,
    query_right,
    query_magnitude,
    key_base,
    key_left,
    key_right,
    key_magnitude,
    value_base,
    value_left,
    value_right,
    value_magnitude,
    output_base,
    output_left,
    output_right,
    output_magnitude,
    gate_base,
    gate_left,
    gate_right,
    gate_magnitude,
    up_base,
    up_left,
    up_right,
    up_magnitude,
    down_base,
    down_left,
    down_right,
    down_magnitude,
    cotangent,
):
    z, xl = lax.axis_index("z"), lax.axis_index("xl")
    y, core = lax.axis_index("y"), lax.axis_index("core")
    resid = hidden_in[0].astype(F32)
    rows, width = resid.shape
    segments = segment_ids[0]
    length = segments.shape[0]
    blocks = length // rows
    heads_width = query_base.shape[1]
    hidden = gate_base.shape[1]

    normal_one, inverse_one, normed_one = rms_forward(resid, attention_gain)
    row_blocks = gather_row(normed_one)
    row_normed = jnp.concatenate(row_blocks, axis=0)
    slots = jnp.stack(
        [
            jnp.array(SLOT_AT, jnp.int32)[(block // 2 - z) % 4, (block % 2) ^ xl]
            for block in range(blocks)
        ]
    )
    block_of_slot = jnp.stack([2 * ((z + dz) % 4) + (xl ^ dx) for dz, dx in SLOTS])

    out_weight, out_squares = adapted_weight(output_base, output_left, output_right)
    query_weight, query_squares = adapted_weight(query_base, query_left, query_right)
    key_weight, key_squares = adapted_weight(key_base, key_left, key_right)
    value_weight, value_squares = adapted_weight(value_base, value_left, value_right)
    gate_weight, gate_squares = adapted_weight(gate_base, gate_left, gate_right)
    up_weight, up_squares = adapted_weight(up_base, up_left, up_right)
    down_weight, down_squares = adapted_weight(down_base, down_left, down_right)

    block_columns = width // 8
    piece = lax.dynamic_slice_in_dim(out_weight, (2 * y + core) * block_columns, block_columns, 1)
    column_own = of_everyone(piece, TENSOR).reshape(width, block_columns)
    y_up = lambda a: lax.ppermute(a, "y", UP)
    y_down = lambda a: lax.ppermute(a, "y", DOWN)
    half = width // 2
    column_below, column_above = y_up(column_own), y_down(column_own)
    column_far = jnp.concatenate([y_up(column_below[:half]), y_down(column_above[half:])], axis=0)
    relative = jnp.stack([column_own, column_above, column_far, column_below])
    ordered = jnp.stack([relative[(j - y) % 4] for j in range(4)])
    both = (ordered, core_swap(ordered))
    pair = [jnp.where(core == c, both[0], both[1]) for c in range(2)]
    whole_output = jnp.stack(pair, axis=1)
    whole_output = whole_output.transpose(2, 0, 1, 3).reshape(width, width)

    def other_half(weight):
        count = weight.shape[0] // 2
        pulled = from_x_neighbour(lax.dynamic_slice_in_dim(weight, core * count, count, 0))
        swapped = core_swap(pulled)
        return jnp.concatenate(
            [jnp.where(core == 0, pulled, swapped), jnp.where(core == 0, swapped, pulled)], axis=0
        )

    gate_other = other_half(gate_weight)
    up_other = other_half(up_weight)
    down_other = other_half(down_weight)

    gate_scale = gate_magnitude * lax.rsqrt(gate_squares)
    up_scale = up_magnitude * lax.rsqrt(up_squares)
    vectors = x_swap(jnp.stack([gate_scale, up_scale]))
    gate_scale_other, up_scale_other = vectors[0], vectors[1]
    factors = x_swap(
        jnp.concatenate([gate_right, up_right, down_left.T], axis=0).astype(BF16)
    )
    gate_right_other = factors[:RANK]
    up_right_other = factors[RANK : 2 * RANK]
    down_left_other = factors[2 * RANK :].T

    squares = of_everyone(jnp.stack([out_squares, down_squares]), TENSOR).sum(axis=0)
    out_norm, down_norm = jnp.sqrt(squares[0]), jnp.sqrt(squares[1])
    out_scale, down_scale = output_magnitude / out_norm, down_magnitude / down_norm
    whole_left = of_everyone(output_left.T.astype(BF16), TENSOR)
    whole_left = whole_left.transpose(1, 0, 2).reshape(RANK, width)

    cot_all = gather_z(cotangent[0])

    qkv_weight = jnp.concatenate([query_weight, key_weight, value_weight], axis=1)
    qkv_scale = jnp.concatenate([query_magnitude, key_magnitude, value_magnitude]) * lax.rsqrt(
        jnp.concatenate([query_squares, key_squares, value_squares])
    )
    qkv_values = dot(row_normed, qkv_weight) * qkv_scale
    index = jnp.arange(length, dtype=jnp.int32)
    change = jnp.concatenate([jnp.ones((1,), dtype=bool), segments[1:] != segments[:-1]])
    starts = lax.cummax(jnp.where(change, index, 0), axis=0)
    positions = (index - starts).astype(F32)
    positions = jnp.take(positions.reshape(blocks, rows), block_of_slot, axis=0).reshape(length)
    frequency = 10000.0 ** (-jnp.arange(0, HEAD_DIM, 2, dtype=F32) / HEAD_DIM)
    angles = positions[:, None] * frequency[None, :]
    cosine = jnp.concatenate([jnp.cos(angles), jnp.cos(angles)], axis=-1)[:, None, :]
    sine = jnp.concatenate([jnp.sin(angles), jnp.sin(angles)], axis=-1)[:, None, :]
    pairs = qkv_values[:, : 2 * heads_width].reshape(length, -1, HEAD_DIM)
    turned = (pairs * cosine + rotate_half(pairs) * sine).reshape(length, 2 * heads_width)
    qkv = jnp.concatenate([turned, qkv_values[:, 2 * heads_width :]], axis=1).astype(BF16)
    qkv = qkv.reshape(blocks, rows, 3 * heads_width)
    seg_rows, seg_cols = segments[:, None], segments[None, :]
    attended, logs = attend(slots, seg_rows, seg_cols, qkv)

    arrived = lax.all_to_all(attended, TENSOR, split_axis=0, concat_axis=1, tiled=True)
    out_raw = dot(arrived, whole_output)
    resid_two = resid + out_raw * out_scale
    normal_two, inverse_two, normed_two = rms_forward(resid_two, mlp_gain)
    normed_all = gather_z(normed_two)

    gate_value = dot(normed_all, gate_weight) * gate_scale
    up_value = dot(normed_all, up_weight) * up_scale
    gate_value_other = dot(normed_all, gate_other) * gate_scale_other
    up_value_other = dot(normed_all, up_other) * up_scale_other
    down_grad = (cot_all.astype(F32) * down_scale).astype(BF16)

    def activation(gate, upper, weight):
        sigmoid = jax.nn.sigmoid(gate)
        activated = (gate * sigmoid * upper).astype(BF16)
        grad_activated = dot_nt(down_grad, weight)
        grad_gate = grad_activated * upper * sigmoid * (1.0 + gate * (1.0 - sigmoid))
        grad_up = grad_activated * gate * sigmoid
        return activated, grad_gate, grad_up

    activated, grad_gate, grad_up = activation(gate_value, up_value, down_weight)
    activated_other, grad_gate_other, grad_up_other = activation(
        gate_value_other, up_value_other, down_other
    )
    gate_back = (grad_gate * gate_scale).astype(BF16)
    up_back = (grad_up * up_scale).astype(BF16)
    gate_back_other = (grad_gate_other * gate_scale_other).astype(BF16)
    up_back_other = (grad_up_other * up_scale_other).astype(BF16)
    grad_normed_all = (
        dot_nt(gate_back, gate_weight)
        + dot_nt(up_back, up_weight)
        + dot_nt(gate_back_other, gate_other)
        + dot_nt(up_back_other, up_other)
    ).astype(BF16)
    grad_normed_two = scatter_z(grad_normed_all, rows)
    grad_layer = cotangent[0].astype(F32)
    grad_resid_two = grad_layer + rms_backward(grad_normed_two, normal_two, inverse_two, mlp_gain)
    out_grad_raw = (grad_resid_two * out_scale).astype(BF16)
    head_part = dot_nt(out_grad_raw, whole_output).astype(BF16)
    grad_attended = lax.all_to_all(head_part, TENSOR, split_axis=1, concat_axis=0, tiled=True)

    down_raw = scatter_z(
        (dot(activated, down_weight) + dot(activated_other, down_other)).astype(BF16), rows
    )
    layer = resid_two + down_raw * down_scale

    gate_sum, up_sum = jnp.sum(grad_gate * gate_value, axis=0), jnp.sum(grad_up * up_value, axis=0)
    gate_sum_other = jnp.sum(grad_gate_other * gate_value_other, axis=0)
    up_sum_other = jnp.sum(grad_up_other * up_value_other, axis=0)
    low_gate_up = dot(normed_all, jnp.concatenate([gate_left, up_left], axis=1))
    low_gate, low_up = low_gate_up[:, :RANK], low_gate_up[:, RANK:]
    down_through = dot_nt(down_grad, down_right)
    sent = jnp.concatenate(
        [
            dot_tn(low_gate, gate_back_other),
            dot_tn(low_up, up_back_other),
            dot_tn(down_through, activated_other),
            gate_sum_other[None],
            up_sum_other[None],
        ],
        axis=0,
    )
    given = x_swap(sent.astype(BF16)).astype(F32)
    gate_sum = (gate_sum + given[3 * RANK]) / gate_magnitude
    up_sum = (up_sum + given[3 * RANK + 1]) / up_magnitude
    gate_right_part = dot_tn(low_gate, gate_back) + given[:RANK]
    up_right_part = dot_tn(low_up, up_back) + given[RANK : 2 * RANK]
    down_left_part = dot_tn(down_through, activated) + given[2 * RANK : 3 * RANK]

    def column_norm_terms(total, magnitude, weight, squares, left, right):
        coefficient = -total * magnitude / squares
        return (
            dot_nt(right * coefficient, weight),
            dot_tn(left, weight) * coefficient,
        )

    gate_left_norm, gate_right_norm = column_norm_terms(
        gate_sum, gate_magnitude, gate_weight, gate_squares, gate_left, gate_right
    )
    up_left_norm, up_right_norm = column_norm_terms(
        up_sum, up_magnitude, up_weight, up_squares, up_left, up_right
    )
    gate_through = dot_nt(gate_back, gate_right) + dot_nt(gate_back_other, gate_right_other)
    up_through = dot_nt(up_back, up_right) + dot_nt(up_back_other, up_right_other)
    throughs = jnp.concatenate([gate_through, up_through], axis=1)
    gate_up_left = dot_tn(throughs, normed_all)
    gate_left_part = FACTOR * (gate_up_left[:RANK] + gate_left_norm)
    up_left_part = FACTOR * (gate_up_left[RANK:] + up_left_norm)
    gate_right_part = FACTOR * (gate_right_part + gate_right_norm)
    up_right_part = FACTOR * (up_right_part + up_right_norm)

    low_down = dot(activated, down_left) + dot(activated_other, down_left_other)
    out_low = dot_nt(arrived, whole_left)
    out_through = dot_nt(out_grad_raw, output_right)
    out_sum_part = jnp.sum(grad_resid_two * out_raw, axis=0)
    down_sum_part = jnp.sum(grad_layer * down_raw, axis=0)
    row_sums = of_everyone(jnp.stack([out_sum_part, down_sum_part]), TENSOR).sum(axis=0)
    out_coefficient = -row_sums[0] * output_magnitude / (out_norm * out_norm * out_norm)
    down_coefficient = -row_sums[1] * down_magnitude / (down_norm * down_norm * down_norm)
    out_right_part = FACTOR * (
        dot_tn(out_low, out_grad_raw) + dot_tn(output_left, out_weight) * out_coefficient
    )
    down_right_part = FACTOR * (
        dot_tn(low_down, down_grad) + dot_tn(down_left, down_weight) * down_coefficient
    )
    through_row = of_everyone(out_through.T.astype(BF16), TENSOR)
    through_row = through_row.transpose(1, 0, 2).reshape(RANK, length)
    out_left_part = FACTOR * (
        dot(through_row, attended) + dot_nt(output_right * out_coefficient, out_weight)
    )
    down_left_part = FACTOR * (
        down_left_part + dot_nt(down_right * down_coefficient, down_weight)
    )
    middle = summed(
        [gate_left_part, up_left_part, out_right_part, down_right_part, out_sum_part, down_sum_part],
        ALL,
    )
    middle_split = summed(
        [gate_right_part, up_right_part, out_left_part, down_left_part, gate_sum, up_sum], DP
    )

    grad_qkv = attend_back(slots, seg_rows, seg_cols, qkv, logs, grad_attended)
    grad_qkv = grad_qkv.reshape(length, 3 * heads_width)
    grad_pairs = grad_qkv[:, : 2 * heads_width].reshape(length, -1, HEAD_DIM)
    grad_pairs = (grad_pairs * cosine - rotate_half(grad_pairs * sine)).reshape(
        length, 2 * heads_width
    )
    grad_qkv = jnp.concatenate([grad_pairs, grad_qkv[:, 2 * heads_width :]], axis=1)
    qkv_back = (grad_qkv * qkv_scale).astype(BF16)
    grad_row = dot_nt(qkv_back, qkv_weight).astype(BF16)
    grad_normed_one = scatter_row([grad_row[s * rows : (s + 1) * rows] for s in range(blocks)])
    input_grad = grad_resid_two + rms_backward(
        grad_normed_one, normal_one, inverse_one, attention_gain
    )
    qkv_magnitude = jnp.concatenate([query_magnitude, key_magnitude, value_magnitude])
    qkv_sum = jnp.sum(grad_qkv * qkv_values, axis=0) / qkv_magnitude
    lefts = jnp.concatenate([query_left, key_left, value_left], axis=1)
    lows = dot(row_normed, lefts)
    last, last_split = [], []
    throughs, norms = [], []
    for i, (weight, squares_of, left, right, magnitude) in enumerate(
        (
            (query_weight, query_squares, query_left, query_right, query_magnitude),
            (key_weight, key_squares, key_left, key_right, key_magnitude),
            (value_weight, value_squares, value_left, value_right, value_magnitude),
        )
    ):
        at = slice(i * heads_width, (i + 1) * heads_width)
        back = qkv_back[:, at]
        left_norm, right_norm = column_norm_terms(
            qkv_sum[at], magnitude, weight, squares_of, left, right
        )
        throughs.append(dot_nt(back, right))
        norms.append(left_norm)
        last_split.append(
            FACTOR * (dot_tn(lows[:, i * RANK : (i + 1) * RANK], back) + right_norm)
        )
    left_parts = dot_tn(jnp.concatenate(throughs, axis=1), row_normed)
    last = FACTOR * (left_parts + jnp.concatenate(norms, axis=0))
    (last,) = summed([last], ALL)
    last_split = summed(last_split + [qkv_sum], DP)
    qkv_magnitude_grad = last_split[3]
    return (
        layer.astype(BF16)[None],
        input_grad[None],
        last[:RANK].T,
        last_split[0],
        qkv_magnitude_grad[:heads_width],
        last[RANK : 2 * RANK].T,
        last_split[1],
        qkv_magnitude_grad[heads_width : 2 * heads_width],
        last[2 * RANK :].T,
        last_split[2],
        qkv_magnitude_grad[2 * heads_width :],
        middle_split[2].T,
        middle[2],
        middle[4] / out_norm,
        middle[0].T,
        middle_split[0],
        middle_split[4],
        middle[1].T,
        middle_split[1],
        middle_split[5],
        middle_split[3].T,
        middle[3],
        middle[5] / down_norm,
    )


def solution(mesh):
    torus = Mesh(mesh.devices.reshape(4, 2, 2, 4, 2), ("y", "xh", "core", "z", "xl"))
    column = (P(None, TENSOR), P(), P(None, TENSOR), P(TENSOR))
    row = (P(TENSOR, None), P(TENSOR, None), P(), P())
    column_out, row_out = column[1:], row[1:]
    tokens = P(DP, TENSOR, None)
    return jax.shard_map(
        on_device,
        mesh=torus,
        in_specs=(
            tokens,
            P(DP, None),
            P(),
            P(),
            *column,
            *column,
            *column,
            *row,
            *column,
            *column,
            *row,
            tokens,
        ),
        out_specs=(
            tokens,
            tokens,
            *column_out,
            *column_out,
            *column_out,
            *row_out,
            *column_out,
            *column_out,
            *row_out,
        ),
        check_vma=False,
    )
```

```python
import functools

import jax
import jax.numpy as jnp
from jax import lax
from jax.experimental import pallas as pl
from jax.experimental.pallas import tpu as pltpu
from jax.sharding import Mesh
from jax.sharding import PartitionSpec as P

HEAD_DIM = 128
RANK = 16
ALPHA = 32
FACTOR = ALPHA / RANK
EPSILON = 1e-05
MASKED_SCORE = -1e30
DP = ("y", "xh", "core")
TENSOR = ("z", "xl")
ALL = DP + TENSOR
BF16 = jnp.bfloat16
F32 = jnp.float32

SWAP = ((0, 1), (1, 0))
UP = tuple((i, (i + 1) % 4) for i in range(4))
DOWN = tuple((i, (i + 3) % 4) for i in range(4))
SLOTS = ((0, 0), (0, 1), (-1, 0), (1, 0), (-1, 1), (1, 1), (2, 0), (2, 1))
SLOT_AT = ((0, 1), (3, 5), (6, 7), (2, 4))


def z_up(array):
    return lax.ppermute(array, "z", UP)


def z_down(array):
    return lax.ppermute(array, "z", DOWN)


def y_up(array):
    return lax.ppermute(array, "y", UP)


def y_down(array):
    return lax.ppermute(array, "y", DOWN)


def x_swap(array):
    return lax.ppermute(array, "xl", SWAP)


def core_swap(array):
    return lax.ppermute(array, "core", SWAP)


def from_x_neighbour(array):
    pairs = []
    for x in range(4):
        for core in range(2):
            source = (x ^ 1) if core else (x + 3 if x % 2 == 0 else x + 1) % 4
            pairs.append(
                ((source // 2) * 4 + core * 2 + source % 2, (x // 2) * 4 + core * 2 + x % 2)
            )
    return lax.ppermute(array, ("xh", "core", "xl"), tuple(pairs))


def add(*terms):
    total = terms[0].astype(F32)
    for term in terms[1:]:
        total = total + term.astype(F32)
    return total


def gather_z(own):
    half = own.shape[0] // 2
    below, above = z_up(own), z_down(own)
    return own, below, above, z_up(below[:half]), z_down(above[half:])


def scatter_z(own, below, above, far_low, far_high, meanwhile):
    half = far_low.shape[0]
    low = z_up(far_low)
    high = z_down(far_high)
    low, high = lax.optimization_barrier((low, high, meanwhile()))[:2]
    above_sum = jnp.concatenate([add(above[:half], low).astype(BF16), above[half:]], axis=0)
    below_sum = jnp.concatenate([below[:half], add(below[half:], high).astype(BF16)], axis=0)
    return own, z_up(above_sum), z_down(below_sum), above_sum


def all_to_all(array, axes):
    return lax.all_to_all(array, axes, 0, 0, tiled=True)


def of_everyone(array, axes):
    count = lax.axis_size(axes)
    return all_to_all(jnp.broadcast_to(array[None], (count, *array.shape)), axes)


def dot(left, right):
    return jnp.dot(left.astype(BF16), right.astype(BF16), preferred_element_type=F32)


def dot_nt(left, right):
    return lax.dot_general(
        left.astype(BF16), right.astype(BF16), (((1,), (1,)), ((), ())), preferred_element_type=F32
    )


def dot_tn(left, right):
    return lax.dot_general(
        left.astype(BF16), right.astype(BF16), (((0,), (0,)), ((), ())), preferred_element_type=F32
    )


def after_all(*arrays):
    return lax.optimization_barrier(arrays)[:-1]


def rms_forward(resid, gain):
    inverse = lax.rsqrt(jnp.mean(resid * resid, axis=-1, keepdims=True) + EPSILON)
    normal = resid * inverse
    return normal, inverse, (normal * gain.astype(F32)).astype(BF16)


def rms_backward(grad_normed, normal, inverse, gain):
    scaled = grad_normed * gain.astype(F32)
    return inverse * (scaled - normal * jnp.mean(scaled * normal, axis=-1, keepdims=True))


VMEM = pl.BlockSpec(memory_space=pltpu.VMEM)
SMEM = pl.BlockSpec(memory_space=pltpu.SMEM)
ANY = pl.BlockSpec(memory_space=pl.ANY)
QUERY_ROWS = 256
SCORE_SCALE = HEAD_DIM ** (-0.5)
MIB = 1024 * 1024
LANES = 128
COST = 1.0
SQUARES, SCALE = RANK, RANK + 1
EXTRA_ROWS = 24


def shape(dims, dtype=F32):
    return jax.ShapeDtypeStruct(dims, dtype)


PARAMS = pltpu.CompilerParams(vmem_limit_bytes=60 * MIB)


def cost(micros):
    return pl.CostEstimate(
        flops=0, bytes_accessed=int(micros * COST * 3.69e6), transcendentals=0
    )


def after(array, *earlier):
    return lax.optimization_barrier((array, *earlier))[0]


def whole_spec(dims):
    return pl.BlockSpec(dims, lambda *_: (0,) * len(dims))


def prepare_heads_kernel(q, k, v, al, bl, cl, ar, br, cr, mag, weight_ref, stats_ref, cross_ref):
    step = pl.program_id(0)
    columns = q.shape[1]

    @pl.when(step == 0)
    def _():
        stats_ref[...] = jnp.zeros_like(stats_ref)
        cross_ref[...] = jnp.zeros_like(cross_ref)

    for i, (base, left, right) in enumerate(((q, al, ar), (k, bl, br), (v, cl, cr))):
        at_columns = slice(i * columns, (i + 1) * columns)
        factor = left[...].astype(BF16)
        weight = base[...].astype(F32) + dot_tn(FACTOR * factor, right[...])
        low = weight.astype(BF16)
        weight_ref[:, at_columns] = low
        stats_ref[0:1, at_columns] += jnp.sum(weight * weight, axis=0, keepdims=True)
        cross_ref[:, at_columns] += dot(factor, low)

    @pl.when(step == pl.num_programs(0) - 1)
    def _():
        stats_ref[1:2, :] = mag[...] * lax.rsqrt(stats_ref[0:1, :])


def output_piece_kernel(place, base, left, right, piece_ref):
    weight = (base[...].astype(F32) + FACTOR * dot_tn(left[...], right[...])).astype(BF16)
    for t in range(piece_ref.shape[0]):
        piece_ref[t] = weight


def output_piece(place, base, left, right):
    rows, width = base.shape
    columns = width // 8

    def column(i, place):
        return 0, 2 * place[2] + place[3]

    return pl.pallas_call(
        output_piece_kernel,
        grid_spec=pltpu.PrefetchScalarGridSpec(
            num_scalar_prefetch=1,
            grid=(1,),
            in_specs=[
                pl.BlockSpec((rows, columns), column),
                pl.BlockSpec((RANK, rows), lambda i, place: (0, 0)),
                pl.BlockSpec((RANK, columns), column),
            ],
            out_specs=pl.BlockSpec((8, rows, columns), lambda i, place: (0, 0, 0)),
        ),
        out_shape=shape((8, rows, columns), BF16),
        compiler_params=PARAMS,
        cost_estimate=cost(2.5),
        name="output_piece",
    )(place, base, left, right)


def halves(which):
    def index(place):
        return place[3] if which == 0 else 1 - place[3]

    return index


def adapted_rows(step, bases, factors, squares, sums, cross):
    rows, width = bases[0].shape
    lows = []
    for i, (base, (left, right)) in enumerate(zip(bases, factors)):
        weight = base[...].astype(F32) + dot(left, FACTOR * right)
        low = weight.astype(BF16)
        lows.append(low)
        if i < 2:
            square = weight * weight
            at = pl.ds(pl.multiple_of(step * rows, rows), rows)
            squares[i, at, :] = sum(square[:, j : j + LANES] for j in range(0, width, LANES))
        else:
            sums[...] += jnp.sum(weight * weight, axis=0, keepdims=True)
            cross[...] += dot_tn(left, low)
    return lows


def down_sublanes(factor):
    unit = (
        lax.broadcasted_iota(jnp.int32, (RANK, LANES), 0)
        == lax.broadcasted_iota(jnp.int32, (RANK, LANES), 1)
    ).astype(BF16)
    return dot_tn(factor, unit)


def prepare_send_kernel(
    place, g, u, d, gl, ul, dl, gr, ur, dr, send_ref, squares_ref, sums_ref, cross_ref, columns
):
    step = pl.program_id(0)
    rows = g.shape[0]

    @pl.when(step == 0)
    def _():
        for i, factor in enumerate((gr, ur, dl)):
            columns[i] = down_sublanes(factor[...])
        cross_ref[...] = jnp.zeros_like(cross_ref)
        sums_ref[...] = jnp.zeros_like(sums_ref)

    at = pl.ds(pl.multiple_of((pl.num_programs(0) * place[3] + step) * rows, rows), rows)
    factors = [(columns[i, at, 0:RANK], right[...]) for i, right in enumerate((gl, ul, dr))]
    lows = adapted_rows(step, (g, u, d), factors, squares_ref, sums_ref, cross_ref)
    for i, low in enumerate(lows):
        send_ref[i] = low


def prepare_keep_kernel(
    place, g, u, d, gl, ul, dl, gr, ur, dr, o, ol, orr, mag, squares_in, sums_in, cross_in,
    keep_ref, out_ref, extra_ref, cross_ref, terms_ref, squares, squares_all, columns, sums,
):
    step = pl.program_id(0)
    steps = pl.num_programs(0)
    rows = g.shape[0]
    out_rows, width = o.shape

    @pl.when(step == 0)
    def _():
        for i, factor in enumerate((gr, ur, dl)):
            columns[i] = down_sublanes(factor[...])
        columns[3, 0 : ol.shape[1], :] = down_sublanes(ol[...])
        cross_ref[0] = jnp.zeros_like(cross_in)
        cross_ref[1] = cross_in[...]
        sums[0:1, :] = jnp.zeros_like(sums_in)
        sums[1:2, :] = sums_in[...]

    at = pl.ds(pl.multiple_of((steps * (1 - place[3]) + step) * rows, rows), rows)
    factors = [(columns[i, at, 0:RANK], right[...]) for i, right in enumerate((gl, ul, dr))]
    lows = adapted_rows(step, (g, u, d), factors, squares, sums.at[1:2], cross_ref.at[1])
    for i, low in enumerate(lows):
        keep_ref[i] = low
    left = columns[3, pl.ds(pl.multiple_of(step * out_rows, out_rows), out_rows), 0:RANK]
    weight = o[...].astype(F32) + dot(left, FACTOR * orr[...])
    low = weight.astype(BF16)
    out_ref[...] = low
    cross_ref[0] += dot_tn(left, low)
    sums[0:1, :] += jnp.sum(weight * weight, axis=0, keepdims=True)

    @pl.when(step == steps - 1)
    def _():
        half = squares.shape[1]
        for core, part in ((place[3], squares_in), (1 - place[3], squares)):
            squares_all[:, pl.ds(pl.multiple_of(core * half, half), half), :] = part[...]
        extra_ref[...] = jnp.zeros_like(extra_ref)
        for i, right in enumerate((gr, ur)):
            extra_ref[i, 0:RANK, :] = right[...]
            total = lax.dot_general(
                jnp.ones((8, LANES), F32),
                squares_all[i],
                (((1,), (1,)), ((), ())),
                precision=lax.Precision.HIGHEST,
                preferred_element_type=F32,
            )
            extra_ref[i, SQUARES : SQUARES + 1, :] = total[0:1]
            extra_ref[i, SCALE : SCALE + 1, :] = mag[i : i + 1, :] * lax.rsqrt(total[0:1])
        extra_ref[2, 0:RANK, :] = dl[...]
        lanes = terms_ref.shape[2]
        total = jnp.concatenate(
            [sums[i : i + 1, j : j + lanes] for i in range(2) for j in range(0, width, lanes)], axis=0
        )
        high = total.astype(BF16)
        rest = (total - high.astype(F32)).astype(BF16)
        for t in range(terms_ref.shape[0]):
            terms_ref[t, 0:RANK, :] = ol[...].astype(BF16)
            terms_ref[t, RANK : RANK + 16, :] = high
            terms_ref[t, RANK + 16 :, :] = rest


HALF_STEPS = 2


def half_specs(which, hidden, width):
    rows = hidden // 2 // HALF_STEPS
    half = halves(which)

    def whole(*dims):
        return pl.BlockSpec(dims, lambda i, place: (0,) * len(dims))

    base = pl.BlockSpec((rows, width), lambda i, place: (HALF_STEPS * half(place) + i, 0))
    specs = [base] * 3 + [whole(RANK, width)] * 2 + [whole(RANK, hidden)] * 3 + [whole(RANK, width)]
    return specs, whole, pl.BlockSpec((3, rows, width), lambda i, place: (0, i, 0))


def prepare_first_kernel(place, *refs):
    inputs, heads_inputs, outputs = refs[:9], refs[9:19], refs[19:]
    prepare_send_kernel(place, *inputs, *outputs[:4], outputs[7])
    prepare_heads_kernel(*heads_inputs, *outputs[4:7])


def prepare_first(place, bases, lefts, rights, heads_bases, heads_lefts, heads_rights, magnitude):
    hidden, width = bases[0].shape
    columns = heads_bases[0].shape[1]
    rows = width // HALF_STEPS
    specs, whole, block = half_specs(0, hidden, width)
    return pl.pallas_call(
        prepare_first_kernel,
        grid_spec=pltpu.PrefetchScalarGridSpec(
            num_scalar_prefetch=1,
            grid=(HALF_STEPS,),
            in_specs=specs
            + [pl.BlockSpec((rows, columns), lambda i, place: (i, 0))] * 3
            + [pl.BlockSpec((RANK, rows), lambda i, place: (0, i))] * 3
            + [whole(RANK, columns)] * 3
            + [whole(1, 3 * columns)],
            out_specs=(
                block,
                whole(2, hidden // 2, LANES),
                whole(1, width),
                whole(RANK, width),
                pl.BlockSpec((rows, 3 * columns), lambda i, place: (i, 0)),
                whole(8, 3 * columns),
                whole(RANK, 3 * columns),
            ),
            scratch_shapes=[pltpu.VMEM((3, hidden, LANES), F32)],
        ),
        out_shape=(
            shape((3, hidden // 2, width), BF16),
            shape((2, hidden // 2, LANES)),
            shape((1, width)),
            shape((RANK, width)),
            shape((width, 3 * columns), BF16),
            shape((8, 3 * columns)),
            shape((RANK, 3 * columns)),
        ),
        compiler_params=PARAMS,
        cost_estimate=cost(11),
        name="prepare_first",
    )(place, *bases, *lefts, *rights, *heads_bases, *heads_lefts, *heads_rights, magnitude)


def prepare_second_kernel(place, *refs):
    inputs, near_inputs, outputs = refs[:16], refs[16:24], refs[24:]
    prepare_keep_kernel(place, *inputs, *outputs[:5], *outputs[6:])

    @pl.when(pl.program_id(0) == 0)
    def _():
        project_heads_kernel(0, place, *near_inputs, outputs[5])


def prepare_second(place, bases, lefts, rights, out, magnitude, sent, near):
    hidden, width = bases[0].shape
    out_rows = out[0].shape[0]
    specs, whole, block = half_specs(1, hidden, width)
    out_block = pl.BlockSpec((out_rows // HALF_STEPS, width), lambda i, place: (i, 0))
    rows, heads_width = near[0].shape[0], near[4].shape[1]
    return pl.pallas_call(
        prepare_second_kernel,
        grid_spec=pltpu.PrefetchScalarGridSpec(
            num_scalar_prefetch=1,
            grid=(HALF_STEPS,),
            in_specs=specs
            + [
                out_block,
                whole(RANK, out_rows),
                whole(RANK, width),
                whole(2, hidden),
                whole(2, hidden // 2, LANES),
                whole(1, width),
                whole(RANK, width),
            ]
            + [whole(*a.shape) for a in near],
            out_specs=(
                block,
                out_block,
                whole(3, EXTRA_ROWS, hidden),
                whole(2, RANK, width),
                whole(8, 3 * RANK, width // 8),
                whole(4, rows, heads_width),
            ),
            scratch_shapes=[
                pltpu.VMEM((2, hidden // 2, LANES), F32),
                pltpu.VMEM((2, hidden, LANES), F32),
                pltpu.VMEM((4, hidden, LANES), F32),
                pltpu.VMEM((8, width), F32),
            ],
        ),
        out_shape=(
            shape((3, hidden // 2, width), BF16),
            shape((out_rows, width), BF16),
            shape((3, EXTRA_ROWS, hidden)),
            shape((2, RANK, width)),
            shape((8, 3 * RANK, width // 8), BF16),
            shape((4, rows, heads_width), BF16),
        ),
        compiler_params=PARAMS,
        cost_estimate=cost(14),
        name="prepare_second",
    )(place, *bases, *lefts, *rights, *out, magnitude, *sent, *near)


def slot_of(place, block):
    away = lax.rem(block // 2 - place[0] + 4, 4)
    other = jnp.where(place[1] == block % 2, 0, 1)
    return jnp.where(
        away == 0, other, jnp.where(away == 1, 3 + 2 * other, jnp.where(away == 2, 6 + other, 2 + 2 * other))
    )


def block_of(place, slot):
    dz, dx = SLOTS[slot]
    return 2 * lax.rem(place[0] + dz + 4, 4) + (place[1] if dx == 0 else 1 - place[1])


def turned(values, cosine, sine):
    return values * cosine + pltpu.roll(values, HEAD_DIM // 2, 1) * sine


def turned_back(grads, cosine, sine):
    return grads * cosine - pltpu.roll(grads, HEAD_DIM // 2, 1) * sine


def project_heads_kernel(first_slot, place, b0, b1, b2, b3, weight, stats, cosine, sine, out_ref):
    blocks = jnp.concatenate([b[...] for b in (b0, b1, b2, b3)], axis=0)
    rows = b0.shape[0]
    width = weight.shape[1]
    values = jnp.dot(blocks, weight[...], preferred_element_type=F32) * stats[1:2, :]
    for s in range(4):
        at = pl.ds(pl.multiple_of(block_of(place, first_slot + s) * rows, rows), rows)
        cos, sin = cosine[at, :], sine[at, :]
        for head in range(width // HEAD_DIM):
            head_at = slice(head * HEAD_DIM, (head + 1) * HEAD_DIM)
            part = values[s * rows : (s + 1) * rows, head_at]
            if head < 2 * width // HEAD_DIM // 3:
                part = turned(part, cos, sin)
            out_ref[s, :, head_at] = part.astype(BF16)


def project_heads(first_slot, place, blocks, weight, stats, cosine, sine):
    rows = blocks[0].shape[0]
    return pl.pallas_call(
        functools.partial(project_heads_kernel, first_slot),
        out_shape=shape((4, rows, weight.shape[1]), BF16),
        in_specs=[SMEM] + [VMEM] * 8,
        out_specs=VMEM,
        compiler_params=PARAMS,
        cost_estimate=cost(5.5),
        name="project_heads",
    )(place, *blocks, weight, stats, cosine, sine)


def low_kernel(lefts_t, *refs):
    *blocks, out_ref = refs
    rows = blocks[0].shape[0]
    for s, block in enumerate(blocks):
        out_ref[:, s * rows : (s + 1) * rows] = dot_nt(lefts_t[...], block[...]).astype(BF16)


def low_terms(lefts_t, blocks):
    rows = blocks[0].shape[0]
    return pl.pallas_call(
        low_kernel,
        out_shape=shape((lefts_t.shape[0], rows * len(blocks)), BF16),
        in_specs=[VMEM] * (1 + len(blocks)),
        out_specs=VMEM,
        compiler_params=PARAMS,
        cost_estimate=cost(4.5),
        name="low_terms",
    )(lefts_t, *blocks)


def masked_scores(place, query, key, first_row):
    scores = dot_nt(query, key) * SCORE_SCALE
    row = first_row + lax.broadcasted_iota(jnp.int32, (query.shape[0], 1), 0)
    start = jnp.where(row < place[4], 0, jnp.where(row < place[5], place[4], place[5]))
    column = lax.broadcasted_iota(jnp.int32, scores.shape, 1)
    return jnp.where((column <= row) & (column >= start), scores, MASKED_SCORE)


def place_blocks(place, near, far, held):
    rows = near.shape[1]
    for block in range(2 * near.shape[0]):
        slot = slot_of(place, block)
        at = slice(block * rows, (block + 1) * rows)

        @pl.when(slot < 4)
        def _():
            held[at, :] = near[jnp.minimum(slot, 3)]

        @pl.when(slot >= 4)
        def _():
            held[at, :] = far[jnp.maximum(slot - 4, 0)]


def attend_kernel(place, near, far, terms, out_ref, log_ref, held):
    length = held.shape[0]
    width = out_ref.shape[2]
    rows = near.shape[1]
    out_ref[:, rows:, :] = terms[...]
    place_blocks(place, near, far, held)
    for head in range(width // HEAD_DIM):
        at = slice(head * HEAD_DIM, (head + 1) * HEAD_DIM)
        key_at = slice(width + head * HEAD_DIM, width + (head + 1) * HEAD_DIM)
        value_at = slice(2 * width + head * HEAD_DIM, 2 * width + (head + 1) * HEAD_DIM)
        for first in range(0, length, QUERY_ROWS):
            last = first + QUERY_ROWS
            scores = masked_scores(place, held[first:last, at], held[:last, key_at], first)
            largest = jnp.max(scores, axis=-1, keepdims=True)
            weights = jnp.exp(scores - largest)
            totals = jnp.sum(weights, axis=-1, keepdims=True)
            probs = (weights * (1.0 / totals)).astype(BF16)
            out = jnp.dot(probs, held[:last, value_at], preferred_element_type=F32)
            for i in range(QUERY_ROWS // rows):
                out_ref[first // rows + i, 0:rows, at] = out[i * rows : (i + 1) * rows].astype(BF16)
            log_ref[first:last, at] = jnp.broadcast_to(
                largest + jnp.log(totals), (QUERY_ROWS, HEAD_DIM)
            )


def attend(place, near, far, terms):
    blocks, rows, width = near.shape
    length = 2 * blocks * rows
    groups = terms.shape[0]
    return pl.pallas_call(
        attend_kernel,
        out_shape=(
            shape((groups, length // groups + terms.shape[1], width // 3), BF16),
            shape((length, width // 3)),
        ),
        in_specs=[SMEM] + [VMEM] * 3,
        out_specs=(VMEM, VMEM),
        scratch_shapes=[pltpu.VMEM((length, width), BF16)],
        compiler_params=PARAMS,
        cost_estimate=cost(7.5),
        name="attend",
    )(place, near, far, terms)


def attend_back_kernel(
    place, near, far, log_ref, grad_ref, cosine, sine, stats,
    out_ref, sum_ref, held, total,
):
    length = held.shape[0]
    width = grad_ref.shape[2]
    rows = near.shape[1]
    place_blocks(place, near, far, held)
    for head in range(width // HEAD_DIM):
        at = slice(head * HEAD_DIM, (head + 1) * HEAD_DIM)
        key_at = slice(width + head * HEAD_DIM, width + (head + 1) * HEAD_DIM)
        value_at = slice(2 * width + head * HEAD_DIM, 2 * width + (head + 1) * HEAD_DIM)
        for first in reversed(range(0, length, QUERY_ROWS)):
            last = first + QUERY_ROWS
            query = held[first:last, at]
            key = held[:last, key_at]
            scores = masked_scores(place, query, key, first)
            probs = jnp.exp(scores - log_ref[first:last, head * HEAD_DIM : head * HEAD_DIM + 1])
            grad = jnp.concatenate(
                [grad_ref[i, 0:rows, at] for i in range(first // rows, last // rows)], axis=0
            )
            grad_probs = dot_nt(grad, held[:last, value_at])
            inner = jnp.sum(grad_probs * probs, axis=-1, keepdims=True)
            grad_scores = (probs * (grad_probs - inner) * SCORE_SCALE).astype(BF16)
            total[first:last, at] = jnp.dot(grad_scores, key, preferred_element_type=F32)
            grad_key = dot_tn(grad_scores, query)
            grad_value = dot_tn(probs, grad)
            if last == length:
                total[:, key_at] = grad_key
                total[:, value_at] = grad_value
            else:
                total[:last, key_at] += grad_key
                total[:last, value_at] += grad_value
    heads = 3 * width // HEAD_DIM
    for head in range(heads):
        at = slice(head * HEAD_DIM, (head + 1) * HEAD_DIM)
        sums = jnp.zeros((1, HEAD_DIM), F32)
        for block in range(length // rows):
            block_at = slice(block * rows, (block + 1) * rows)
            grads = total[block_at, at]
            values = held[block_at, at].astype(F32)
            if head < 2 * heads // 3:
                cos, sin = cosine[block_at, :], sine[block_at, :]
                grads = turned_back(grads, cos, sin)
                values = turned_back(values, cos, sin)
            sums += jnp.sum(grads * values, axis=0, keepdims=True)
            out_ref[slot_of(place, block), :, at] = (grads * stats[1:2, at]).astype(BF16)
        sum_ref[:, at] = jnp.broadcast_to(sums, (8, HEAD_DIM))


def attend_back(place, near, far, logs, grad, cosine, sine, stats):
    blocks, rows, width = near.shape
    length = 2 * blocks * rows
    return pl.pallas_call(
        attend_back_kernel,
        out_shape=(shape((2 * blocks, rows, width), BF16), shape((8, width))),
        in_specs=[SMEM] + [VMEM] * 7,
        out_specs=(VMEM, VMEM),
        scratch_shapes=[pltpu.VMEM((length, width), BF16), pltpu.VMEM((length, width), F32)],
        compiler_params=PARAMS,
        cost_estimate=cost(10.5),
        name="attend_back",
    )(place, near, far, logs, grad, cosine, sine, stats)


def heads_back_kernel(grads, source, *refs):
    *outs, dz, weight, sems, out_sems = refs
    rows = grads.shape[1]
    chunks = weight.shape[0]
    columns = weight.shape[1]
    copies = [
        pltpu.make_async_copy(source.at[pl.ds(i * columns, columns)], weight.at[i], sems.at[i])
        for i in range(chunks)
    ]
    start_all([copies])
    for s in range(len(outs)):
        dz[s * rows : (s + 1) * rows, :] = grads[s]
    for i in range(chunks):
        copies[i].wait()
        part = dot_nt(dz[...], weight[i]).astype(BF16)
        for s, out in enumerate(outs):
            out[:, i * columns : (i + 1) * columns] = part[s * rows : (s + 1) * rows]


def heads_back(grads, weight):
    blocks, rows, columns = grads.shape
    depth = weight.shape[0]
    chunks = 4
    return pl.pallas_call(
        heads_back_kernel,
        out_shape=(shape((rows, depth), BF16),) * blocks,
        in_specs=[VMEM, ANY],
        out_specs=(VMEM,) * blocks,
        scratch_shapes=[
            pltpu.VMEM((blocks * rows, columns), BF16),
            pltpu.VMEM((chunks, depth // chunks, columns), BF16),
            pltpu.SemaphoreType.DMA((chunks,)),
            pltpu.SemaphoreType.DMA((blocks,)),
        ],
        compiler_params=PARAMS,
        cost_estimate=cost(8),
        name="heads_back",
    )(grads, weight)


def weight_copies(mine, others, buffer, sems):
    return [
        pltpu.make_async_copy(source.at[i], buffer.at[2 * i + j], sems.at[2 * i + j])
        for i in range(mine.shape[0])
        for j, source in enumerate((mine, others))
    ]


def start_all(copies):
    for group in copies:
        for copy in group:
            copy.start()


def wait_all(group):
    for copy in group:
        copy.wait()


def column_of(place, i, lanes):
    core = place[3] if i % 2 == 0 else 1 - place[3]
    return pl.ds(pl.multiple_of((2 * (i // 2) + core) * lanes, lanes), lanes)


def output_kernel(
    place, arrived, resid, magnitude, gain, mine, others, raw_ref, resid_ref, normed_ref, row_ref, buffer, sems
):
    copies = weight_copies(mine, others, buffer, sems)
    start_all([copies])
    rows = resid.shape[0]
    groups, lanes = arrived.shape[0], arrived.shape[2]
    tokens = jnp.concatenate([arrived[t, 0:rows, :] for t in range(groups)], axis=1)
    squares = 0.0
    for t in range(groups):
        parts = arrived[t, rows + RANK : rows + 3 * RANK, :].astype(F32)
        squares += parts[0:RANK] + parts[RANK : 2 * RANK]
    squares = jnp.concatenate(
        [
            jnp.concatenate([squares[i * 8 + j : i * 8 + j + 1] for j in range(8)], axis=1)
            for i in range(2)
        ],
        axis=0,
    )
    scales = magnitude[...] * lax.rsqrt(squares)
    row_ref[0:2, :] = squares
    row_ref[2:4, :] = scales
    row_ref[4:8, :] = jnp.zeros((4, squares.shape[1]), F32)
    for i, copy in enumerate(copies):
        copy.wait()
        raw_ref[:, column_of(place, i, lanes)] = jnp.dot(
            tokens, buffer[i], preferred_element_type=F32
        )
    resid_two = resid[...].astype(F32) + raw_ref[...] * scales[0:1]
    resid_ref[...] = resid_two
    _, _, normed_ref[...] = rms_forward(resid_two, gain[...])


def output_forward(place, arrived, resid, magnitude, gain, columns):
    rows, width = resid.shape
    return pl.pallas_call(
        output_kernel,
        out_shape=(
            shape((rows, width)),
            shape((rows, width)),
            shape((rows, width), BF16),
            shape((8, width)),
        ),
        in_specs=[SMEM] + [VMEM] * 4 + [ANY] * len(columns),
        out_specs=(VMEM,) * 4,
        scratch_shapes=[
            pltpu.VMEM((8, *columns[0].shape[1:]), BF16),
            pltpu.SemaphoreType.DMA((8,)),
        ],
        compiler_params=PARAMS,
        cost_estimate=cost(7.5),
        name="output_forward",
    )(place, arrived, resid, magnitude, gain, *columns)


def output_back_kernel(
    place, own, below, above, down_own, down_below, down_above, cot, raw, resid, row, gain, right, mine,
    others, grad_ref, dz_ref, head_ref, layer_ref, buffer, total, sems,
):
    copies = weight_copies(mine, others, buffer, sems)
    start_all([copies])
    scales = row[2:4, :]
    grad_normed = own[...].astype(F32) + below[...].astype(F32) + above[...].astype(F32)
    resid_two = resid[...]
    cotangent = cot[...].astype(F32)
    inverse = lax.rsqrt(jnp.mean(resid_two * resid_two, axis=-1, keepdims=True) + EPSILON)
    grad = cotangent + rms_backward(grad_normed, resid_two * inverse, inverse, gain[...])
    grad_ref[...] = grad
    dz = (grad * scales[0:1]).astype(BF16)
    dz_ref[...] = dz
    down = (
        down_own[...].astype(F32) + down_below[...].astype(F32) + down_above[...].astype(F32)
    ) * scales[1:2]
    layer_ref[...] = (resid_two + down).astype(BF16)
    sums = (
        jnp.sum(grad * raw[...], axis=0, keepdims=True) * scales[0:1],
        jnp.sum(cotangent * down, axis=0, keepdims=True),
    )
    rows, lanes = dz.shape[0], buffer.shape[2]
    through = dot_nt(right[...], dz)
    terms = jnp.concatenate(
        [jnp.concatenate([through, jnp.zeros((RANK, lanes - rows), F32)], axis=1)]
        + [s[:, j * lanes : (j + 1) * lanes] for s in sums for j in range(8)],
        axis=0,
    ).astype(BF16)
    for i, copy in enumerate(copies):
        copy.wait()
        part = dot_nt(dz_ref[:, column_of(place, i, lanes)], buffer[i])
        if i == 0:
            total[...] = part
        else:
            total[...] += part
    for t in range(head_ref.shape[0]):
        head_ref[t, 0:rows, :] = total[:, t * lanes : (t + 1) * lanes].astype(BF16)
        head_ref[t, rows:, :] = terms


def output_back(place, back, forward, cot, raw, resid, row, gain, right, columns, groups):
    rows, width = resid.shape
    return pl.pallas_call(
        output_back_kernel,
        out_shape=(
            shape((rows, width)),
            shape((rows, width), BF16),
            shape((groups, rows + 2 * RANK, width // groups), BF16),
            shape((rows, width), BF16),
        ),
        in_specs=[SMEM] + [VMEM] * 12 + [ANY] * len(columns),
        out_specs=(VMEM,) * 4,
        scratch_shapes=[
            pltpu.VMEM((8, *columns[0].shape[1:]), BF16),
            pltpu.VMEM((rows, width), F32),
            pltpu.SemaphoreType.DMA((8,)),
        ],
        compiler_params=PARAMS,
        cost_estimate=cost(8),
        name="output_back",
    )(place, *back, *forward, cot, raw, resid, row, gain, right, *columns)


def hidden_kernel(
    place, own, below, above, far_low, far_high, cot_own, cot_below, cot_above, cot_low, cot_high,
    down_scale, extra, extra_other, send, keep, pulled, swapped,
    b0, b1, b2, b3, b4, f0, f1, f2, f3, f4, act_ref, gate_ref, up_ref, sum_ref, dz_ref,
    tokens, buffer, sems,
):
    core = place[3]
    hidden, depth = buffer.shape[2:]
    half = hidden // 2

    def rows_at(which, count):
        return pl.ds(pl.multiple_of(which * count, count), count)

    copies = [
        pltpu.make_async_copy(
            source.at[i],
            buffer.at[c, i, rows_at(core if j == 0 else 1 - core, half)],
            sems.at[6 * c + 2 * i + j],
        )
        for c, sources in enumerate(((send, keep), (pulled, swapped)))
        for i in range(3)
        for j, source in enumerate(sources)
    ]
    start_all([copies])
    rows = own.shape[0]
    ends = (0, rows, 2 * rows, 3 * rows, 3 * rows + rows // 2, 4 * rows)
    for i, block in enumerate((own, below, above, far_low, far_high)):
        tokens[ends[i] : ends[i + 1], :] = block[...]
    for i, block in enumerate((cot_own, cot_below, cot_above, cot_low, cot_high)):
        dz_ref[ends[i] : ends[i + 1], :] = (block[...].astype(F32) * down_scale[...]).astype(BF16)
    sum_ref[...] = jnp.zeros_like(sum_ref)
    for c in range(2):
        factors = (extra, extra_other)[c]
        gate_scale = factors[0, SCALE : SCALE + 1, :]
        up_scale = factors[1, SCALE : SCALE + 1, :]
        wait_all(copies[6 * c + 0 : 6 * c + 2])
        gate = dot_nt(tokens[...], buffer[c, 0]) * gate_scale
        wait_all(copies[6 * c + 2 : 6 * c + 4])
        upper = dot_nt(tokens[...], buffer[c, 1]) * up_scale
        wait_all(copies[6 * c + 4 : 6 * c + 6])
        grad = dot_nt(dz_ref[...], buffer[c, 2])
        sigmoid = 1.0 / (1.0 + jnp.exp(-gate))
        silu = gate * sigmoid
        act_ref[c] = (silu * upper).astype(BF16)
        grad_up = grad * silu
        grad_gate = grad * upper * (sigmoid + silu * (1.0 - sigmoid))
        sum_ref[c, 0:1, :] = jnp.sum(grad_gate * gate, axis=0, keepdims=True)
        sum_ref[c, 1:2, :] = jnp.sum(grad_up * upper, axis=0, keepdims=True)
        gate_ref[c] = (grad_gate * gate_scale).astype(BF16)
        up_ref[c] = (grad_up * up_scale).astype(BF16)
    columns = 512

    def spread(outs, at, part):
        for i in range(3):
            outs[i][:, at : at + columns] = part[i * rows : (i + 1) * rows]
        outs[3][:, at : at + columns] = part[3 * rows : 3 * rows + rows // 2]
        outs[4][:, at : at + columns] = part[3 * rows + rows // 2 :]

    for at in range(0, depth, columns):
        part = dot(gate_ref[0], buffer[0, 0, :, at : at + columns])
        part += dot(up_ref[0], buffer[0, 1, :, at : at + columns])
        part += dot(gate_ref[1], buffer[1, 0, :, at : at + columns])
        part += dot(up_ref[1], buffer[1, 1, :, at : at + columns])
        spread((b0, b1, b2, b3, b4), at, part.astype(BF16))
    for at in range(0, depth, columns):
        part = dot(act_ref[0], buffer[0, 2, :, at : at + columns])
        part += dot(act_ref[1], buffer[1, 2, :, at : at + columns])
        spread((f0, f1, f2, f3, f4), at, part.astype(BF16))


def feed_forward(place, tokens, cot, down_scale, extra, extra_other, weights):
    rows, width = tokens[0].shape
    hidden = extra.shape[2]
    total = 4 * rows
    pieces = tuple(shape((n, width), BF16) for n in (rows, rows, rows, rows // 2, rows // 2))
    return pl.pallas_call(
        hidden_kernel,
        out_shape=(
            *pieces,
            *pieces,
            shape((2, total, hidden), BF16),
            shape((2, total, hidden), BF16),
            shape((2, total, hidden), BF16),
            shape((2, 8, hidden)),
            shape((total, width), BF16),
        ),
        in_specs=[SMEM] + [VMEM] * 13 + [ANY] * 4,
        out_specs=(VMEM,) * 15,
        scratch_shapes=[
            pltpu.VMEM((total, width), BF16),
            pltpu.VMEM((2, 3, hidden, width), BF16),
            pltpu.SemaphoreType.DMA((12,)),
        ],
        compiler_params=PARAMS,
        cost_estimate=cost(31),
        name="feed_forward",
    )(place, *tokens, *cot, down_scale, extra, extra_other, *weights)


def hidden_grads_kernel(
    own, below, above, far_low, far_high, dz, act, gate, upper, sums, extra, extra_other, lefts_t,
    down_right, left_ref, down_ref, mine_ref, sent_ref,
):
    tokens = jnp.concatenate([r[...] for r in (own, below, above, far_low, far_high)], axis=0)
    lows = dot_nt(lefts_t[...], tokens)
    down_through = dot_nt(down_right[...], dz[...])
    throughs = [0.0, 0.0]
    low_down = 0.0
    for c, (factors, out) in enumerate(((extra, mine_ref), (extra_other, sent_ref))):
        for i, back in enumerate((gate, upper)):
            throughs[i] += dot_nt(factors[i, 0:RANK, :], back[c])
            out[i * RANK : (i + 1) * RANK, :] = dot(lows[i * RANK : (i + 1) * RANK], back[c]).astype(
                out.dtype
            )
        low_down += dot_nt(factors[2, 0:RANK, :], act[c])
        out[2 * RANK : 3 * RANK, :] = dot(down_through, act[c]).astype(out.dtype)
        out[3 * RANK :, :] = jnp.concatenate(
            [sums[c], jnp.zeros_like(sums[c])], axis=0
        ).astype(out.dtype)
    through = jnp.concatenate(throughs, axis=0)
    left_ref[...] = dot(through, tokens)
    down_ref[...] = dot(low_down, dz[...])


def hidden_grads(tokens, dz, act, gate, upper, sums, extra, extra_other, lefts_t, down_right):
    width = dz.shape[1]
    hidden = act.shape[2]
    return pl.pallas_call(
        hidden_grads_kernel,
        out_shape=(
            shape((2 * RANK, width)),
            shape((RANK, width)),
            shape((4 * RANK, hidden)),
            shape((4 * RANK, hidden), BF16),
        ),
        in_specs=[VMEM] * 14,
        out_specs=(VMEM,) * 4,
        compiler_params=PARAMS,
        cost_estimate=cost(8.4),
        name="hidden_grads",
    )(*tokens, dz, act, gate, upper, sums, extra, extra_other, lefts_t, down_right)


def half_copies(place, send, keep, planes, buffer, sems):
    half = buffer.shape[1] // 2
    copies = []
    for j, (source, which) in enumerate(((send, place[3]), (keep, 1 - place[3]))):
        rows = pl.ds(pl.multiple_of(which * half, half), half)
        copies.append(
            pltpu.make_async_copy(source.at[planes], buffer.at[:, rows], sems.at[j])
        )
    return copies


def hidden_norms_kernel(
    place, left, mine, given, extra, lefts_t, send, keep, left_ref, split_ref, weight, sems
):
    copies = half_copies(place, send, keep, slice(0, 2), weight, sems)
    start_all([copies])
    wait_all(copies)
    hidden = mine.shape[1]
    parts = mine[...] + given[...].astype(F32)
    rows = []
    for i in range(2):
        sums = parts[3 * RANK + i : 3 * RANK + i + 1, :]
        coefficient = -sums / extra[i, SQUARES : SQUARES + 1, :]
        at = slice(i * RANK, (i + 1) * RANK)
        left_ref[at, :] = FACTOR * (
            left[at, :] + dot(extra[i, 0:RANK, :] * coefficient, weight[i])
        )
        rows.append(
            FACTOR * (parts[at, :] + dot_nt(lefts_t[at, :], weight[i]) * coefficient)
        )
    rows.append(parts[3 * RANK :, :])
    split_ref[:, 0:hidden] = jnp.concatenate(rows, axis=0).astype(BF16)
    split_ref[:, hidden:] = jnp.zeros((3 * RANK, split_ref.shape[1] - hidden), BF16)


def hidden_norms(place, left, mine, given, extra, lefts_t, send, keep):
    width, hidden = left.shape[1], mine.shape[1]
    lanes = (hidden + LANES - 1) // LANES * LANES
    return pl.pallas_call(
        hidden_norms_kernel,
        out_shape=(shape((2 * RANK, width)), shape((3 * RANK, lanes), BF16)),
        in_specs=[SMEM] + [VMEM] * 5 + [ANY] * 2,
        out_specs=(VMEM, VMEM),
        scratch_shapes=[pltpu.VMEM((2, hidden, width), BF16), pltpu.SemaphoreType.DMA((2,))],
        compiler_params=PARAMS,
        cost_estimate=cost(5),
        name="hidden_norms",
    )(place, left, mine, given, extra, lefts_t, send, keep)


SPLIT_LANES = 256


def gathered_sums(received, tokens):
    sums = 0.0
    for t in range(received.shape[0]):
        sums += received[t, tokens + RANK : tokens + 2 * RANK, :].astype(F32)
    return jnp.concatenate(
        [
            jnp.concatenate([sums[8 * i + j : 8 * i + j + 1] for j in range(8)], axis=1)
            for i in range(2)
        ],
        axis=0,
    )


def split_grads_kernel(
    place, send, keep, grads, lows, heads_stats, heads_sums, heads_cross, mine, given, row, received,
    out_right, down_right, out_weight, attended, hidden_split, split_ref, down_weight, sems,
):
    copies = half_copies(place, send, keep, slice(2, 3), down_weight, sems)
    start_all([copies])
    width = row.shape[1]
    columns = heads_sums.shape[1] // 3
    slots, tokens = grads.shape[:2]
    row_sums = gathered_sums(received, tokens)
    above = hidden_split.shape[0]
    split_ref[0:above, :] = hidden_split[...]
    split_ref[above:, 2 * SPLIT_LANES :] = jnp.zeros(
        (split_ref.shape[0] - above, split_ref.shape[1] - 2 * SPLIT_LANES), BF16
    )

    def put(lanes, values):
        split_ref[above:, lanes] = values.astype(BF16)

    coefficient = -heads_sums[0:1, :] / heads_stats[0:1, :]
    first = []
    for i in range(3):
        at = slice(i * columns, (i + 1) * columns)
        dz = jnp.concatenate([grads[s, :, at] for s in range(slots)], axis=0)
        first.append(
            FACTOR
            * (
                jnp.dot(lows[i * RANK : (i + 1) * RANK, :], dz, preferred_element_type=F32)
                + heads_cross[:, at] * coefficient[:, at]
            )
        )
    out_coefficient, down_coefficient = (
        -row_sums[i : i + 1, :] / row[i : i + 1, :] for i in range(2)
    )
    out_left = 0.0
    for t in range(received.shape[0]):
        through = received[t, tokens : tokens + RANK, 0:tokens]
        out_left += dot(through, attended[t, 0:tokens, :])
    first.append(FACTOR * (out_left + dot_nt(out_right[...] * out_coefficient, out_weight[...])))
    first.append(jnp.zeros((RANK, SPLIT_LANES), F32))
    put(slice(0, SPLIT_LANES), jnp.concatenate(first, axis=0))
    at = slice(2 * RANK, 3 * RANK)
    wait_all(copies)
    down_left = FACTOR * (
        mine[at, :]
        + given[at, :].astype(F32)
        + dot_nt(down_right[...] * down_coefficient, down_weight[0])
    )
    hidden = down_left.shape[1]
    padded = (hidden + SPLIT_LANES - 1) // SPLIT_LANES * SPLIT_LANES
    down_left = jnp.concatenate([down_left, jnp.zeros((RANK, padded - hidden), F32)], axis=1)
    second = [
        down_left[:, j * SPLIT_LANES : (j + 1) * SPLIT_LANES] for j in range(padded // SPLIT_LANES)
    ]
    second += [
        row_sums[i : i + 1, j * SPLIT_LANES : (j + 1) * SPLIT_LANES]
        for i in range(2)
        for j in range(width // SPLIT_LANES)
    ]
    second += [heads_sums[0:1, i * columns : (i + 1) * columns] for i in range(3)]
    used = sum(r.shape[0] for r in second)
    second.append(jnp.zeros((5 * RANK - used, SPLIT_LANES), F32))
    put(slice(SPLIT_LANES, 2 * SPLIT_LANES), jnp.concatenate(second, axis=0))


def split_grads(*arrays):
    half, width = arrays[1].shape[1:]
    above, lanes = arrays[-1].shape
    return pl.pallas_call(
        split_grads_kernel,
        out_shape=shape((above + 5 * RANK, lanes), BF16),
        in_specs=[SMEM, ANY, ANY] + [VMEM] * (len(arrays) - 3),
        out_specs=VMEM,
        scratch_shapes=[pltpu.VMEM((1, 2 * half, width), BF16), pltpu.SemaphoreType.DMA((2,))],
        compiler_params=PARAMS,
        cost_estimate=cost(7),
        name="split_grads",
    )(*arrays)


def shared_grads_kernel(
    grads, heads_weight, heads_stats, heads_sums, qr, kr, vr, left, down, row, received,
    row_cross, arrived, out_dz, *refs,
):
    *blocks, terms_ref = refs
    tokens, width = out_dz.shape
    row_sums = gathered_sums(received, tokens)

    def put(group, rows):
        rows = rows.astype(BF16)
        lane_blocks = width // LANES
        for i in range(lane_blocks):
            terms_ref[group * lane_blocks + i] = rows[:, i * LANES : (i + 1) * LANES]

    columns = heads_weight.shape[1] // 3
    coefficient = -heads_sums[0:1, :] / heads_stats[0:1, :]
    throughs, norms = [], []
    for i, right in enumerate((qr, kr, vr)):
        at = slice(i * columns, (i + 1) * columns)
        dz = jnp.concatenate([grads[s, :, at] for s in range(len(blocks))], axis=0)
        throughs.append(dot_nt(right[...], dz))
        norms.append(right[...] * coefficient[:, at])
    through = jnp.concatenate(throughs, axis=0).astype(BF16)
    total = 0.0
    for s in range(0, len(blocks), 2):
        pair = jnp.concatenate([blocks[s][...], blocks[s + 1][...]], axis=0)
        total += jnp.dot(
            through[:, s * tokens : (s + 2) * tokens], pair, preferred_element_type=F32
        )
    for i in range(3):
        at = slice(i * columns, (i + 1) * columns)
        rows = total[i * RANK : (i + 1) * RANK]
        put(i, FACTOR * (rows + dot_nt(norms[i], heads_weight[:, at])))
    put(3, left[0:RANK, :])
    put(4, left[RANK : 2 * RANK, :])
    out_coefficient, down_coefficient = (
        -row_sums[i : i + 1, :] / row[i : i + 1, :] for i in range(2)
    )
    low = 0.0
    for t in range(arrived.shape[0]):
        low += dot_nt(arrived[t, tokens : tokens + RANK, :], arrived[t, 0:tokens, :])
    put(5, FACTOR * (dot(low, out_dz[...]) + row_cross[0] * out_coefficient))
    put(6, FACTOR * (down[...] + row_cross[1] * down_coefficient))
    put(7, jnp.zeros((RANK, width), F32))


def shared_grads(arrays, blocks):
    width = blocks[0].shape[1]
    return pl.pallas_call(
        shared_grads_kernel,
        out_shape=shape((8 * width // LANES, RANK, LANES), BF16),
        in_specs=[VMEM] * (len(arrays) + len(blocks)),
        out_specs=VMEM,
        compiler_params=PARAMS,
        cost_estimate=cost(8),
        name="shared_grads",
    )(*arrays, *blocks)


def on_device(
    hidden_in,
    segment_ids,
    attention_gain,
    mlp_gain,
    query_base,
    query_left,
    query_right,
    query_magnitude,
    key_base,
    key_left,
    key_right,
    key_magnitude,
    value_base,
    value_left,
    value_right,
    value_magnitude,
    output_base,
    output_left,
    output_right,
    output_magnitude,
    gate_base,
    gate_left,
    gate_right,
    gate_magnitude,
    up_base,
    up_left,
    up_right,
    up_magnitude,
    down_base,
    down_left,
    down_right,
    down_magnitude,
    cotangent,
):
    resid = hidden_in[0]
    cot = cotangent[0]
    rows, width = resid.shape
    segments = segment_ids[0]
    length = segments.shape[0]
    heads_width = query_base.shape[1]
    hidden = gate_base.shape[1]
    mlp_row = mlp_gain[None]
    zero_count = jnp.sum((segments == 0).astype(jnp.int32))
    one_count = jnp.sum((segments <= 1).astype(jnp.int32))
    place = jnp.stack(
        [lax.axis_index(a).astype(jnp.int32) for a in ("z", "xl", "y", "core")]
        + [zero_count, one_count]
    )

    _, _, normed_one = rms_forward(resid.astype(F32), attention_gain)
    other, below, above = x_swap(normed_one), z_up(normed_one), z_down(normed_one)

    piece = output_piece(after(place, normed_one), output_base, output_left.T, output_right)
    received = all_to_all(piece, TENSOR)

    hidden_bases = (gate_base.T, up_base.T, down_base)
    hidden_lefts = (gate_left.T, up_left.T, down_left.T)
    hidden_rights = (gate_right, up_right, down_right)
    heads_magnitude = jnp.concatenate([query_magnitude, key_magnitude, value_magnitude])[None]
    hidden_send, *hidden_sent, heads_weight, heads_stats, heads_cross = prepare_first(
        after(place, piece),
        hidden_bases,
        hidden_lefts,
        hidden_rights,
        (query_base, key_base, value_base),
        (query_left.T, key_left.T, value_left.T),
        (query_right, key_right, value_right),
        heads_magnitude,
    )
    other, below, above, _ = lax.optimization_barrier((other, below, above, heads_stats))

    starts = jnp.where(segments == 0, 0, jnp.where(segments == 1, zero_count, one_count))
    positions = (jnp.arange(length, dtype=jnp.int32) - starts).astype(F32)
    frequency = 10000.0 ** (-jnp.arange(0, HEAD_DIM, 2, dtype=F32) / HEAD_DIM)
    angles = positions[:, None] * frequency[None, :]
    cosine, sine = jnp.cos(angles), jnp.sin(angles)
    cosine = jnp.concatenate([cosine, cosine], axis=-1)
    sine = jnp.concatenate([-sine, sine], axis=-1)

    other_below, other_above, far_one = z_up(other), z_down(other), z_up(below)
    pulled = from_x_neighbour(after(hidden_send, received, other))
    second_place, received = lax.optimization_barrier((place, received))
    out_mine = of_everyone(received.reshape(width, piece.shape[2]), "y")
    hidden_magnitude = jnp.stack([gate_magnitude, up_magnitude])
    hidden_keep, out_weight, extra, row_cross, row_terms, near = prepare_second(
        second_place,
        hidden_bases,
        hidden_lefts,
        hidden_rights,
        (output_base, output_left.T, output_right),
        hidden_magnitude,
        hidden_sent,
        (normed_one, other, below, above, heads_weight, heads_stats, cosine, sine),
    )
    other_below, other_above, far_one, extra = lax.optimization_barrier(
        (other_below, other_above, far_one, extra)
    )
    other_far = z_down(other_above)
    extra_other = x_swap(extra)
    other_far, far_place, cot_held = lax.optimization_barrier((other_far, place, cot))
    cot_near = (z_up(cot_held), z_down(cot_held))
    row_blocks = [
        normed_one, other, below, above, other_below, other_above, far_one, other_far
    ]
    far = project_heads(4, far_place, row_blocks[4:], heads_weight, heads_stats, cosine, sine)
    attended, logs = attend(after(place, extra_other), near, far, row_terms)
    attended, *cot_near = lax.optimization_barrier((attended, *cot_near))
    half_rows = rows // 2
    cot_all = (
        cot,
        *cot_near,
        z_up(cot_near[0][:half_rows]),
        z_down(cot_near[1][half_rows:]),
    )
    out_columns = (out_mine, core_swap(out_mine))
    swapped = core_swap(after(pulled, attended))
    row_magnitude = jnp.stack([output_magnitude, down_magnitude])
    arrived = all_to_all(attended, TENSOR)

    out_raw, resid_two, normed_two, row = output_forward(
        after(place, *cot_all[3:], swapped), arrived, resid, row_magnitude, mlp_row, out_columns
    )
    tokens = gather_z(normed_two)
    *pieces, act, gate_back, up_back, hidden_sums, down_dz = feed_forward(
        place,
        tokens,
        cot_all,
        row[3:4],
        extra,
        extra_other,
        (hidden_send, hidden_keep, pulled, swapped),
    )
    back, forward = pieces[:5], pieces[5:]
    gate_up_lefts = jnp.concatenate([gate_left.T, up_left.T], axis=0)
    hidden_terms = hidden_grads(
        tokens,
        down_dz,
        act,
        gate_back,
        up_back,
        hidden_sums,
        extra,
        extra_other,
        gate_up_lefts,
        down_right,
    )
    gate_up_left, down_right_part, mine, sent = hidden_terms
    own, below, above, second = scatter_z(*back, lambda: mine)
    given = x_swap(sent)
    heads_lefts = jnp.concatenate([query_left.T, key_left.T, value_left.T], axis=0)
    heads_lows = low_terms(after(heads_lefts, second), row_blocks)
    gate_up_left, hidden_split = hidden_norms(
        after(place, heads_lows),
        gate_up_left,
        mine,
        given,
        extra,
        gate_up_lefts,
        hidden_send,
        hidden_keep,
    )
    forward = lax.optimization_barrier((*forward, mine))[:5]
    forward = scatter_z(*forward, lambda: (heads_lows, given))[:3]
    grad_two, out_dz, head_part, layer = output_back(
        after(place, gate_up_left),
        (own, below, above),
        forward,
        cot,
        out_raw,
        resid_two,
        row,
        mlp_row,
        output_right,
        out_columns,
        8,
    )
    received = all_to_all(head_part, TENSOR)

    heads_dz, heads_sums = attend_back(
        place, near, far, logs, received, cosine, sine, heads_stats
    )
    terms = shared_grads(
        (
            heads_dz,
            heads_weight,
            heads_stats,
            heads_sums,
            query_right,
            key_right,
            value_right,
            gate_up_left,
            down_right_part,
            row,
            received,
            row_cross,
            arrived,
            out_dz,
        ),
        row_blocks,
    )
    parts = heads_back(after(heads_dz, terms), heads_weight)
    hop, other_hop = z_up(parts[6]), z_down(parts[7])
    split = split_grads(
        after(place, parts[0]),
        hidden_send,
        hidden_keep,
        heads_dz,
        heads_lows,
        heads_stats,
        heads_sums,
        heads_cross,
        mine,
        given,
        row,
        received,
        output_right,
        down_right,
        out_weight,
        attended,
        hidden_split,
    )
    total = after(all_to_all(terms, ALL), split).astype(F32).sum(axis=0).astype(BF16)
    hop, other_hop, _ = lax.optimization_barrier((hop, other_hop, split))
    other_from_below = z_up(parts[5])
    other_from_above = z_down(add(parts[4], other_hop).astype(BF16))
    split = add(split, core_swap(split)).astype(BF16)
    split = add(split, lax.ppermute(split, "xh", SWAP)).astype(BF16)
    across = x_swap(add(parts[1], other_from_below, other_from_above).astype(BF16))
    from_below = z_up(add(parts[3], hop).astype(BF16))
    from_above = z_down(parts[2])
    grad_normed_one = add(parts[0], from_below, from_above, across)
    resid = resid.astype(F32)
    inverse = lax.rsqrt(jnp.mean(resid * resid, axis=-1, keepdims=True) + EPSILON)
    input_grad = grad_two + rms_backward(grad_normed_one, resid * inverse, inverse, attention_gain)
    split = add(split, lax.ppermute(split, "y", ((0, 1), (1, 0), (2, 3), (3, 2)))).astype(BF16)
    split = add(split, lax.ppermute(split, "y", ((0, 2), (2, 0), (1, 3), (3, 1))))
    hidden_split, split = split[: 3 * RANK, :hidden], split[3 * RANK :]
    total = after(of_everyone(total, ALL), across).reshape(8, width // LANES, RANK, LANES)
    total = total.transpose(0, 2, 1, 3).reshape(8, RANK, width).astype(F32)
    hidden_magnitude_grad = hidden_split[2 * RANK : 2 * RANK + 2] / hidden_magnitude
    heads, rest = split[:, :SPLIT_LANES], split[:, SPLIT_LANES : 2 * SPLIT_LANES]
    parts = (hidden + SPLIT_LANES - 1) // SPLIT_LANES
    down_left_grad = jnp.concatenate([rest[i * RANK : (i + 1) * RANK] for i in range(parts)], axis=1)
    at = parts * RANK
    row_magnitude_grad = rest[at : at + 2 * width // SPLIT_LANES].reshape(2, width) / row_magnitude
    at += 2 * width // SPLIT_LANES
    heads_magnitude_grad = rest[at : at + 3] / heads_magnitude.reshape(3, -1)
    return (
        layer[None],
        input_grad[None],
        total[0].T,
        heads[:RANK],
        heads_magnitude_grad[0],
        total[1].T,
        heads[RANK : 2 * RANK],
        heads_magnitude_grad[1],
        total[2].T,
        heads[2 * RANK : 3 * RANK],
        heads_magnitude_grad[2],
        heads[3 * RANK : 4 * RANK].T,
        total[5],
        row_magnitude_grad[0],
        total[3].T,
        hidden_split[:RANK],
        hidden_magnitude_grad[0],
        total[4].T,
        hidden_split[RANK : 2 * RANK],
        hidden_magnitude_grad[1],
        down_left_grad[:, :hidden].T,
        total[6],
        row_magnitude_grad[1],
    )


def solution(mesh):
    torus = Mesh(mesh.devices.reshape(4, 2, 2, 4, 2), ("y", "xh", "core", "z", "xl"))
    column = (P(None, TENSOR), P(), P(None, TENSOR), P(TENSOR))
    row = (P(TENSOR, None), P(TENSOR, None), P(), P())
    column_out, row_out = column[1:], row[1:]
    tokens = P(DP, TENSOR, None)
    return jax.shard_map(
        on_device,
        mesh=torus,
        in_specs=(
            tokens,
            P(DP, None),
            P(),
            P(),
            *column,
            *column,
            *column,
            *row,
            *column,
            *column,
            *row,
            tokens,
        ),
        out_specs=(
            tokens,
            tokens,
            *column_out,
            *column_out,
            *column_out,
            *row_out,
            *column_out,
            *column_out,
            *row_out,
        ),
        check_vma=False,
    )
```

```python
import functools

import jax
import jax.numpy as jnp
from jax import lax
from jax.experimental import pallas as pl
from jax.experimental.pallas import tpu as pltpu
from jax.sharding import Mesh
from jax.sharding import PartitionSpec as P

HEAD_DIM = 128
RANK = 16
ALPHA = 32
FACTOR = ALPHA / RANK
EPSILON = 1e-05
MASKED_SCORE = -1e30
DP = ("y", "xh", "core")
TENSOR = ("z", "xl")
ALL = DP + TENSOR
BF16 = jnp.bfloat16
F32 = jnp.float32

SWAP = ((0, 1), (1, 0))
UP = tuple((i, (i + 1) % 4) for i in range(4))
DOWN = tuple((i, (i + 3) % 4) for i in range(4))
SLOTS = ((0, 0), (0, 1), (-1, 0), (1, 0), (-1, 1), (1, 1), (2, 0), (2, 1))
SLOT_AT = ((0, 1), (3, 5), (6, 7), (2, 4))


def z_up(array):
    return lax.ppermute(array, "z", UP)


def z_down(array):
    return lax.ppermute(array, "z", DOWN)


def y_up(array):
    return lax.ppermute(array, "y", UP)


def y_down(array):
    return lax.ppermute(array, "y", DOWN)


def x_swap(array):
    return lax.ppermute(array, "xl", SWAP)


def core_swap(array):
    return lax.ppermute(array, "core", SWAP)


def from_x_neighbour(array):
    pairs = []
    for x in range(4):
        for core in range(2):
            source = (x ^ 1) if core else (x + 3 if x % 2 == 0 else x + 1) % 4
            pairs.append(
                ((source // 2) * 4 + core * 2 + source % 2, (x // 2) * 4 + core * 2 + x % 2)
            )
    return lax.ppermute(array, ("xh", "core", "xl"), tuple(pairs))


def add(*terms):
    total = terms[0].astype(F32)
    for term in terms[1:]:
        total = total + term.astype(F32)
    return total


def gather_z(own, meanwhile):
    half = own.shape[0] // 2
    below, above, _ = lax.optimization_barrier((z_up(own), z_down(own), meanwhile()))
    return own, below, above, z_up(below[:half]), z_down(above[half:])


def scatter_z(own, below, above, far_low, far_high, meanwhile):
    half = far_low.shape[0]
    low = z_up(far_low)
    high = z_down(far_high)
    low, high = lax.optimization_barrier((low, high, meanwhile()))[:2]
    above_sum = jnp.concatenate([add(above[:half], low).astype(BF16), above[half:]], axis=0)
    below_sum = jnp.concatenate([below[:half], add(below[half:], high).astype(BF16)], axis=0)
    return own, z_up(above_sum), z_down(below_sum), above_sum


def all_to_all(array, axes):
    return lax.all_to_all(array, axes, 0, 0, tiled=True)


def of_everyone(array, axes):
    count = lax.axis_size(axes)
    return all_to_all(jnp.broadcast_to(array[None], (count, *array.shape)), axes)


def dot(left, right):
    return jnp.dot(left.astype(BF16), right.astype(BF16), preferred_element_type=F32)


def dot_nt(left, right):
    return lax.dot_general(
        left.astype(BF16), right.astype(BF16), (((1,), (1,)), ((), ())), preferred_element_type=F32
    )


def dot_tn(left, right):
    return lax.dot_general(
        left.astype(BF16), right.astype(BF16), (((0,), (0,)), ((), ())), preferred_element_type=F32
    )


def after_all(*arrays):
    return lax.optimization_barrier(arrays)[:-1]


def rms_forward(resid, gain):
    inverse = lax.rsqrt(jnp.mean(resid * resid, axis=-1, keepdims=True) + EPSILON)
    normal = resid * inverse
    return normal, inverse, (normal * gain.astype(F32)).astype(BF16)


def rms_backward(grad_normed, normal, inverse, gain):
    scaled = grad_normed * gain.astype(F32)
    return inverse * (scaled - normal * jnp.mean(scaled * normal, axis=-1, keepdims=True))


VMEM = pl.BlockSpec(memory_space=pltpu.VMEM)
SMEM = pl.BlockSpec(memory_space=pltpu.SMEM)
ANY = pl.BlockSpec(memory_space=pl.ANY)
QUERY_ROWS = 256
SCORE_SCALE = HEAD_DIM ** (-0.5)
MIB = 1024 * 1024
LANES = 128
COST = 1.0
SQUARES, SCALE = RANK, RANK + 1
EXTRA_ROWS = 24


def shape(dims, dtype=F32):
    return jax.ShapeDtypeStruct(dims, dtype)


PARAMS = pltpu.CompilerParams(vmem_limit_bytes=60 * MIB)


def cost(micros):
    return pl.CostEstimate(
        flops=0, bytes_accessed=int(micros * COST * 3.69e6), transcendentals=0
    )


def after(array, *earlier):
    return lax.optimization_barrier((array, *earlier))[0]


def whole_spec(dims):
    return pl.BlockSpec(dims, lambda *_: (0,) * len(dims))


def prepare_heads_kernel(q, k, v, al, bl, cl, ar, br, cr, mag, weight_ref, stats_ref, cross_ref):
    step = pl.program_id(0)
    columns = q.shape[1]

    @pl.when(step == 0)
    def _():
        stats_ref[...] = jnp.zeros_like(stats_ref)
        cross_ref[...] = jnp.zeros_like(cross_ref)

    for i, (base, left, right) in enumerate(((q, al, ar), (k, bl, br), (v, cl, cr))):
        at_columns = slice(i * columns, (i + 1) * columns)
        factor = left[...].astype(BF16)
        weight = base[...].astype(F32) + dot_tn(FACTOR * factor, right[...])
        low = weight.astype(BF16)
        weight_ref[:, at_columns] = low
        stats_ref[0:1, at_columns] += jnp.sum(weight * weight, axis=0, keepdims=True)
        cross_ref[:, at_columns] += dot(factor, low)

    @pl.when(step == pl.num_programs(0) - 1)
    def _():
        stats_ref[1:2, :] = mag[...] * lax.rsqrt(stats_ref[0:1, :])


def output_piece_kernel(place, base, left, right, piece_ref):
    weight = (base[...].astype(F32) + FACTOR * dot_tn(left[...], right[...])).astype(BF16)
    for t in range(piece_ref.shape[0]):
        piece_ref[t] = weight


def output_piece(place, base, left, right):
    rows, width = base.shape
    columns = width // 8

    def column(i, place):
        return 0, 2 * place[2] + place[3]

    return pl.pallas_call(
        output_piece_kernel,
        grid_spec=pltpu.PrefetchScalarGridSpec(
            num_scalar_prefetch=1,
            grid=(1,),
            in_specs=[
                pl.BlockSpec((rows, columns), column),
                pl.BlockSpec((RANK, rows), lambda i, place: (0, 0)),
                pl.BlockSpec((RANK, columns), column),
            ],
            out_specs=pl.BlockSpec((8, rows, columns), lambda i, place: (0, 0, 0)),
        ),
        out_shape=shape((8, rows, columns), BF16),
        compiler_params=PARAMS,
        cost_estimate=cost(2.5),
        name="output_piece",
    )(place, base, left, right)


def halves(which):
    def index(place):
        return place[3] if which == 0 else 1 - place[3]

    return index


def adapted_rows(step, bases, factors, squares, sums, cross):
    rows, width = bases[0].shape
    lows = []
    for i, (base, (left, right)) in enumerate(zip(bases, factors)):
        weight = base[...].astype(F32) + dot(left, FACTOR * right)
        low = weight.astype(BF16)
        lows.append(low)
        if i < 2:
            square = weight * weight
            at = pl.ds(pl.multiple_of(step * rows, rows), rows)
            squares[i, at, :] = sum(square[:, j : j + LANES] for j in range(0, width, LANES))
        else:
            sums[...] += jnp.sum(weight * weight, axis=0, keepdims=True)
            cross[...] += dot_tn(left, low)
    return lows


def down_sublanes(factor):
    unit = (
        lax.broadcasted_iota(jnp.int32, (RANK, LANES), 0)
        == lax.broadcasted_iota(jnp.int32, (RANK, LANES), 1)
    ).astype(BF16)
    return dot_tn(factor, unit)


def prepare_send_kernel(
    place, g, u, d, gl, ul, dl, gr, ur, dr, send_ref, squares_ref, sums_ref, cross_ref, columns
):
    step = pl.program_id(0)
    rows = g.shape[0]

    @pl.when(step == 0)
    def _():
        for i, factor in enumerate((gr, ur, dl)):
            columns[i] = down_sublanes(factor[...])
        cross_ref[...] = jnp.zeros_like(cross_ref)
        sums_ref[...] = jnp.zeros_like(sums_ref)

    at = pl.ds(pl.multiple_of((pl.num_programs(0) * place[3] + step) * rows, rows), rows)
    factors = [(columns[i, at, 0:RANK], right[...]) for i, right in enumerate((gl, ul, dr))]
    lows = adapted_rows(step, (g, u, d), factors, squares_ref, sums_ref, cross_ref)
    for i, low in enumerate(lows):
        send_ref[i] = low


def prepare_keep_kernel(
    place, g, u, d, gl, ul, dl, gr, ur, dr, o, ol, orr, mag, squares_in, sums_in, cross_in,
    keep_ref, out_ref, extra_ref, cross_ref, terms_ref, squares, squares_all, columns, sums,
):
    step = pl.program_id(0)
    steps = pl.num_programs(0)
    rows = g.shape[0]
    out_rows, width = o.shape

    @pl.when(step == 0)
    def _():
        for i, factor in enumerate((gr, ur, dl)):
            columns[i] = down_sublanes(factor[...])
        columns[3, 0 : ol.shape[1], :] = down_sublanes(ol[...])
        cross_ref[0] = jnp.zeros_like(cross_in)
        cross_ref[1] = cross_in[...]
        sums[0:1, :] = jnp.zeros_like(sums_in)
        sums[1:2, :] = sums_in[...]

    at = pl.ds(pl.multiple_of((steps * (1 - place[3]) + step) * rows, rows), rows)
    factors = [(columns[i, at, 0:RANK], right[...]) for i, right in enumerate((gl, ul, dr))]
    lows = adapted_rows(step, (g, u, d), factors, squares, sums.at[1:2], cross_ref.at[1])
    for i, low in enumerate(lows):
        keep_ref[i] = low
    left = columns[3, pl.ds(pl.multiple_of(step * out_rows, out_rows), out_rows), 0:RANK]
    weight = o[...].astype(F32) + dot(left, FACTOR * orr[...])
    low = weight.astype(BF16)
    out_ref[...] = low
    cross_ref[0] += dot_tn(left, low)
    sums[0:1, :] += jnp.sum(weight * weight, axis=0, keepdims=True)

    @pl.when(step == steps - 1)
    def _():
        half = squares.shape[1]
        for core, part in ((place[3], squares_in), (1 - place[3], squares)):
            squares_all[:, pl.ds(pl.multiple_of(core * half, half), half), :] = part[...]
        extra_ref[...] = jnp.zeros_like(extra_ref)
        for i, right in enumerate((gr, ur)):
            extra_ref[i, 0:RANK, :] = right[...]
            total = lax.dot_general(
                jnp.ones((8, LANES), F32),
                squares_all[i],
                (((1,), (1,)), ((), ())),
                precision=lax.Precision.HIGHEST,
                preferred_element_type=F32,
            )
            extra_ref[i, SQUARES : SQUARES + 1, :] = total[0:1]
            extra_ref[i, SCALE : SCALE + 1, :] = mag[i : i + 1, :] * lax.rsqrt(total[0:1])
        extra_ref[2, 0:RANK, :] = dl[...]
        lanes = terms_ref.shape[2]
        total = jnp.concatenate(
            [sums[i : i + 1, j : j + lanes] for i in range(2) for j in range(0, width, lanes)], axis=0
        )
        high = total.astype(BF16)
        rest = (total - high.astype(F32)).astype(BF16)
        for t in range(terms_ref.shape[0]):
            terms_ref[t, 0:RANK, :] = ol[...].astype(BF16)
            terms_ref[t, RANK : RANK + 16, :] = high
            terms_ref[t, RANK + 16 :, :] = rest


HALF_STEPS = 2


def half_specs(which, hidden, width):
    rows = hidden // 2 // HALF_STEPS
    half = halves(which)

    def whole(*dims):
        return pl.BlockSpec(dims, lambda i, place: (0,) * len(dims))

    base = pl.BlockSpec((rows, width), lambda i, place: (HALF_STEPS * half(place) + i, 0))
    specs = [base] * 3 + [whole(RANK, width)] * 2 + [whole(RANK, hidden)] * 3 + [whole(RANK, width)]
    return specs, whole, pl.BlockSpec((3, rows, width), lambda i, place: (0, i, 0))


def prepare_send(place, bases, lefts, rights):
    hidden, width = bases[0].shape
    specs, whole, block = half_specs(0, hidden, width)
    return pl.pallas_call(
        prepare_send_kernel,
        grid_spec=pltpu.PrefetchScalarGridSpec(
            num_scalar_prefetch=1,
            grid=(HALF_STEPS,),
            in_specs=specs,
            out_specs=(block, whole(2, hidden // 2, LANES), whole(1, width), whole(RANK, width)),
            scratch_shapes=[pltpu.VMEM((3, hidden, LANES), F32)],
        ),
        out_shape=(
            shape((3, hidden // 2, width), BF16),
            shape((2, hidden // 2, LANES)),
            shape((1, width)),
            shape((RANK, width)),
        ),
        compiler_params=PARAMS,
        cost_estimate=cost(6),
        name="prepare_send",
    )(place, *bases, *lefts, *rights)


def prepare_heads(bases, lefts, rights, magnitude):
    width, columns = bases[0].shape
    rows = width // HALF_STEPS
    return pl.pallas_call(
        prepare_heads_kernel,
        grid=(HALF_STEPS,),
        out_shape=(
            shape((width, 3 * columns), BF16),
            shape((8, 3 * columns)),
            shape((RANK, 3 * columns)),
        ),
        in_specs=[pl.BlockSpec((rows, columns), lambda i: (i, 0))] * 3
        + [pl.BlockSpec((RANK, rows), lambda i: (0, i))] * 3
        + [whole_spec((RANK, columns))] * 3
        + [whole_spec((1, 3 * columns))],
        out_specs=(
            pl.BlockSpec((rows, 3 * columns), lambda i: (i, 0)),
            whole_spec((8, 3 * columns)),
            whole_spec((RANK, 3 * columns)),
        ),
        compiler_params=PARAMS,
        cost_estimate=cost(6),
        name="prepare_heads",
    )(*bases, *lefts, *rights, magnitude)


def prepare_second_kernel(place, *refs):
    inputs, near_inputs, outputs = refs[:16], refs[16:24], refs[24:]
    prepare_keep_kernel(place, *inputs, *outputs[:5], *outputs[6:])

    @pl.when(pl.program_id(0) == 0)
    def _():
        project_heads_kernel(0, place, *near_inputs, outputs[5])


def prepare_second(place, bases, lefts, rights, out, magnitude, sent, near):
    hidden, width = bases[0].shape
    out_rows = out[0].shape[0]
    specs, whole, block = half_specs(1, hidden, width)
    out_block = pl.BlockSpec((out_rows // HALF_STEPS, width), lambda i, place: (i, 0))
    rows, heads_width = near[0].shape[0], near[4].shape[1]
    return pl.pallas_call(
        prepare_second_kernel,
        grid_spec=pltpu.PrefetchScalarGridSpec(
            num_scalar_prefetch=1,
            grid=(HALF_STEPS,),
            in_specs=specs
            + [
                out_block,
                whole(RANK, out_rows),
                whole(RANK, width),
                whole(2, hidden),
                whole(2, hidden // 2, LANES),
                whole(1, width),
                whole(RANK, width),
            ]
            + [whole(*a.shape) for a in near],
            out_specs=(
                block,
                out_block,
                whole(3, EXTRA_ROWS, hidden),
                whole(2, RANK, width),
                whole(8, 3 * RANK, width // 8),
                whole(4, rows, heads_width),
            ),
            scratch_shapes=[
                pltpu.VMEM((2, hidden // 2, LANES), F32),
                pltpu.VMEM((2, hidden, LANES), F32),
                pltpu.VMEM((4, hidden, LANES), F32),
                pltpu.VMEM((8, width), F32),
            ],
        ),
        out_shape=(
            shape((3, hidden // 2, width), BF16),
            shape((out_rows, width), BF16),
            shape((3, EXTRA_ROWS, hidden)),
            shape((2, RANK, width)),
            shape((8, 3 * RANK, width // 8), BF16),
            shape((4, rows, heads_width), BF16),
        ),
        compiler_params=PARAMS,
        cost_estimate=cost(14),
        name="prepare_second",
    )(place, *bases, *lefts, *rights, *out, magnitude, *sent, *near)


def slot_of(place, block):
    away = lax.rem(block // 2 - place[0] + 4, 4)
    other = jnp.where(place[1] == block % 2, 0, 1)
    return jnp.where(
        away == 0, other, jnp.where(away == 1, 3 + 2 * other, jnp.where(away == 2, 6 + other, 2 + 2 * other))
    )


def block_of(place, slot):
    dz, dx = SLOTS[slot]
    return 2 * lax.rem(place[0] + dz + 4, 4) + (place[1] if dx == 0 else 1 - place[1])


def turned(values, cosine, sine):
    return values * cosine + pltpu.roll(values, HEAD_DIM // 2, 1) * sine


def turned_back(grads, cosine, sine):
    return grads * cosine - pltpu.roll(grads, HEAD_DIM // 2, 1) * sine


def project_heads_kernel(first_slot, place, b0, b1, b2, b3, weight, stats, cosine, sine, out_ref):
    blocks = jnp.concatenate([b[...] for b in (b0, b1, b2, b3)], axis=0)
    rows = b0.shape[0]
    width = weight.shape[1]
    values = jnp.dot(blocks, weight[...], preferred_element_type=F32) * stats[1:2, :]
    for s in range(4):
        at = pl.ds(pl.multiple_of(block_of(place, first_slot + s) * rows, rows), rows)
        cos, sin = cosine[at, :], sine[at, :]
        for head in range(width // HEAD_DIM):
            head_at = slice(head * HEAD_DIM, (head + 1) * HEAD_DIM)
            part = values[s * rows : (s + 1) * rows, head_at]
            if head < 2 * width // HEAD_DIM // 3:
                part = turned(part, cos, sin)
            out_ref[s, :, head_at] = part.astype(BF16)


def project_heads(first_slot, place, blocks, weight, stats, cosine, sine):
    rows = blocks[0].shape[0]
    return pl.pallas_call(
        functools.partial(project_heads_kernel, first_slot),
        out_shape=shape((4, rows, weight.shape[1]), BF16),
        in_specs=[SMEM] + [VMEM] * 8,
        out_specs=VMEM,
        compiler_params=PARAMS,
        cost_estimate=cost(5.5),
        name="project_heads",
    )(place, *blocks, weight, stats, cosine, sine)


def low_kernel(lefts_t, *refs):
    *blocks, out_ref = refs
    rows = blocks[0].shape[0]
    for s, block in enumerate(blocks):
        out_ref[:, s * rows : (s + 1) * rows] = dot_nt(lefts_t[...], block[...]).astype(BF16)


def low_terms(lefts_t, blocks):
    rows = blocks[0].shape[0]
    return pl.pallas_call(
        low_kernel,
        out_shape=shape((lefts_t.shape[0], rows * len(blocks)), BF16),
        in_specs=[VMEM] * (1 + len(blocks)),
        out_specs=VMEM,
        compiler_params=PARAMS,
        cost_estimate=cost(4.5),
        name="low_terms",
    )(lefts_t, *blocks)


def masked_scores(place, query, key, first_row):
    scores = dot_nt(query, key) * SCORE_SCALE
    row = first_row + lax.broadcasted_iota(jnp.int32, (query.shape[0], 1), 0)
    start = jnp.where(row < place[4], 0, jnp.where(row < place[5], place[4], place[5]))
    column = lax.broadcasted_iota(jnp.int32, scores.shape, 1)
    return jnp.where((column <= row) & (column >= start), scores, MASKED_SCORE)


def place_blocks(place, near, far, held):
    rows = near.shape[1]
    for block in range(2 * near.shape[0]):
        slot = slot_of(place, block)
        at = slice(block * rows, (block + 1) * rows)

        @pl.when(slot < 4)
        def _():
            held[at, :] = near[jnp.minimum(slot, 3)]

        @pl.when(slot >= 4)
        def _():
            held[at, :] = far[jnp.maximum(slot - 4, 0)]


def attend_kernel(place, near, far, terms, out_ref, log_ref, held):
    length = held.shape[0]
    width = out_ref.shape[2]
    rows = near.shape[1]
    out_ref[:, rows:, :] = terms[...]
    place_blocks(place, near, far, held)
    for head in range(width // HEAD_DIM):
        at = slice(head * HEAD_DIM, (head + 1) * HEAD_DIM)
        key_at = slice(width + head * HEAD_DIM, width + (head + 1) * HEAD_DIM)
        value_at = slice(2 * width + head * HEAD_DIM, 2 * width + (head + 1) * HEAD_DIM)
        for first in range(0, length, QUERY_ROWS):
            last = first + QUERY_ROWS
            scores = masked_scores(place, held[first:last, at], held[:last, key_at], first)
            largest = jnp.max(scores, axis=-1, keepdims=True)
            weights = jnp.exp(scores - largest)
            totals = jnp.sum(weights, axis=-1, keepdims=True)
            probs = (weights * (1.0 / totals)).astype(BF16)
            out = jnp.dot(probs, held[:last, value_at], preferred_element_type=F32)
            for i in range(QUERY_ROWS // rows):
                out_ref[first // rows + i, 0:rows, at] = out[i * rows : (i + 1) * rows].astype(BF16)
            log_ref[first:last, at] = jnp.broadcast_to(
                largest + jnp.log(totals), (QUERY_ROWS, HEAD_DIM)
            )


def attend(place, near, far, terms):
    blocks, rows, width = near.shape
    length = 2 * blocks * rows
    groups = terms.shape[0]
    return pl.pallas_call(
        attend_kernel,
        out_shape=(
            shape((groups, length // groups + terms.shape[1], width // 3), BF16),
            shape((length, width // 3)),
        ),
        in_specs=[SMEM] + [VMEM] * 3,
        out_specs=(VMEM, VMEM),
        scratch_shapes=[pltpu.VMEM((length, width), BF16)],
        compiler_params=PARAMS,
        cost_estimate=cost(7.5),
        name="attend",
    )(place, near, far, terms)


def attend_back_kernel(
    place, near, far, log_ref, grad_ref, cosine, sine, stats,
    out_ref, sum_ref, held, total,
):
    length = held.shape[0]
    width = grad_ref.shape[2]
    rows = near.shape[1]
    place_blocks(place, near, far, held)
    for head in range(width // HEAD_DIM):
        at = slice(head * HEAD_DIM, (head + 1) * HEAD_DIM)
        key_at = slice(width + head * HEAD_DIM, width + (head + 1) * HEAD_DIM)
        value_at = slice(2 * width + head * HEAD_DIM, 2 * width + (head + 1) * HEAD_DIM)
        for first in reversed(range(0, length, QUERY_ROWS)):
            last = first + QUERY_ROWS
            query = held[first:last, at]
            key = held[:last, key_at]
            scores = masked_scores(place, query, key, first)
            probs = jnp.exp(scores - log_ref[first:last, head * HEAD_DIM : head * HEAD_DIM + 1])
            grad = jnp.concatenate(
                [grad_ref[i, 0:rows, at] for i in range(first // rows, last // rows)], axis=0
            )
            grad_probs = dot_nt(grad, held[:last, value_at])
            inner = jnp.sum(grad_probs * probs, axis=-1, keepdims=True)
            grad_scores = (probs * (grad_probs - inner) * SCORE_SCALE).astype(BF16)
            total[first:last, at] = jnp.dot(grad_scores, key, preferred_element_type=F32)
            grad_key = dot_tn(grad_scores, query)
            grad_value = dot_tn(probs, grad)
            if last == length:
                total[:, key_at] = grad_key
                total[:, value_at] = grad_value
            else:
                total[:last, key_at] += grad_key
                total[:last, value_at] += grad_value
    heads = 3 * width // HEAD_DIM
    for head in range(heads):
        at = slice(head * HEAD_DIM, (head + 1) * HEAD_DIM)
        sums = jnp.zeros((1, HEAD_DIM), F32)
        for block in range(length // rows):
            block_at = slice(block * rows, (block + 1) * rows)
            grads = total[block_at, at]
            values = held[block_at, at].astype(F32)
            if head < 2 * heads // 3:
                cos, sin = cosine[block_at, :], sine[block_at, :]
                grads = turned_back(grads, cos, sin)
                values = turned_back(values, cos, sin)
            sums += jnp.sum(grads * values, axis=0, keepdims=True)
            out_ref[slot_of(place, block), :, at] = (grads * stats[1:2, at]).astype(BF16)
        sum_ref[:, at] = jnp.broadcast_to(sums, (8, HEAD_DIM))


def attend_back(place, near, far, logs, grad, cosine, sine, stats):
    blocks, rows, width = near.shape
    length = 2 * blocks * rows
    return pl.pallas_call(
        attend_back_kernel,
        out_shape=(shape((2 * blocks, rows, width), BF16), shape((8, width))),
        in_specs=[SMEM] + [VMEM] * 7,
        out_specs=(VMEM, VMEM),
        scratch_shapes=[pltpu.VMEM((length, width), BF16), pltpu.VMEM((length, width), F32)],
        compiler_params=PARAMS,
        cost_estimate=cost(10.5),
        name="attend_back",
    )(place, near, far, logs, grad, cosine, sine, stats)


def heads_back_kernel(grads, source, *refs):
    *outs, dz, weight, sems = refs
    rows = grads.shape[1]
    chunks = weight.shape[0]
    columns = weight.shape[1]
    copies = [
        pltpu.make_async_copy(source.at[pl.ds(i * columns, columns)], weight.at[i], sems.at[i])
        for i in range(chunks)
    ]
    start_all([copies])
    for s in range(len(outs)):
        dz[s * rows : (s + 1) * rows, :] = grads[s]
    for i in range(chunks):
        copies[i].wait()
        part = dot_nt(dz[...], weight[i]).astype(BF16)
        for s, out in enumerate(outs):
            out[:, i * columns : (i + 1) * columns] = part[s * rows : (s + 1) * rows]


def weight_copies(mine, others, buffer, sems):
    return [
        pltpu.make_async_copy(source.at[i], buffer.at[2 * i + j], sems.at[2 * i + j])
        for i in range(mine.shape[0])
        for j, source in enumerate((mine, others))
    ]


def start_all(copies):
    for group in copies:
        for copy in group:
            copy.start()


def wait_all(group):
    for copy in group:
        copy.wait()


def column_of(place, i, lanes):
    core = place[3] if i % 2 == 0 else 1 - place[3]
    return pl.ds(pl.multiple_of((2 * (i // 2) + core) * lanes, lanes), lanes)


def output_kernel(
    place, arrived, resid, magnitude, gain, mine, others, raw_ref, resid_ref, normed_ref, row_ref, buffer, sems
):
    copies = weight_copies(mine, others, buffer, sems)
    start_all([copies])
    rows = resid.shape[0]
    groups, lanes = arrived.shape[0], arrived.shape[2]
    tokens = jnp.concatenate([arrived[t, 0:rows, :] for t in range(groups)], axis=1)
    squares = 0.0
    for t in range(groups):
        parts = arrived[t, rows + RANK : rows + 3 * RANK, :].astype(F32)
        squares += parts[0:RANK] + parts[RANK : 2 * RANK]
    squares = jnp.concatenate(
        [
            jnp.concatenate([squares[i * 8 + j : i * 8 + j + 1] for j in range(8)], axis=1)
            for i in range(2)
        ],
        axis=0,
    )
    scales = magnitude[...] * lax.rsqrt(squares)
    row_ref[0:2, :] = squares
    row_ref[2:4, :] = scales
    row_ref[4:8, :] = jnp.zeros((4, squares.shape[1]), F32)
    for i, copy in enumerate(copies):
        copy.wait()
        raw_ref[:, column_of(place, i, lanes)] = jnp.dot(
            tokens, buffer[i], preferred_element_type=F32
        )
    resid_two = resid[...].astype(F32) + raw_ref[...] * scales[0:1]
    resid_ref[...] = resid_two
    _, _, normed_ref[...] = rms_forward(resid_two, gain[...])


def output_forward(place, arrived, resid, magnitude, gain, columns):
    rows, width = resid.shape
    return pl.pallas_call(
        output_kernel,
        out_shape=(
            shape((rows, width)),
            shape((rows, width)),
            shape((rows, width), BF16),
            shape((8, width)),
        ),
        in_specs=[SMEM] + [VMEM] * 4 + [ANY] * len(columns),
        out_specs=(VMEM,) * 4,
        scratch_shapes=[
            pltpu.VMEM((8, *columns[0].shape[1:]), BF16),
            pltpu.SemaphoreType.DMA((8,)),
        ],
        compiler_params=PARAMS,
        cost_estimate=cost(7.5),
        name="output_forward",
    )(place, arrived, resid, magnitude, gain, *columns)


def output_back_kernel(
    place, own, below, above, down_own, down_below, down_above, cot, raw, resid, row, gain, right, mine,
    others, grad_ref, dz_ref, head_ref, layer_ref, buffer, total, sems,
):
    copies = weight_copies(mine, others, buffer, sems)
    start_all([copies])
    scales = row[2:4, :]
    grad_normed = own[...].astype(F32) + below[...].astype(F32) + above[...].astype(F32)
    resid_two = resid[...]
    cotangent = cot[...].astype(F32)
    inverse = lax.rsqrt(jnp.mean(resid_two * resid_two, axis=-1, keepdims=True) + EPSILON)
    grad = cotangent + rms_backward(grad_normed, resid_two * inverse, inverse, gain[...])
    grad_ref[...] = grad
    dz = (grad * scales[0:1]).astype(BF16)
    dz_ref[...] = dz
    down = (
        down_own[...].astype(F32) + down_below[...].astype(F32) + down_above[...].astype(F32)
    ) * scales[1:2]
    layer_ref[...] = (resid_two + down).astype(BF16)
    sums = (
        jnp.sum(grad * raw[...], axis=0, keepdims=True) * scales[0:1],
        jnp.sum(cotangent * down, axis=0, keepdims=True),
    )
    rows, lanes = dz.shape[0], buffer.shape[2]
    through = dot_nt(right[...], dz)
    terms = jnp.concatenate(
        [jnp.concatenate([through, jnp.zeros((RANK, lanes - rows), F32)], axis=1)]
        + [s[:, j * lanes : (j + 1) * lanes] for s in sums for j in range(8)],
        axis=0,
    ).astype(BF16)
    for i, copy in enumerate(copies):
        copy.wait()
        part = dot_nt(dz_ref[:, column_of(place, i, lanes)], buffer[i])
        if i == 0:
            total[...] = part
        else:
            total[...] += part
    for t in range(head_ref.shape[0]):
        head_ref[t, 0:rows, :] = total[:, t * lanes : (t + 1) * lanes].astype(BF16)
        head_ref[t, rows:, :] = terms


def output_back(place, back, forward, cot, raw, resid, row, gain, right, columns, groups):
    rows, width = resid.shape
    return pl.pallas_call(
        output_back_kernel,
        out_shape=(
            shape((rows, width)),
            shape((rows, width), BF16),
            shape((groups, rows + 2 * RANK, width // groups), BF16),
            shape((rows, width), BF16),
        ),
        in_specs=[SMEM] + [VMEM] * 12 + [ANY] * len(columns),
        out_specs=(VMEM,) * 4,
        scratch_shapes=[
            pltpu.VMEM((8, *columns[0].shape[1:]), BF16),
            pltpu.VMEM((rows, width), F32),
            pltpu.SemaphoreType.DMA((8,)),
        ],
        compiler_params=PARAMS,
        cost_estimate=cost(8),
        name="output_back",
    )(place, *back, *forward, cot, raw, resid, row, gain, right, *columns)


def hidden_copies(place, halves_of, planes, buffer, sems):
    half = buffer.shape[2] // 2
    copies = []
    for c in range(2):
        for k, plane in enumerate(planes):
            for j, which in enumerate((place[3], 1 - place[3])):
                rows = pl.ds(pl.multiple_of(which * half, half), half)
                copies.append(
                    pltpu.make_async_copy(
                        halves_of[2 * c + j].at[plane],
                        buffer.at[c, k, rows],
                        sems.at[2 * len(planes) * c + 2 * k + j],
                    )
                )
    return copies


def ends_of(rows):
    return (0, rows, 2 * rows, 3 * rows, 3 * rows + rows // 2, 4 * rows)


def hidden_start_kernel(
    place, cot_own, cot_below, cot_above, cot_low, cot_high, down_scale, send, keep, pulled, swapped,
    grad_ref, dz_ref, buffer, sems,
):
    copies = hidden_copies(place, (send, keep, pulled, swapped), (2,), buffer, sems)
    start_all([copies])
    ends = ends_of(cot_own.shape[0])
    for i, block in enumerate((cot_own, cot_below, cot_above, cot_low, cot_high)):
        dz_ref[ends[i] : ends[i + 1], :] = (block[...].astype(F32) * down_scale[...]).astype(BF16)
    for c in range(2):
        wait_all(copies[2 * c : 2 * c + 2])
        grad_ref[c] = dot_nt(dz_ref[...], buffer[c, 0]).astype(BF16)


def hidden_start(place, cot, down_scale, weights):
    rows, width = cot[0].shape
    hidden = 2 * weights[0].shape[1]
    return pl.pallas_call(
        hidden_start_kernel,
        out_shape=(shape((2, 4 * rows, hidden), BF16), shape((4 * rows, width), BF16)),
        in_specs=[SMEM] + [VMEM] * 6 + [ANY] * 4,
        out_specs=(VMEM,) * 2,
        scratch_shapes=[pltpu.VMEM((2, 1, hidden, width), BF16), pltpu.SemaphoreType.DMA((4,))],
        compiler_params=PARAMS,
        cost_estimate=cost(7),
        name="hidden_start",
    )(place, *cot, down_scale, *weights)


def hidden_middle_kernel(
    place, own, below, above, far_low, far_high, grads, extra, extra_other, send, keep, pulled, swapped,
    f0, f1, f2, f3, f4, act_ref, gate_ref, up_ref, sum_ref, tokens, buffer, sems,
):
    copies = hidden_copies(place, (send, keep, pulled, swapped), (0, 1, 2), buffer, sems)
    start_all([copies])
    ends = ends_of(own.shape[0])
    for i, block in enumerate((own, below, above, far_low, far_high)):
        tokens[ends[i] : ends[i + 1], :] = block[...]
    sum_ref[...] = jnp.zeros_like(sum_ref)
    for c in range(2):
        factors = (extra, extra_other)[c]
        gate_scale = factors[0, SCALE : SCALE + 1, :]
        up_scale = factors[1, SCALE : SCALE + 1, :]
        wait_all(copies[6 * c : 6 * c + 2])
        gate = dot_nt(tokens[...], buffer[c, 0]) * gate_scale
        wait_all(copies[6 * c + 2 : 6 * c + 4])
        upper = dot_nt(tokens[...], buffer[c, 1]) * up_scale
        grad = grads[c].astype(F32)
        sigmoid = 1.0 / (1.0 + jnp.exp(-gate))
        silu = gate * sigmoid
        act_ref[c] = (silu * upper).astype(BF16)
        grad_up = grad * silu
        grad_gate = grad * upper * (sigmoid + silu * (1.0 - sigmoid))
        sum_ref[c, 0:1, :] = jnp.sum(grad_gate * gate, axis=0, keepdims=True)
        sum_ref[c, 1:2, :] = jnp.sum(grad_up * upper, axis=0, keepdims=True)
        gate_ref[c] = (grad_gate * gate_scale).astype(BF16)
        up_ref[c] = (grad_up * up_scale).astype(BF16)
        wait_all(copies[6 * c + 4 : 6 * c + 6])
    columns = 512
    outs = (f0, f1, f2, f3, f4)
    for at in range(0, tokens.shape[1], columns):
        part = dot(act_ref[0], buffer[0, 2, :, at : at + columns])
        part = (part + dot(act_ref[1], buffer[1, 2, :, at : at + columns])).astype(BF16)
        for i, out in enumerate(outs):
            out[:, at : at + columns] = part[ends[i] : ends[i + 1]]


def hidden_middle(place, tokens, grads, extra, extra_other, weights):
    rows, width = tokens[0].shape
    hidden = extra.shape[2]
    total = 4 * rows
    return pl.pallas_call(
        hidden_middle_kernel,
        out_shape=(
            *(shape((n, width), BF16) for n in (rows, rows, rows, rows // 2, rows // 2)),
            *(shape((2, total, hidden), BF16),) * 3,
            shape((2, 8, hidden)),
        ),
        in_specs=[SMEM] + [VMEM] * 8 + [ANY] * 4,
        out_specs=(VMEM,) * 9,
        scratch_shapes=[
            pltpu.VMEM((total, width), BF16),
            pltpu.VMEM((2, 3, hidden, width), BF16),
            pltpu.SemaphoreType.DMA((12,)),
        ],
        compiler_params=PARAMS,
        cost_estimate=cost(20),
        name="hidden_middle",
    )(place, *tokens, grads, extra, extra_other, *weights)


def hidden_back_kernel(first, place, gate, upper, send, keep, pulled, swapped, *refs):
    *outs, total, buffer, sems = refs
    copies = hidden_copies(place, (send, keep, pulled, swapped), (0, 1), buffer, sems)
    start_all([copies])
    rows = total.shape[0]
    for c in range(2):
        for k, back in enumerate((gate, upper)):
            wait_all(copies[4 * c + 2 * k : 4 * c + 2 * k + 2])
            part = dot(back[c, first : first + rows, :], buffer[c, k])
            if c + k == 0:
                total[...] = part
            else:
                total[...] += part
    at = 0
    for out in outs:
        out[...] = total[at : at + out.shape[0], :].astype(BF16)
        at += out.shape[0]


def hidden_back(far, place, gate, upper, weights, rows):
    width = weights[0].shape[2]
    hidden = gate.shape[2]
    counts = (rows // 2, rows // 2) if far else (rows, rows, rows)
    return pl.pallas_call(
        functools.partial(hidden_back_kernel, 3 * rows if far else 0),
        out_shape=tuple(shape((n, width), BF16) for n in counts),
        in_specs=[SMEM] + [VMEM] * 2 + [ANY] * 4,
        out_specs=(VMEM,) * len(counts),
        scratch_shapes=[
            pltpu.VMEM((sum(counts), width), F32),
            pltpu.VMEM((2, 2, hidden, width), BF16),
            pltpu.SemaphoreType.DMA((8,)),
        ],
        compiler_params=PARAMS,
        cost_estimate=cost(8),
        name="hidden_back",
    )(place, gate, upper, *weights)


def hidden_grads_kernel(
    own, below, above, far_low, far_high, dz, act, gate, upper, sums, extra, extra_other, lefts_t,
    down_right, left_ref, down_ref, mine_ref, sent_ref,
):
    tokens = jnp.concatenate([r[...] for r in (own, below, above, far_low, far_high)], axis=0)
    lows = dot_nt(lefts_t[...], tokens)
    down_through = dot_nt(down_right[...], dz[...])
    throughs = [0.0, 0.0]
    low_down = 0.0
    for c, (factors, out) in enumerate(((extra, mine_ref), (extra_other, sent_ref))):
        for i, back in enumerate((gate, upper)):
            throughs[i] += dot_nt(factors[i, 0:RANK, :], back[c])
            out[i * RANK : (i + 1) * RANK, :] = dot(lows[i * RANK : (i + 1) * RANK], back[c]).astype(
                out.dtype
            )
        low_down += dot_nt(factors[2, 0:RANK, :], act[c])
        out[2 * RANK : 3 * RANK, :] = dot(down_through, act[c]).astype(out.dtype)
        out[3 * RANK :, :] = jnp.concatenate(
            [sums[c], jnp.zeros_like(sums[c])], axis=0
        ).astype(out.dtype)
    through = jnp.concatenate(throughs, axis=0)
    left_ref[...] = dot(through, tokens)
    down_ref[...] = dot(low_down, dz[...])


def hidden_grads(tokens, dz, act, gate, upper, sums, extra, extra_other, lefts_t, down_right):
    width = dz.shape[1]
    hidden = act.shape[2]
    return pl.pallas_call(
        hidden_grads_kernel,
        out_shape=(
            shape((2 * RANK, width)),
            shape((RANK, width)),
            shape((4 * RANK, hidden)),
            shape((4 * RANK, hidden), BF16),
        ),
        in_specs=[VMEM] * 14,
        out_specs=(VMEM,) * 4,
        compiler_params=PARAMS,
        cost_estimate=cost(8.4),
        name="hidden_grads",
    )(*tokens, dz, act, gate, upper, sums, extra, extra_other, lefts_t, down_right)


def half_copies(place, send, keep, planes, buffer, sems):
    half = buffer.shape[1] // 2
    copies = []
    for j, (source, which) in enumerate(((send, place[3]), (keep, 1 - place[3]))):
        rows = pl.ds(pl.multiple_of(which * half, half), half)
        copies.append(
            pltpu.make_async_copy(source.at[planes], buffer.at[:, rows], sems.at[j])
        )
    return copies


def hidden_norms_kernel(
    place, left, mine, given, extra, lefts_t, send, keep, left_ref, split_ref, weight, sems
):
    copies = half_copies(place, send, keep, slice(0, 2), weight, sems)
    start_all([copies])
    wait_all(copies)
    hidden = mine.shape[1]
    parts = mine[...] + given[...].astype(F32)
    rows = []
    for i in range(2):
        sums = parts[3 * RANK + i : 3 * RANK + i + 1, :]
        coefficient = -sums / extra[i, SQUARES : SQUARES + 1, :]
        at = slice(i * RANK, (i + 1) * RANK)
        left_ref[at, :] = FACTOR * (
            left[at, :] + dot(extra[i, 0:RANK, :] * coefficient, weight[i])
        )
        rows.append(
            FACTOR * (parts[at, :] + dot_nt(lefts_t[at, :], weight[i]) * coefficient)
        )
    rows.append(parts[3 * RANK :, :])
    split_ref[:, 0:hidden] = jnp.concatenate(rows, axis=0).astype(BF16)
    split_ref[:, hidden:] = jnp.zeros((3 * RANK, split_ref.shape[1] - hidden), BF16)


def hidden_norms(place, left, mine, given, extra, lefts_t, send, keep):
    width, hidden = left.shape[1], mine.shape[1]
    lanes = (hidden + LANES - 1) // LANES * LANES
    return pl.pallas_call(
        hidden_norms_kernel,
        out_shape=(shape((2 * RANK, width)), shape((3 * RANK, lanes), BF16)),
        in_specs=[SMEM] + [VMEM] * 5 + [ANY] * 2,
        out_specs=(VMEM, VMEM),
        scratch_shapes=[pltpu.VMEM((2, hidden, width), BF16), pltpu.SemaphoreType.DMA((2,))],
        compiler_params=PARAMS,
        cost_estimate=cost(5),
        name="hidden_norms",
    )(place, left, mine, given, extra, lefts_t, send, keep)


SPLIT_LANES = 256


def gathered_sums(received, tokens):
    sums = 0.0
    for t in range(received.shape[0]):
        sums += received[t, tokens + RANK : tokens + 2 * RANK, :].astype(F32)
    return jnp.concatenate(
        [
            jnp.concatenate([sums[8 * i + j : 8 * i + j + 1] for j in range(8)], axis=1)
            for i in range(2)
        ],
        axis=0,
    )


def split_grads_kernel(
    place, send, keep, grads, lows, heads_stats, heads_sums, heads_cross, mine, given, row, received,
    out_right, down_right, out_weight, attended, hidden_split, split_ref, down_weight, sems,
):
    copies = half_copies(place, send, keep, slice(2, 3), down_weight, sems)
    start_all([copies])
    width = row.shape[1]
    columns = heads_sums.shape[1] // 3
    slots, tokens = grads.shape[:2]
    row_sums = gathered_sums(received, tokens)
    above = hidden_split.shape[0]
    split_ref[0:above, :] = hidden_split[...]
    split_ref[above:, 2 * SPLIT_LANES :] = jnp.zeros(
        (split_ref.shape[0] - above, split_ref.shape[1] - 2 * SPLIT_LANES), BF16
    )

    def put(lanes, values):
        split_ref[above:, lanes] = values.astype(BF16)

    coefficient = -heads_sums[0:1, :] / heads_stats[0:1, :]
    first = []
    for i in range(3):
        at = slice(i * columns, (i + 1) * columns)
        dz = jnp.concatenate([grads[s, :, at] for s in range(slots)], axis=0)
        first.append(
            FACTOR
            * (
                jnp.dot(lows[i * RANK : (i + 1) * RANK, :], dz, preferred_element_type=F32)
                + heads_cross[:, at] * coefficient[:, at]
            )
        )
    out_coefficient, down_coefficient = (
        -row_sums[i : i + 1, :] / row[i : i + 1, :] for i in range(2)
    )
    out_left = 0.0
    for t in range(received.shape[0]):
        through = received[t, tokens : tokens + RANK, 0:tokens]
        out_left += dot(through, attended[t, 0:tokens, :])
    first.append(FACTOR * (out_left + dot_nt(out_right[...] * out_coefficient, out_weight[...])))
    first.append(jnp.zeros((RANK, SPLIT_LANES), F32))
    put(slice(0, SPLIT_LANES), jnp.concatenate(first, axis=0))
    at = slice(2 * RANK, 3 * RANK)
    wait_all(copies)
    down_left = FACTOR * (
        mine[at, :]
        + given[at, :].astype(F32)
        + dot_nt(down_right[...] * down_coefficient, down_weight[0])
    )
    hidden = down_left.shape[1]
    padded = (hidden + SPLIT_LANES - 1) // SPLIT_LANES * SPLIT_LANES
    down_left = jnp.concatenate([down_left, jnp.zeros((RANK, padded - hidden), F32)], axis=1)
    second = [
        down_left[:, j * SPLIT_LANES : (j + 1) * SPLIT_LANES] for j in range(padded // SPLIT_LANES)
    ]
    second += [
        row_sums[i : i + 1, j * SPLIT_LANES : (j + 1) * SPLIT_LANES]
        for i in range(2)
        for j in range(width // SPLIT_LANES)
    ]
    second += [heads_sums[0:1, i * columns : (i + 1) * columns] for i in range(3)]
    used = sum(r.shape[0] for r in second)
    second.append(jnp.zeros((5 * RANK - used, SPLIT_LANES), F32))
    put(slice(SPLIT_LANES, 2 * SPLIT_LANES), jnp.concatenate(second, axis=0))


def tail_kernel(*refs):
    inputs, (weight, *rest) = refs[:17], refs[17:]
    outs, (split_ref, dz, buffer, sems, down_weight, down_sems) = rest[:-6], rest[-6:]
    heads_back_kernel(inputs[3], weight, *outs, dz, buffer, sems)
    split_grads_kernel(*inputs, split_ref, down_weight, down_sems)


def tail(arrays, weight):
    half, width = arrays[1].shape[1:]
    above, lanes = arrays[-1].shape
    blocks, rows, columns = arrays[3].shape
    chunks = 4
    return pl.pallas_call(
        tail_kernel,
        out_shape=(
            *(shape((rows, width), BF16),) * blocks,
            shape((above + 5 * RANK, lanes), BF16),
        ),
        in_specs=[SMEM, ANY, ANY] + [VMEM] * (len(arrays) - 3) + [ANY],
        out_specs=(VMEM,) * (blocks + 1),
        scratch_shapes=[
            pltpu.VMEM((blocks * rows, columns), BF16),
            pltpu.VMEM((chunks, width // chunks, columns), BF16),
            pltpu.SemaphoreType.DMA((chunks,)),
            pltpu.VMEM((1, 2 * half, width), BF16),
            pltpu.SemaphoreType.DMA((2,)),
        ],
        compiler_params=PARAMS,
        cost_estimate=cost(13),
        name="tail",
    )(*arrays, weight)


def shared_grads_kernel(
    grads, heads_weight, heads_stats, heads_sums, qr, kr, vr, left, down, row, received,
    row_cross, arrived, out_dz, *refs,
):
    *blocks, terms_ref = refs
    tokens, width = out_dz.shape
    row_sums = gathered_sums(received, tokens)

    def put(group, rows):
        rows = rows.astype(BF16)
        lane_blocks = width // LANES
        for i in range(lane_blocks):
            terms_ref[group * lane_blocks + i] = rows[:, i * LANES : (i + 1) * LANES]

    columns = heads_weight.shape[1] // 3
    coefficient = -heads_sums[0:1, :] / heads_stats[0:1, :]
    throughs, norms = [], []
    for i, right in enumerate((qr, kr, vr)):
        at = slice(i * columns, (i + 1) * columns)
        dz = jnp.concatenate([grads[s, :, at] for s in range(len(blocks))], axis=0)
        throughs.append(dot_nt(right[...], dz))
        norms.append(right[...] * coefficient[:, at])
    through = jnp.concatenate(throughs, axis=0).astype(BF16)
    total = 0.0
    for s in range(0, len(blocks), 2):
        pair = jnp.concatenate([blocks[s][...], blocks[s + 1][...]], axis=0)
        total += jnp.dot(
            through[:, s * tokens : (s + 2) * tokens], pair, preferred_element_type=F32
        )
    for i in range(3):
        at = slice(i * columns, (i + 1) * columns)
        rows = total[i * RANK : (i + 1) * RANK]
        put(i, FACTOR * (rows + dot_nt(norms[i], heads_weight[:, at])))
    put(3, left[0:RANK, :])
    put(4, left[RANK : 2 * RANK, :])
    out_coefficient, down_coefficient = (
        -row_sums[i : i + 1, :] / row[i : i + 1, :] for i in range(2)
    )
    low = 0.0
    for t in range(arrived.shape[0]):
        low += dot_nt(arrived[t, tokens : tokens + RANK, :], arrived[t, 0:tokens, :])
    put(5, FACTOR * (dot(low, out_dz[...]) + row_cross[0] * out_coefficient))
    put(6, FACTOR * (down[...] + row_cross[1] * down_coefficient))
    put(7, jnp.zeros((RANK, width), F32))


def shared_grads(arrays, blocks):
    width = blocks[0].shape[1]
    return pl.pallas_call(
        shared_grads_kernel,
        out_shape=shape((8 * width // LANES, RANK, LANES), BF16),
        in_specs=[VMEM] * (len(arrays) + len(blocks)),
        out_specs=VMEM,
        compiler_params=PARAMS,
        cost_estimate=cost(8),
        name="shared_grads",
    )(*arrays, *blocks)


def on_device(
    hidden_in,
    segment_ids,
    attention_gain,
    mlp_gain,
    query_base,
    query_left,
    query_right,
    query_magnitude,
    key_base,
    key_left,
    key_right,
    key_magnitude,
    value_base,
    value_left,
    value_right,
    value_magnitude,
    output_base,
    output_left,
    output_right,
    output_magnitude,
    gate_base,
    gate_left,
    gate_right,
    gate_magnitude,
    up_base,
    up_left,
    up_right,
    up_magnitude,
    down_base,
    down_left,
    down_right,
    down_magnitude,
    cotangent,
):
    resid = hidden_in[0]
    cot = cotangent[0]
    rows, width = resid.shape
    segments = segment_ids[0]
    length = segments.shape[0]
    heads_width = query_base.shape[1]
    hidden = gate_base.shape[1]
    mlp_row = mlp_gain[None]
    zero_count = jnp.sum((segments == 0).astype(jnp.int32))
    one_count = jnp.sum((segments <= 1).astype(jnp.int32))
    place = jnp.stack(
        [lax.axis_index(a).astype(jnp.int32) for a in ("z", "xl", "y", "core")]
        + [zero_count, one_count]
    )

    _, _, normed_one = rms_forward(resid.astype(F32), attention_gain)
    other, below, above = x_swap(normed_one), z_up(normed_one), z_down(normed_one)

    piece = output_piece(after(place, normed_one), output_base, output_left.T, output_right)
    received = all_to_all(piece, TENSOR)

    hidden_bases = (gate_base.T, up_base.T, down_base)
    hidden_lefts = (gate_left.T, up_left.T, down_left.T)
    hidden_rights = (gate_right, up_right, down_right)
    heads_magnitude = jnp.concatenate([query_magnitude, key_magnitude, value_magnitude])[None]
    hidden_send, *hidden_sent = prepare_send(
        after(place, piece), hidden_bases, hidden_lefts, hidden_rights
    )
    other, below, above, hidden_send = lax.optimization_barrier((other, below, above, hidden_send))

    other_below, other_above, far_one = z_up(other), z_down(other), z_up(below)
    pulled = from_x_neighbour(hidden_send)
    heads_weight, heads_stats, heads_cross = prepare_heads(
        (query_base, key_base, value_base),
        (query_left.T, key_left.T, value_left.T),
        (query_right, key_right, value_right),
        after(heads_magnitude, received, other),
    )
    out_mine = of_everyone(received.reshape(width, piece.shape[2]), "y")
    starts = jnp.where(segments == 0, 0, jnp.where(segments == 1, zero_count, one_count))
    positions = (jnp.arange(length, dtype=jnp.int32) - after(starts, other)).astype(F32)
    frequency = 10000.0 ** (-jnp.arange(0, HEAD_DIM, 2, dtype=F32) / HEAD_DIM)
    angles = positions[:, None] * frequency[None, :]
    cosine, sine = jnp.cos(angles), jnp.sin(angles)
    cosine = jnp.concatenate([cosine, cosine], axis=-1)
    sine = jnp.concatenate([-sine, sine], axis=-1)

    other_below, other_above, far_one, second_place, _ = lax.optimization_barrier(
        (other_below, other_above, far_one, place, heads_stats)
    )
    other_far = z_down(other_above)
    hidden_magnitude = jnp.stack([gate_magnitude, up_magnitude])
    hidden_keep, out_weight, extra, row_cross, row_terms, near = prepare_second(
        second_place,
        hidden_bases,
        hidden_lefts,
        hidden_rights,
        (output_base, output_left.T, output_right),
        hidden_magnitude,
        hidden_sent,
        (normed_one, other, below, above, heads_weight, heads_stats, cosine, sine),
    )
    other_far, far_place, cot_held, extra = lax.optimization_barrier(
        (other_far, place, cot, extra)
    )
    extra_other = x_swap(extra)
    cot_near = (z_up(cot_held), z_down(cot_held))
    row_blocks = [
        normed_one, other, below, above, other_below, other_above, far_one, other_far
    ]
    far = project_heads(4, far_place, row_blocks[4:], heads_weight, heads_stats, cosine, sine)
    *cot_near, extra_other, attend_place, _ = lax.optimization_barrier(
        (*cot_near, extra_other, place, far)
    )
    half_rows = rows // 2
    cot_all = (
        cot,
        *cot_near,
        z_up(cot_near[0][:half_rows]),
        z_down(cot_near[1][half_rows:]),
    )
    attended, logs = attend(attend_place, near, far, row_terms)
    attended, *cot_ends = lax.optimization_barrier((attended, *cot_all[3:]))
    cot_all = (*cot_all[:3], *cot_ends)
    row_magnitude = jnp.stack([output_magnitude, down_magnitude])
    out_mine = after(out_mine, attended)
    out_columns = (out_mine, core_swap(out_mine))
    arrived = all_to_all(attended, TENSOR)
    swapped = core_swap(after(pulled, attended))

    out_raw, resid_two, normed_two, row = output_forward(
        place, arrived, resid, row_magnitude, mlp_row, out_columns
    )
    hidden_weights = (hidden_send, hidden_keep, pulled, swapped)
    grad_activated, down_dz = hidden_start(place, cot_all, row[3:4], hidden_weights)
    heads_lefts = jnp.concatenate([query_left.T, key_left.T, value_left.T], axis=0)
    heads_lows = low_terms(after(heads_lefts, grad_activated), row_blocks)
    tokens = gather_z(normed_two, lambda: grad_activated)
    tokens = (*tokens[:3], *lax.optimization_barrier((*tokens[3:], heads_lows))[:2])
    *forward, act, gate_back, up_back, hidden_sums = hidden_middle(
        place, tokens, grad_activated, extra, extra_other, hidden_weights
    )
    far_parts = hidden_back(
        True, after(place, forward[0]), gate_back, up_back, hidden_weights, rows
    )
    forward = scatter_z(*forward, lambda: far_parts[0])
    near_parts = hidden_back(
        False, after(place, far_parts[0], forward[3]), gate_back, up_back, hidden_weights, rows
    )
    back = scatter_z(*near_parts, *far_parts, lambda: (near_parts[0], forward[1], forward[2]))
    gate_up_lefts = jnp.concatenate([gate_left.T, up_left.T], axis=0)
    hidden_terms = hidden_grads(
        tokens,
        after(down_dz, back[3]),
        act,
        gate_back,
        up_back,
        hidden_sums,
        extra,
        extra_other,
        gate_up_lefts,
        down_right,
    )
    gate_up_left, down_right_part, mine, sent = hidden_terms
    given = x_swap(sent)
    grad_two, out_dz, head_part, layer = output_back(
        after(place, given),
        back[:3],
        forward[:3],
        cot,
        out_raw,
        resid_two,
        row,
        mlp_row,
        output_right,
        out_columns,
        8,
    )
    gate_up_left, hidden_split = hidden_norms(
        after(place, head_part),
        gate_up_left,
        mine,
        given,
        extra,
        gate_up_lefts,
        hidden_send,
        hidden_keep,
    )
    received = after(all_to_all(head_part, TENSOR), gate_up_left)

    heads_dz, heads_sums = attend_back(
        place, near, far, logs, received, cosine, sine, heads_stats
    )
    *parts, split = tail(
        (
            place,
            hidden_send,
            hidden_keep,
            heads_dz,
            heads_lows,
            heads_stats,
            heads_sums,
            heads_cross,
            mine,
            given,
            row,
            received,
            output_right,
            down_right,
            out_weight,
            attended,
            hidden_split,
        ),
        heads_weight,
    )
    terms = shared_grads(
        (
            after(heads_dz, parts[0]),
            heads_weight,
            heads_stats,
            heads_sums,
            query_right,
            key_right,
            value_right,
            gate_up_left,
            down_right_part,
            row,
            received,
            row_cross,
            arrived,
            out_dz,
        ),
        row_blocks,
    )
    hop, other_hop = z_up(parts[6]), z_down(parts[7])
    other_from_below = z_up(parts[5])
    from_above = z_down(parts[2])
    hop, other_hop, other_from_below, from_above, _ = lax.optimization_barrier(
        (hop, other_hop, other_from_below, from_above, terms)
    )
    other_part = add(parts[4], other_hop).astype(BF16)
    other_from_above = z_down(other_part)
    from_below = z_up(add(parts[3], hop).astype(BF16))
    split = add(split, core_swap(split)).astype(BF16)
    split = add(split, lax.ppermute(split, "xh", SWAP)).astype(BF16)
    split = add(split, lax.ppermute(split, "y", ((0, 1), (1, 0), (2, 3), (3, 2)))).astype(BF16)
    total = after(all_to_all(terms, ALL), other_part, split).astype(F32).sum(axis=0).astype(BF16)
    split_other = lax.ppermute(split, "y", ((0, 2), (2, 0), (1, 3), (3, 1)))
    other_from_above, split_other = lax.optimization_barrier((other_from_above, split_other))
    split = add(split, split_other)
    across = add(parts[1], other_from_below, other_from_above).astype(BF16)
    grad_normed_one = add(parts[0], from_below, from_above, x_swap(across))
    resid = resid.astype(F32)
    inverse = lax.rsqrt(jnp.mean(resid * resid, axis=-1, keepdims=True) + EPSILON)
    input_grad = grad_two + rms_backward(grad_normed_one, resid * inverse, inverse, attention_gain)
    hidden_split, split = split[: 3 * RANK, :hidden], split[3 * RANK :]
    total = after(of_everyone(total, ALL), other_from_above).reshape(8, width // LANES, RANK, LANES)
    total = total.transpose(0, 2, 1, 3).reshape(8, RANK, width).astype(F32)
    hidden_magnitude_grad = hidden_split[2 * RANK : 2 * RANK + 2] / hidden_magnitude
    heads, rest = split[:, :SPLIT_LANES], split[:, SPLIT_LANES : 2 * SPLIT_LANES]
    parts = (hidden + SPLIT_LANES - 1) // SPLIT_LANES
    down_left_grad = jnp.concatenate([rest[i * RANK : (i + 1) * RANK] for i in range(parts)], axis=1)
    at = parts * RANK
    row_magnitude_grad = rest[at : at + 2 * width // SPLIT_LANES].reshape(2, width) / row_magnitude
    at += 2 * width // SPLIT_LANES
    heads_magnitude_grad = rest[at : at + 3] / heads_magnitude.reshape(3, -1)
    return (
        layer[None],
        input_grad[None],
        total[0].T,
        heads[:RANK],
        heads_magnitude_grad[0],
        total[1].T,
        heads[RANK : 2 * RANK],
        heads_magnitude_grad[1],
        total[2].T,
        heads[2 * RANK : 3 * RANK],
        heads_magnitude_grad[2],
        heads[3 * RANK : 4 * RANK].T,
        total[5],
        row_magnitude_grad[0],
        total[3].T,
        hidden_split[:RANK],
        hidden_magnitude_grad[0],
        total[4].T,
        hidden_split[RANK : 2 * RANK],
        hidden_magnitude_grad[1],
        down_left_grad[:, :hidden].T,
        total[6],
        row_magnitude_grad[1],
    )


def solution(mesh):
    torus = Mesh(mesh.devices.reshape(4, 2, 2, 4, 2), ("y", "xh", "core", "z", "xl"))
    column = (P(None, TENSOR), P(), P(None, TENSOR), P(TENSOR))
    row = (P(TENSOR, None), P(TENSOR, None), P(), P())
    column_out, row_out = column[1:], row[1:]
    tokens = P(DP, TENSOR, None)
    return jax.shard_map(
        on_device,
        mesh=torus,
        in_specs=(
            tokens,
            P(DP, None),
            P(),
            P(),
            *column,
            *column,
            *column,
            *row,
            *column,
            *column,
            *row,
            tokens,
        ),
        out_specs=(
            tokens,
            tokens,
            *column_out,
            *column_out,
            *column_out,
            *row_out,
            *column_out,
            *column_out,
            *row_out,
        ),
        check_vma=False,
    )
```

```python
import functools

import jax
import jax.numpy as jnp
from jax import lax
from jax.experimental import pallas as pl
from jax.experimental.pallas import tpu as pltpu
from jax.sharding import Mesh
from jax.sharding import PartitionSpec as P

HEAD_DIM = 128
RANK = 16
ALPHA = 32
FACTOR = ALPHA / RANK
EPSILON = 1e-05
MASKED_SCORE = -1e30
DP = ("y", "xh", "core")
TENSOR = ("z", "xl")
ALL = DP + TENSOR
BF16 = jnp.bfloat16
F32 = jnp.float32

SWAP = ((0, 1), (1, 0))
UP = tuple((i, (i + 1) % 4) for i in range(4))
DOWN = tuple((i, (i + 3) % 4) for i in range(4))
SLOTS = ((0, 0), (0, 1), (-1, 0), (1, 0), (-1, 1), (1, 1), (2, 0), (2, 1))
SLOT_AT = ((0, 1), (3, 5), (6, 7), (2, 4))


def z_up(array):
    return lax.ppermute(array, "z", UP)


def z_down(array):
    return lax.ppermute(array, "z", DOWN)


def y_up(array):
    return lax.ppermute(array, "y", UP)


def y_down(array):
    return lax.ppermute(array, "y", DOWN)


def x_swap(array):
    return lax.ppermute(array, "xl", SWAP)


def core_swap(array):
    return lax.ppermute(array, "core", SWAP)


def from_x_neighbour(array):
    pairs = []
    for x in range(4):
        for core in range(2):
            source = (x ^ 1) if core else (x + 3 if x % 2 == 0 else x + 1) % 4
            pairs.append(
                ((source // 2) * 4 + core * 2 + source % 2, (x // 2) * 4 + core * 2 + x % 2)
            )
    return lax.ppermute(array, ("xh", "core", "xl"), tuple(pairs))


def add(*terms):
    total = terms[0].astype(F32)
    for term in terms[1:]:
        total = total + term.astype(F32)
    return total


def gather_z(own, meanwhile):
    half = own.shape[0] // 2
    below, above, _ = lax.optimization_barrier((z_up(own), z_down(own), meanwhile()))
    return own, below, above, z_up(below[:half]), z_down(above[half:])


def halves_kernel(above, below, low, high, above_ref, below_ref):
    half = low.shape[0]
    above_ref[0:half, :] = (above[0:half, :].astype(F32) + low[...].astype(F32)).astype(BF16)
    above_ref[half:, :] = above[half:, :]
    below_ref[0:half, :] = below[0:half, :]
    below_ref[half:, :] = (below[half:, :].astype(F32) + high[...].astype(F32)).astype(BF16)


def add_halves(above, below, low, high):
    vmem = pl.BlockSpec(memory_space=pltpu.VMEM)
    return pl.pallas_call(
        halves_kernel,
        out_shape=(jax.ShapeDtypeStruct(above.shape, BF16),) * 2,
        in_specs=[vmem] * 4,
        out_specs=(vmem,) * 2,
        name="add_halves",
    )(above, below, low, high)


def scatter_z(own, below, above, far_low, far_high, meanwhile):
    low = z_up(far_low)
    high = z_down(far_high)
    low, high = lax.optimization_barrier((low, high, meanwhile()))[:2]
    above_sum, below_sum = add_halves(above, below, low, high)
    return own, z_up(above_sum), z_down(below_sum), above_sum


def all_to_all(array, axes):
    return lax.all_to_all(array, axes, 0, 0, tiled=True)


def of_everyone(array, axes):
    count = lax.axis_size(axes)
    return all_to_all(jnp.broadcast_to(array[None], (count, *array.shape)), axes)


def dot(left, right):
    return jnp.dot(left.astype(BF16), right.astype(BF16), preferred_element_type=F32)


def dot_nt(left, right):
    return lax.dot_general(
        left.astype(BF16), right.astype(BF16), (((1,), (1,)), ((), ())), preferred_element_type=F32
    )


def dot_tn(left, right):
    return lax.dot_general(
        left.astype(BF16), right.astype(BF16), (((0,), (0,)), ((), ())), preferred_element_type=F32
    )


def after_all(*arrays):
    return lax.optimization_barrier(arrays)[:-1]


def rms_forward(resid, gain):
    inverse = lax.rsqrt(jnp.mean(resid * resid, axis=-1, keepdims=True) + EPSILON)
    normal = resid * inverse
    return normal, inverse, (normal * gain.astype(F32)).astype(BF16)


def rms_backward(grad_normed, normal, inverse, gain):
    scaled = grad_normed * gain.astype(F32)
    return inverse * (scaled - normal * jnp.mean(scaled * normal, axis=-1, keepdims=True))


VMEM = pl.BlockSpec(memory_space=pltpu.VMEM)
SMEM = pl.BlockSpec(memory_space=pltpu.SMEM)
ANY = pl.BlockSpec(memory_space=pl.ANY)
QUERY_ROWS = 256
SCORE_SCALE = HEAD_DIM ** (-0.5)
MIB = 1024 * 1024
LANES = 128
COST = 1.0
SQUARES, SCALE = RANK, RANK + 1
EXTRA_ROWS = 24


def shape(dims, dtype=F32):
    return jax.ShapeDtypeStruct(dims, dtype)


PARAMS = pltpu.CompilerParams(vmem_limit_bytes=60 * MIB)


def cost(micros):
    return pl.CostEstimate(
        flops=0, bytes_accessed=int(micros * COST * 3.69e6), transcendentals=0
    )


def after(array, *earlier):
    return lax.optimization_barrier((array, *earlier))[0]


def whole_spec(dims):
    return pl.BlockSpec(dims, lambda *_: (0,) * len(dims))


def prepare_heads_kernel(q, k, v, al, bl, cl, ar, br, cr, mag, weight_ref, stats_ref, cross_ref):
    step = pl.program_id(0)
    columns = q.shape[1]

    @pl.when(step == 0)
    def _():
        stats_ref[...] = jnp.zeros_like(stats_ref)
        cross_ref[...] = jnp.zeros_like(cross_ref)

    for i, (base, left, right) in enumerate(((q, al, ar), (k, bl, br), (v, cl, cr))):
        at_columns = slice(i * columns, (i + 1) * columns)
        factor = left[...].astype(BF16)
        weight = base[...].astype(F32) + dot_tn(FACTOR * factor, right[...])
        low = weight.astype(BF16)
        weight_ref[:, at_columns] = low
        stats_ref[0:1, at_columns] += jnp.sum(weight * weight, axis=0, keepdims=True)
        cross_ref[:, at_columns] += dot(factor, low)

    @pl.when(step == pl.num_programs(0) - 1)
    def _():
        stats_ref[1:2, :] = mag[...] * lax.rsqrt(stats_ref[0:1, :])


def output_piece_kernel(place, base, left, right, piece_ref):
    weight = (base[...].astype(F32) + FACTOR * dot_tn(left[...], right[...])).astype(BF16)
    for t in range(piece_ref.shape[0]):
        piece_ref[t] = weight


def output_piece(place, base, left, right):
    rows, width = base.shape
    columns = width // 8

    def column(i, place):
        return 0, 2 * place[2] + place[3]

    return pl.pallas_call(
        output_piece_kernel,
        grid_spec=pltpu.PrefetchScalarGridSpec(
            num_scalar_prefetch=1,
            grid=(1,),
            in_specs=[
                pl.BlockSpec((rows, columns), column),
                pl.BlockSpec((RANK, rows), lambda i, place: (0, 0)),
                pl.BlockSpec((RANK, columns), column),
            ],
            out_specs=pl.BlockSpec((8, rows, columns), lambda i, place: (0, 0, 0)),
        ),
        out_shape=shape((8, rows, columns), BF16),
        compiler_params=PARAMS,
        cost_estimate=cost(2.5),
        name="output_piece",
    )(place, base, left, right)


def halves(which):
    def index(place):
        return place[3] if which == 0 else 1 - place[3]

    return index


def adapted_rows(step, bases, factors, squares, sums, cross):
    rows, width = bases[0].shape
    lows = []
    for i, (base, (left, right)) in enumerate(zip(bases, factors)):
        weight = base[...].astype(F32) + dot(left, FACTOR * right)
        low = weight.astype(BF16)
        lows.append(low)
        if i < 2:
            square = weight * weight
            at = pl.ds(pl.multiple_of(step * rows, rows), rows)
            squares[i, at, :] = sum(square[:, j : j + LANES] for j in range(0, width, LANES))
        else:
            sums[...] += jnp.sum(weight * weight, axis=0, keepdims=True)
            cross[...] += dot_tn(left, low)
    return lows


def down_sublanes(factor):
    unit = (
        lax.broadcasted_iota(jnp.int32, (RANK, LANES), 0)
        == lax.broadcasted_iota(jnp.int32, (RANK, LANES), 1)
    ).astype(BF16)
    return dot_tn(factor, unit)


def prepare_send_kernel(
    place, g, u, d, gl, ul, dl, gr, ur, dr, send_ref, squares_ref, sums_ref, cross_ref, columns
):
    step = pl.program_id(0)
    rows = g.shape[0]

    @pl.when(step == 0)
    def _():
        for i, factor in enumerate((gr, ur, dl)):
            columns[i] = down_sublanes(factor[...])
        cross_ref[...] = jnp.zeros_like(cross_ref)
        sums_ref[...] = jnp.zeros_like(sums_ref)

    at = pl.ds(pl.multiple_of((pl.num_programs(0) * place[3] + step) * rows, rows), rows)
    factors = [(columns[i, at, 0:RANK], right[...]) for i, right in enumerate((gl, ul, dr))]
    lows = adapted_rows(step, (g, u, d), factors, squares_ref, sums_ref, cross_ref)
    for i, low in enumerate(lows):
        send_ref[i] = low


def prepare_keep_kernel(
    place, g, u, d, gl, ul, dl, gr, ur, dr, o, ol, orr, mag, squares_in, sums_in, cross_in,
    keep_ref, out_ref, extra_ref, cross_ref, terms_ref, squares, squares_all, columns, sums,
):
    step = pl.program_id(0)
    steps = pl.num_programs(0)
    rows = g.shape[0]
    out_rows, width = o.shape

    @pl.when(step == 0)
    def _():
        for i, factor in enumerate((gr, ur, dl)):
            columns[i] = down_sublanes(factor[...])
        columns[3, 0 : ol.shape[1], :] = down_sublanes(ol[...])
        cross_ref[0] = jnp.zeros_like(cross_in)
        cross_ref[1] = cross_in[...]
        sums[0:1, :] = jnp.zeros_like(sums_in)
        sums[1:2, :] = sums_in[...]

    at = pl.ds(pl.multiple_of((steps * (1 - place[3]) + step) * rows, rows), rows)
    factors = [(columns[i, at, 0:RANK], right[...]) for i, right in enumerate((gl, ul, dr))]
    lows = adapted_rows(step, (g, u, d), factors, squares, sums.at[1:2], cross_ref.at[1])
    for i, low in enumerate(lows):
        keep_ref[i] = low
    left = columns[3, pl.ds(pl.multiple_of(step * out_rows, out_rows), out_rows), 0:RANK]
    weight = o[...].astype(F32) + dot(left, FACTOR * orr[...])
    low = weight.astype(BF16)
    out_ref[...] = low
    cross_ref[0] += dot_tn(left, low)
    sums[0:1, :] += jnp.sum(weight * weight, axis=0, keepdims=True)

    @pl.when(step == steps - 1)
    def _():
        half = squares.shape[1]
        for core, part in ((place[3], squares_in), (1 - place[3], squares)):
            squares_all[:, pl.ds(pl.multiple_of(core * half, half), half), :] = part[...]
        extra_ref[...] = jnp.zeros_like(extra_ref)
        for i, right in enumerate((gr, ur)):
            extra_ref[i, 0:RANK, :] = right[...]
            total = lax.dot_general(
                jnp.ones((8, LANES), F32),
                squares_all[i],
                (((1,), (1,)), ((), ())),
                precision=lax.Precision.HIGHEST,
                preferred_element_type=F32,
            )
            extra_ref[i, SQUARES : SQUARES + 1, :] = total[0:1]
            extra_ref[i, SCALE : SCALE + 1, :] = mag[i : i + 1, :] * lax.rsqrt(total[0:1])
        extra_ref[2, 0:RANK, :] = dl[...]
        lanes = terms_ref.shape[2]
        total = jnp.concatenate(
            [sums[i : i + 1, j : j + lanes] for i in range(2) for j in range(0, width, lanes)], axis=0
        )
        high = total.astype(BF16)
        rest = (total - high.astype(F32)).astype(BF16)
        for t in range(terms_ref.shape[0]):
            terms_ref[t, 0:RANK, :] = ol[...].astype(BF16)
            terms_ref[t, RANK : RANK + 16, :] = high
            terms_ref[t, RANK + 16 :, :] = rest


HALF_STEPS = 2


def half_specs(which, hidden, width):
    rows = hidden // 2 // HALF_STEPS
    half = halves(which)

    def whole(*dims):
        return pl.BlockSpec(dims, lambda i, place: (0,) * len(dims))

    base = pl.BlockSpec((rows, width), lambda i, place: (HALF_STEPS * half(place) + i, 0))
    specs = [base] * 3 + [whole(RANK, width)] * 2 + [whole(RANK, hidden)] * 3 + [whole(RANK, width)]
    return specs, whole, pl.BlockSpec((3, rows, width), lambda i, place: (0, i, 0))


def prepare_send(place, bases, lefts, rights):
    hidden, width = bases[0].shape
    specs, whole, block = half_specs(0, hidden, width)
    return pl.pallas_call(
        prepare_send_kernel,
        grid_spec=pltpu.PrefetchScalarGridSpec(
            num_scalar_prefetch=1,
            grid=(HALF_STEPS,),
            in_specs=specs,
            out_specs=(block, whole(2, hidden // 2, LANES), whole(1, width), whole(RANK, width)),
            scratch_shapes=[pltpu.VMEM((3, hidden, LANES), F32)],
        ),
        out_shape=(
            shape((3, hidden // 2, width), BF16),
            shape((2, hidden // 2, LANES)),
            shape((1, width)),
            shape((RANK, width)),
        ),
        compiler_params=PARAMS,
        cost_estimate=cost(6),
        name="prepare_send",
    )(place, *bases, *lefts, *rights)


def prepare_heads(bases, lefts, rights, magnitude):
    width, columns = bases[0].shape
    rows = width // HALF_STEPS
    return pl.pallas_call(
        prepare_heads_kernel,
        grid=(HALF_STEPS,),
        out_shape=(
            shape((width, 3 * columns), BF16),
            shape((8, 3 * columns)),
            shape((RANK, 3 * columns)),
        ),
        in_specs=[pl.BlockSpec((rows, columns), lambda i: (i, 0))] * 3
        + [pl.BlockSpec((RANK, rows), lambda i: (0, i))] * 3
        + [whole_spec((RANK, columns))] * 3
        + [whole_spec((1, 3 * columns))],
        out_specs=(
            pl.BlockSpec((rows, 3 * columns), lambda i: (i, 0)),
            whole_spec((8, 3 * columns)),
            whole_spec((RANK, 3 * columns)),
        ),
        compiler_params=PARAMS,
        cost_estimate=cost(6),
        name="prepare_heads",
    )(*bases, *lefts, *rights, magnitude)


def prepare_second_kernel(place, *refs):
    inputs, near_inputs, outputs = refs[:16], refs[16:24], refs[24:]
    prepare_keep_kernel(place, *inputs, *outputs[:5], *outputs[6:])

    @pl.when(pl.program_id(0) == 0)
    def _():
        project_heads_kernel(0, place, *near_inputs, outputs[5])


def prepare_second(place, bases, lefts, rights, out, magnitude, sent, near):
    hidden, width = bases[0].shape
    out_rows = out[0].shape[0]
    specs, whole, block = half_specs(1, hidden, width)
    out_block = pl.BlockSpec((out_rows // HALF_STEPS, width), lambda i, place: (i, 0))
    rows, heads_width = near[0].shape[0], near[4].shape[1]
    return pl.pallas_call(
        prepare_second_kernel,
        grid_spec=pltpu.PrefetchScalarGridSpec(
            num_scalar_prefetch=1,
            grid=(HALF_STEPS,),
            in_specs=specs
            + [
                out_block,
                whole(RANK, out_rows),
                whole(RANK, width),
                whole(2, hidden),
                whole(2, hidden // 2, LANES),
                whole(1, width),
                whole(RANK, width),
            ]
            + [whole(*a.shape) for a in near],
            out_specs=(
                block,
                out_block,
                whole(3, EXTRA_ROWS, hidden),
                whole(2, RANK, width),
                whole(8, 3 * RANK, width // 8),
                whole(4, rows, heads_width),
            ),
            scratch_shapes=[
                pltpu.VMEM((2, hidden // 2, LANES), F32),
                pltpu.VMEM((2, hidden, LANES), F32),
                pltpu.VMEM((4, hidden, LANES), F32),
                pltpu.VMEM((8, width), F32),
            ],
        ),
        out_shape=(
            shape((3, hidden // 2, width), BF16),
            shape((out_rows, width), BF16),
            shape((3, EXTRA_ROWS, hidden)),
            shape((2, RANK, width)),
            shape((8, 3 * RANK, width // 8), BF16),
            shape((4, rows, heads_width), BF16),
        ),
        compiler_params=PARAMS,
        cost_estimate=cost(14),
        name="prepare_second",
    )(place, *bases, *lefts, *rights, *out, magnitude, *sent, *near)


def slot_of(place, block):
    away = lax.rem(block // 2 - place[0] + 4, 4)
    other = jnp.where(place[1] == block % 2, 0, 1)
    return jnp.where(
        away == 0, other, jnp.where(away == 1, 3 + 2 * other, jnp.where(away == 2, 6 + other, 2 + 2 * other))
    )


def block_of(place, slot):
    dz, dx = SLOTS[slot]
    return 2 * lax.rem(place[0] + dz + 4, 4) + (place[1] if dx == 0 else 1 - place[1])


def turned(values, cosine, sine):
    return values * cosine + pltpu.roll(values, HEAD_DIM // 2, 1) * sine


def turned_back(grads, cosine, sine):
    return grads * cosine - pltpu.roll(grads, HEAD_DIM // 2, 1) * sine


def project_heads_kernel(first_slot, place, b0, b1, b2, b3, weight, stats, cosine, sine, out_ref):
    blocks = jnp.concatenate([b[...] for b in (b0, b1, b2, b3)], axis=0)
    rows = b0.shape[0]
    width = weight.shape[1]
    values = jnp.dot(blocks, weight[...], preferred_element_type=F32) * stats[1:2, :]
    for s in range(4):
        at = pl.ds(pl.multiple_of(block_of(place, first_slot + s) * rows, rows), rows)
        cos, sin = cosine[at, :], sine[at, :]
        for head in range(width // HEAD_DIM):
            head_at = slice(head * HEAD_DIM, (head + 1) * HEAD_DIM)
            part = values[s * rows : (s + 1) * rows, head_at]
            if head < 2 * width // HEAD_DIM // 3:
                part = turned(part, cos, sin)
            out_ref[s, :, head_at] = part.astype(BF16)


def project_heads(first_slot, place, blocks, weight, stats, cosine, sine):
    rows = blocks[0].shape[0]
    return pl.pallas_call(
        functools.partial(project_heads_kernel, first_slot),
        out_shape=shape((4, rows, weight.shape[1]), BF16),
        in_specs=[SMEM] + [VMEM] * 8,
        out_specs=VMEM,
        compiler_params=PARAMS,
        cost_estimate=cost(5.5),
        name="project_heads",
    )(place, *blocks, weight, stats, cosine, sine)


def low_kernel(ql, kl, vl, *refs):
    *blocks, out_ref = refs
    rows = blocks[0].shape[0]
    lefts = jnp.concatenate([ql[...], kl[...], vl[...]], axis=0)
    for s, block in enumerate(blocks):
        out_ref[:, s * rows : (s + 1) * rows] = dot_nt(lefts, block[...]).astype(BF16)


def low_terms(lefts, blocks):
    rows = blocks[0].shape[0]
    return pl.pallas_call(
        low_kernel,
        out_shape=shape((3 * RANK, rows * len(blocks)), BF16),
        in_specs=[VMEM] * (3 + len(blocks)),
        out_specs=VMEM,
        compiler_params=PARAMS,
        cost_estimate=cost(4.5),
        name="low_terms",
    )(*lefts, *blocks)


def masked_scores(place, query, key, first_row):
    scores = dot_nt(query, key) * SCORE_SCALE
    row = first_row + lax.broadcasted_iota(jnp.int32, (query.shape[0], 1), 0)
    start = jnp.where(row < place[4], 0, jnp.where(row < place[5], place[4], place[5]))
    column = lax.broadcasted_iota(jnp.int32, scores.shape, 1)
    return jnp.where((column <= row) & (column >= start), scores, MASKED_SCORE)


def place_blocks(place, near, far, held):
    rows = near.shape[1]
    for block in range(2 * near.shape[0]):
        slot = slot_of(place, block)
        at = slice(block * rows, (block + 1) * rows)

        @pl.when(slot < 4)
        def _():
            held[at, :] = near[jnp.minimum(slot, 3)]

        @pl.when(slot >= 4)
        def _():
            held[at, :] = far[jnp.maximum(slot - 4, 0)]


def attend_kernel(place, near, far, terms, out_ref, log_ref, held):
    length = held.shape[0]
    width = out_ref.shape[2]
    rows = near.shape[1]
    out_ref[:, rows:, :] = terms[...]
    place_blocks(place, near, far, held)
    for head in range(width // HEAD_DIM):
        at = slice(head * HEAD_DIM, (head + 1) * HEAD_DIM)
        key_at = slice(width + head * HEAD_DIM, width + (head + 1) * HEAD_DIM)
        value_at = slice(2 * width + head * HEAD_DIM, 2 * width + (head + 1) * HEAD_DIM)
        for first in range(0, length, QUERY_ROWS):
            last = first + QUERY_ROWS
            scores = masked_scores(place, held[first:last, at], held[:last, key_at], first)
            largest = jnp.max(scores, axis=-1, keepdims=True)
            weights = jnp.exp(scores - largest)
            totals = jnp.sum(weights, axis=-1, keepdims=True)
            probs = (weights * (1.0 / totals)).astype(BF16)
            out = jnp.dot(probs, held[:last, value_at], preferred_element_type=F32)
            for i in range(QUERY_ROWS // rows):
                out_ref[first // rows + i, 0:rows, at] = out[i * rows : (i + 1) * rows].astype(BF16)
            log_ref[first:last, at] = jnp.broadcast_to(
                largest + jnp.log(totals), (QUERY_ROWS, HEAD_DIM)
            )


def attend(place, near, far, terms):
    blocks, rows, width = near.shape
    length = 2 * blocks * rows
    groups = terms.shape[0]
    return pl.pallas_call(
        attend_kernel,
        out_shape=(
            shape((groups, length // groups + terms.shape[1], width // 3), BF16),
            shape((length, width // 3)),
        ),
        in_specs=[SMEM] + [VMEM] * 3,
        out_specs=(VMEM, VMEM),
        scratch_shapes=[pltpu.VMEM((length, width), BF16)],
        compiler_params=PARAMS,
        cost_estimate=cost(7.5),
        name="attend",
    )(place, near, far, terms)


def attend_back_kernel(
    place, near, far, log_ref, grad_ref, cosine, sine, stats,
    out_ref, sum_ref, held, total,
):
    length = held.shape[0]
    width = grad_ref.shape[2]
    rows = near.shape[1]
    place_blocks(place, near, far, held)
    for head in range(width // HEAD_DIM):
        at = slice(head * HEAD_DIM, (head + 1) * HEAD_DIM)
        key_at = slice(width + head * HEAD_DIM, width + (head + 1) * HEAD_DIM)
        value_at = slice(2 * width + head * HEAD_DIM, 2 * width + (head + 1) * HEAD_DIM)
        for first in reversed(range(0, length, QUERY_ROWS)):
            last = first + QUERY_ROWS
            query = held[first:last, at]
            key = held[:last, key_at]
            scores = masked_scores(place, query, key, first)
            probs = jnp.exp(scores - log_ref[first:last, head * HEAD_DIM : head * HEAD_DIM + 1])
            grad = jnp.concatenate(
                [grad_ref[i, 0:rows, at] for i in range(first // rows, last // rows)], axis=0
            )
            grad_probs = dot_nt(grad, held[:last, value_at])
            inner = jnp.sum(grad_probs * probs, axis=-1, keepdims=True)
            grad_scores = (probs * (grad_probs - inner) * SCORE_SCALE).astype(BF16)
            total[first:last, at] = jnp.dot(grad_scores, key, preferred_element_type=F32)
            grad_key = dot_tn(grad_scores, query)
            grad_value = dot_tn(probs, grad)
            if last == length:
                total[:, key_at] = grad_key
                total[:, value_at] = grad_value
            else:
                total[:last, key_at] += grad_key
                total[:last, value_at] += grad_value
    heads = 3 * width // HEAD_DIM
    for head in range(heads):
        at = slice(head * HEAD_DIM, (head + 1) * HEAD_DIM)
        sums = jnp.zeros((1, HEAD_DIM), F32)
        for block in range(length // rows):
            block_at = slice(block * rows, (block + 1) * rows)
            grads = total[block_at, at]
            values = held[block_at, at].astype(F32)
            if head < 2 * heads // 3:
                cos, sin = cosine[block_at, :], sine[block_at, :]
                grads = turned_back(grads, cos, sin)
                values = turned_back(values, cos, sin)
            sums += jnp.sum(grads * values, axis=0, keepdims=True)
            out_ref[slot_of(place, block), :, at] = (grads * stats[1:2, at]).astype(BF16)
        sum_ref[:, at] = jnp.broadcast_to(sums, (8, HEAD_DIM))


def attend_back(place, near, far, logs, grad, cosine, sine, stats):
    blocks, rows, width = near.shape
    length = 2 * blocks * rows
    return pl.pallas_call(
        attend_back_kernel,
        out_shape=(shape((2 * blocks, rows, width), BF16), shape((8, width))),
        in_specs=[SMEM] + [VMEM] * 7,
        out_specs=(VMEM, VMEM),
        scratch_shapes=[pltpu.VMEM((length, width), BF16), pltpu.VMEM((length, width), F32)],
        compiler_params=PARAMS,
        cost_estimate=cost(10.5),
        name="attend_back",
    )(place, near, far, logs, grad, cosine, sine, stats)


def heads_back_kernel(grads, source, *refs):
    *outs, dz, weight, sems = refs
    rows = grads.shape[1]
    chunks = weight.shape[0]
    columns = weight.shape[1]
    copies = [
        pltpu.make_async_copy(source.at[pl.ds(i * columns, columns)], weight.at[i], sems.at[i])
        for i in range(chunks)
    ]
    start_all([copies])
    for s in range(len(outs)):
        dz[s * rows : (s + 1) * rows, :] = grads[s]
    for i in range(chunks):
        copies[i].wait()
        part = dot_nt(dz[...], weight[i]).astype(BF16)
        for s, out in enumerate(outs):
            out[:, i * columns : (i + 1) * columns] = part[s * rows : (s + 1) * rows]


def weight_copies(mine, others, buffer, sems):
    return [
        pltpu.make_async_copy(source.at[i], buffer.at[2 * i + j], sems.at[2 * i + j])
        for i in range(mine.shape[0])
        for j, source in enumerate((mine, others))
    ]


def start_all(copies):
    for group in copies:
        for copy in group:
            copy.start()


def wait_all(group):
    for copy in group:
        copy.wait()


def column_of(place, i, lanes):
    core = place[3] if i % 2 == 0 else 1 - place[3]
    return pl.ds(pl.multiple_of((2 * (i // 2) + core) * lanes, lanes), lanes)


def output_kernel(
    place, arrived, resid, magnitude, gain, mine, others, raw_ref, resid_ref, normed_ref, row_ref, buffer, sems
):
    copies = weight_copies(mine, others, buffer, sems)
    start_all([copies])
    rows = resid.shape[0]
    groups, lanes = arrived.shape[0], arrived.shape[2]
    tokens = jnp.concatenate([arrived[t, 0:rows, :] for t in range(groups)], axis=1)
    squares = 0.0
    for t in range(groups):
        parts = arrived[t, rows + RANK : rows + 3 * RANK, :].astype(F32)
        squares += parts[0:RANK] + parts[RANK : 2 * RANK]
    squares = jnp.concatenate(
        [
            jnp.concatenate([squares[i * 8 + j : i * 8 + j + 1] for j in range(8)], axis=1)
            for i in range(2)
        ],
        axis=0,
    )
    scales = magnitude[...] * lax.rsqrt(squares)
    row_ref[0:2, :] = squares
    row_ref[2:4, :] = scales
    row_ref[4:8, :] = jnp.zeros((4, squares.shape[1]), F32)
    for i, copy in enumerate(copies):
        copy.wait()
        raw_ref[:, column_of(place, i, lanes)] = jnp.dot(
            tokens, buffer[i], preferred_element_type=F32
        )
    resid_two = resid[...].astype(F32) + raw_ref[...] * scales[0:1]
    resid_ref[...] = resid_two
    _, _, normed_ref[...] = rms_forward(resid_two, gain[...])


def output_forward(place, arrived, resid, magnitude, gain, columns):
    rows, width = resid.shape
    return pl.pallas_call(
        output_kernel,
        out_shape=(
            shape((rows, width)),
            shape((rows, width)),
            shape((rows, width), BF16),
            shape((8, width)),
        ),
        in_specs=[SMEM] + [VMEM] * 4 + [ANY] * len(columns),
        out_specs=(VMEM,) * 4,
        scratch_shapes=[
            pltpu.VMEM((8, *columns[0].shape[1:]), BF16),
            pltpu.SemaphoreType.DMA((8,)),
        ],
        compiler_params=PARAMS,
        cost_estimate=cost(7.5),
        name="output_forward",
    )(place, arrived, resid, magnitude, gain, *columns)


def output_back_kernel(
    place, own, below, above, down_own, down_below, down_above, cot, raw, resid, row, gain, right, mine,
    others, grad_ref, dz_ref, head_ref, layer_ref, buffer, total, sems,
):
    copies = weight_copies(mine, others, buffer, sems)
    start_all([copies])
    scales = row[2:4, :]
    grad_normed = own[...].astype(F32) + below[...].astype(F32) + above[...].astype(F32)
    resid_two = resid[...]
    cotangent = cot[...].astype(F32)
    inverse = lax.rsqrt(jnp.mean(resid_two * resid_two, axis=-1, keepdims=True) + EPSILON)
    grad = cotangent + rms_backward(grad_normed, resid_two * inverse, inverse, gain[...])
    grad_ref[...] = grad
    dz = (grad * scales[0:1]).astype(BF16)
    dz_ref[...] = dz
    down = (
        down_own[...].astype(F32) + down_below[...].astype(F32) + down_above[...].astype(F32)
    ) * scales[1:2]
    layer_ref[...] = (resid_two + down).astype(BF16)
    sums = (
        jnp.sum(grad * raw[...], axis=0, keepdims=True) * scales[0:1],
        jnp.sum(cotangent * down, axis=0, keepdims=True),
    )
    rows, lanes = dz.shape[0], buffer.shape[2]
    through = dot_nt(right[...], dz)
    terms = jnp.concatenate(
        [jnp.concatenate([through, jnp.zeros((RANK, lanes - rows), F32)], axis=1)]
        + [s[:, j * lanes : (j + 1) * lanes] for s in sums for j in range(8)],
        axis=0,
    ).astype(BF16)
    for i, copy in enumerate(copies):
        copy.wait()
        part = dot_nt(dz_ref[:, column_of(place, i, lanes)], buffer[i])
        if i == 0:
            total[...] = part
        else:
            total[...] += part
    for t in range(head_ref.shape[0]):
        head_ref[t, 0:rows, :] = total[:, t * lanes : (t + 1) * lanes].astype(BF16)
        head_ref[t, rows:, :] = terms


def output_back(place, back, forward, cot, raw, resid, row, gain, right, columns, groups):
    rows, width = resid.shape
    return pl.pallas_call(
        output_back_kernel,
        out_shape=(
            shape((rows, width)),
            shape((rows, width), BF16),
            shape((groups, rows + 2 * RANK, width // groups), BF16),
            shape((rows, width), BF16),
        ),
        in_specs=[SMEM] + [VMEM] * 12 + [ANY] * len(columns),
        out_specs=(VMEM,) * 4,
        scratch_shapes=[
            pltpu.VMEM((8, *columns[0].shape[1:]), BF16),
            pltpu.VMEM((rows, width), F32),
            pltpu.SemaphoreType.DMA((8,)),
        ],
        compiler_params=PARAMS,
        cost_estimate=cost(8),
        name="output_back",
    )(place, *back, *forward, cot, raw, resid, row, gain, right, *columns)


def hidden_copies(place, halves_of, planes, buffer, sems):
    half = buffer.shape[2] // 2
    copies = []
    for c in range(2):
        for k, plane in enumerate(planes):
            for j, which in enumerate((place[3], 1 - place[3])):
                rows = pl.ds(pl.multiple_of(which * half, half), half)
                copies.append(
                    pltpu.make_async_copy(
                        halves_of[2 * c + j].at[plane],
                        buffer.at[c, k, rows],
                        sems.at[2 * len(planes) * c + 2 * k + j],
                    )
                )
    return copies


def ends_of(rows):
    return (0, rows, 2 * rows, 3 * rows, 3 * rows + rows // 2, 4 * rows)


def hidden_start_kernel(
    place, cot_own, cot_below, cot_above, cot_low, cot_high, row, send, keep, pulled, swapped,
    grad_ref, dz_ref, buffer, sems,
):
    copies = hidden_copies(place, (send, keep, pulled, swapped), (2,), buffer, sems)
    start_all([copies])
    ends = ends_of(cot_own.shape[0])
    for i, block in enumerate((cot_own, cot_below, cot_above, cot_low, cot_high)):
        dz_ref[ends[i] : ends[i + 1], :] = (block[...].astype(F32) * row[3:4, :]).astype(BF16)
    for c in range(2):
        wait_all(copies[2 * c : 2 * c + 2])
        grad_ref[c] = dot_nt(dz_ref[...], buffer[c, 0]).astype(BF16)


def hidden_start(place, cot, row, weights):
    rows, width = cot[0].shape
    hidden = 2 * weights[0].shape[1]
    return pl.pallas_call(
        hidden_start_kernel,
        out_shape=(shape((2, 4 * rows, hidden), BF16), shape((4 * rows, width), BF16)),
        in_specs=[SMEM] + [VMEM] * 6 + [ANY] * 4,
        out_specs=(VMEM,) * 2,
        scratch_shapes=[pltpu.VMEM((2, 1, hidden, width), BF16), pltpu.SemaphoreType.DMA((4,))],
        compiler_params=PARAMS,
        cost_estimate=cost(7),
        name="hidden_start",
    )(place, *cot, row, *weights)


def hidden_middle_kernel(
    place, own, below, above, far_low, far_high, grads, extra, extra_other, send, keep, pulled, swapped,
    f0, f1, f2, f3, f4, act_ref, gate_ref, up_ref, sum_ref, tokens, buffer, sems,
):
    copies = hidden_copies(place, (send, keep, pulled, swapped), (0, 1, 2), buffer, sems)
    start_all([copies])
    ends = ends_of(own.shape[0])
    for i, block in enumerate((own, below, above, far_low, far_high)):
        tokens[ends[i] : ends[i + 1], :] = block[...]
    sum_ref[...] = jnp.zeros_like(sum_ref)
    for c in range(2):
        factors = (extra, extra_other)[c]
        gate_scale = factors[0, SCALE : SCALE + 1, :]
        up_scale = factors[1, SCALE : SCALE + 1, :]
        wait_all(copies[6 * c : 6 * c + 2])
        gate = dot_nt(tokens[...], buffer[c, 0]) * gate_scale
        wait_all(copies[6 * c + 2 : 6 * c + 4])
        upper = dot_nt(tokens[...], buffer[c, 1]) * up_scale
        grad = grads[c].astype(F32)
        sigmoid = 0.5 + 0.5 * jnp.tanh(0.5 * gate)
        silu = gate * sigmoid
        act_ref[c] = (silu * upper).astype(BF16)
        grad_up = grad * silu
        grad_gate = grad * upper * (sigmoid + silu * (1.0 - sigmoid))
        sum_ref[c, 0:1, :] = jnp.sum(grad_gate * gate, axis=0, keepdims=True)
        sum_ref[c, 1:2, :] = jnp.sum(grad_up * upper, axis=0, keepdims=True)
        gate_ref[c] = (grad_gate * gate_scale).astype(BF16)
        up_ref[c] = (grad_up * up_scale).astype(BF16)
        wait_all(copies[6 * c + 4 : 6 * c + 6])
    columns = 512
    outs = (f0, f1, f2, f3, f4)
    for at in range(0, tokens.shape[1], columns):
        part = dot(act_ref[0], buffer[0, 2, :, at : at + columns])
        part = (part + dot(act_ref[1], buffer[1, 2, :, at : at + columns])).astype(BF16)
        for i, out in enumerate(outs):
            out[:, at : at + columns] = part[ends[i] : ends[i + 1]]


def hidden_middle(place, tokens, grads, extra, extra_other, weights):
    rows, width = tokens[0].shape
    hidden = extra.shape[2]
    total = 4 * rows
    return pl.pallas_call(
        hidden_middle_kernel,
        out_shape=(
            *(shape((n, width), BF16) for n in (rows, rows, rows, rows // 2, rows // 2)),
            *(shape((2, total, hidden), BF16),) * 3,
            shape((2, 8, hidden)),
        ),
        in_specs=[SMEM] + [VMEM] * 8 + [ANY] * 4,
        out_specs=(VMEM,) * 9,
        scratch_shapes=[
            pltpu.VMEM((total, width), BF16),
            pltpu.VMEM((2, 3, hidden, width), BF16),
            pltpu.SemaphoreType.DMA((12,)),
        ],
        compiler_params=PARAMS,
        cost_estimate=cost(20),
        name="hidden_middle",
    )(place, *tokens, grads, extra, extra_other, *weights)


def hidden_back_kernel(first, place, gate, upper, send, keep, pulled, swapped, *refs):
    *outs, total, backs, buffer, sems, back_sems = refs
    copies = hidden_copies(place, (send, keep, pulled, swapped), (0, 1), buffer, sems)
    rows = total.shape[0]
    back_copies = [
        pltpu.make_async_copy(
            source.at[c, pl.ds(first, rows)], backs.at[c, k], back_sems.at[2 * c + k]
        )
        for c in range(2)
        for k, source in enumerate((gate, upper))
    ]
    for i, copy in enumerate(back_copies):
        start_all([[copy], copies[2 * i : 2 * i + 2]])
    columns = 512
    for i, copy in enumerate(back_copies):
        wait_all([copy, *copies[2 * i : 2 * i + 2]])
        c, k = i // 2, i % 2
        for lanes in range(0, total.shape[1], columns):
            lane_at = slice(lanes, lanes + columns)
            part = dot(backs[c, k], buffer[c, k, :, lane_at])
            if i == 0:
                total[:, lane_at] = part
            elif i < 3:
                total[:, lane_at] += part
            else:
                part = (part + total[:, lane_at]).astype(BF16)
                at = 0
                for out in outs:
                    out[:, lane_at] = part[at : at + out.shape[0], :]
                    at += out.shape[0]


def hidden_back(far, place, gate, upper, weights, rows):
    width = weights[0].shape[2]
    hidden = gate.shape[2]
    counts = (rows // 2, rows // 2) if far else (rows, rows, rows)
    return pl.pallas_call(
        functools.partial(hidden_back_kernel, 3 * rows if far else 0),
        out_shape=tuple(shape((n, width), BF16) for n in counts),
        in_specs=[SMEM] + [ANY] * 6,
        out_specs=(VMEM,) * len(counts),
        scratch_shapes=[
            pltpu.VMEM((sum(counts), width), F32),
            pltpu.VMEM((2, 2, sum(counts), hidden), BF16),
            pltpu.VMEM((2, 2, hidden, width), BF16),
            pltpu.SemaphoreType.DMA((8,)),
            pltpu.SemaphoreType.DMA((4,)),
        ],
        compiler_params=PARAMS,
        cost_estimate=cost(8),
        name="hidden_back",
    )(place, gate, upper, *weights)


def hidden_grads_kernel(
    own, below, above, far_low, far_high, dz, act, gate, upper, sums, extra, extra_other, lefts_t,
    lefts_u, down_right, left_ref, down_ref, mine_ref, sent_ref,
):
    tokens = jnp.concatenate([r[...] for r in (own, below, above, far_low, far_high)], axis=0)
    lows = dot_nt(jnp.concatenate([lefts_t[...], lefts_u[...]], axis=0), tokens)
    down_through = dot_nt(down_right[...], dz[...])
    throughs = [0.0, 0.0]
    low_down = 0.0
    for c, (factors, out) in enumerate(((extra, mine_ref), (extra_other, sent_ref))):
        for i, back in enumerate((gate, upper)):
            throughs[i] += dot_nt(factors[i, 0:RANK, :], back[c])
            out[i * RANK : (i + 1) * RANK, :] = dot(lows[i * RANK : (i + 1) * RANK], back[c]).astype(
                out.dtype
            )
        low_down += dot_nt(factors[2, 0:RANK, :], act[c])
        out[2 * RANK : 3 * RANK, :] = dot(down_through, act[c]).astype(out.dtype)
        out[3 * RANK :, :] = jnp.concatenate(
            [sums[c], jnp.zeros_like(sums[c])], axis=0
        ).astype(out.dtype)
    through = jnp.concatenate(throughs, axis=0)
    left_ref[...] = dot(through, tokens)
    down_ref[...] = dot(low_down, dz[...])


def hidden_grads(tokens, dz, act, gate, upper, sums, extra, extra_other, lefts_t, lefts_u, down_right):
    width = dz.shape[1]
    hidden = act.shape[2]
    return pl.pallas_call(
        hidden_grads_kernel,
        out_shape=(
            shape((2 * RANK, width)),
            shape((RANK, width)),
            shape((4 * RANK, hidden)),
            shape((4 * RANK, hidden)),
        ),
        in_specs=[VMEM] * 15,
        out_specs=(VMEM,) * 4,
        compiler_params=PARAMS,
        cost_estimate=cost(8.4),
        name="hidden_grads",
    )(*tokens, dz, act, gate, upper, sums, extra, extra_other, lefts_t, lefts_u, down_right)


def half_copies(place, send, keep, planes, buffer, sems):
    half = buffer.shape[1] // 2
    copies = []
    for j, (source, which) in enumerate(((send, place[3]), (keep, 1 - place[3]))):
        rows = pl.ds(pl.multiple_of(which * half, half), half)
        copies.append(
            pltpu.make_async_copy(source.at[planes], buffer.at[:, rows], sems.at[j])
        )
    return copies


def hidden_norms_kernel(
    place, left, mine, other, extra, extra_other, lefts_t, lefts_u, send, keep, pulled, swapped,
    left_ref, mine_ref, sent_ref, weight, sems,
):
    copies = hidden_copies(place, (send, keep, pulled, swapped), (0, 1), weight, sems)
    start_all([copies])
    totals = [left[0:RANK, :], left[RANK : 2 * RANK, :]]
    for c, (factors, parts, out) in enumerate(((extra, mine, mine_ref), (extra_other, other, sent_ref))):
        rows = []
        for i in range(2):
            sums = parts[3 * RANK + i : 3 * RANK + i + 1, :]
            coefficient = -sums / factors[i, SQUARES : SQUARES + 1, :]
            at = slice(i * RANK, (i + 1) * RANK)
            wait_all(copies[4 * c + 2 * i : 4 * c + 2 * i + 2])
            totals[i] += dot(factors[i, 0:RANK, :] * coefficient, weight[c, i])
            rows.append(
                FACTOR * (parts[at, :] + dot_nt((lefts_t, lefts_u)[i][...], weight[c, i]) * coefficient)
            )
        rows.append(parts[2 * RANK :, :])
        out[...] = jnp.concatenate(rows, axis=0).astype(out.dtype)
    left_ref[...] = FACTOR * jnp.concatenate(totals, axis=0)


def hidden_norms(place, left, mine, other, extra, extra_other, lefts_t, lefts_u, weights):
    width, hidden = left.shape[1], mine.shape[1]
    return pl.pallas_call(
        hidden_norms_kernel,
        out_shape=(shape((2 * RANK, width)), shape(mine.shape), shape(mine.shape, BF16)),
        in_specs=[SMEM] + [VMEM] * 7 + [ANY] * 4,
        out_specs=(VMEM,) * 3,
        scratch_shapes=[
            pltpu.VMEM((2, 2, hidden, width), BF16),
            pltpu.SemaphoreType.DMA((8,)),
        ],
        compiler_params=PARAMS,
        cost_estimate=cost(9),
        name="hidden_norms",
    )(place, left, mine, other, extra, extra_other, lefts_t, lefts_u, *weights)


SPLIT_LANES = 256


def gathered_sums(received, tokens):
    sums = 0.0
    for t in range(received.shape[0]):
        sums += received[t, tokens + RANK : tokens + 2 * RANK, :].astype(F32)
    return jnp.concatenate(
        [
            jnp.concatenate([sums[8 * i + j : 8 * i + j + 1] for j in range(8)], axis=1)
            for i in range(2)
        ],
        axis=0,
    )


def split_grads_kernel(
    place, send, keep, grads, lows, heads_stats, heads_sums, heads_cross, mine, given, row, received,
    out_right, down_right, out_weight, attended, split_ref, down_weight, sems,
):
    copies = half_copies(place, send, keep, slice(2, 3), down_weight, sems)
    start_all([copies])
    width = row.shape[1]
    columns = heads_sums.shape[1] // 3
    slots, tokens = grads.shape[:2]
    row_sums = gathered_sums(received, tokens)
    above = 3 * RANK
    hidden = mine.shape[1]
    parts = mine[...] + given[...].astype(F32)
    split_ref[0:above, 0:hidden] = jnp.concatenate(
        [parts[0 : 2 * RANK], parts[3 * RANK :]], axis=0
    ).astype(BF16)
    split_ref[0:above, hidden:] = jnp.zeros((above, split_ref.shape[1] - hidden), BF16)
    split_ref[above:, 2 * SPLIT_LANES :] = jnp.zeros(
        (split_ref.shape[0] - above, split_ref.shape[1] - 2 * SPLIT_LANES), BF16
    )

    def put(lanes, values):
        split_ref[above:, lanes] = values.astype(BF16)

    coefficient = -heads_sums[0:1, :] / heads_stats[0:1, :]
    first = []
    for i in range(3):
        at = slice(i * columns, (i + 1) * columns)
        dz = jnp.concatenate([grads[s, :, at] for s in range(slots)], axis=0)
        first.append(
            FACTOR
            * (
                jnp.dot(lows[i * RANK : (i + 1) * RANK, :], dz, preferred_element_type=F32)
                + heads_cross[:, at] * coefficient[:, at]
            )
        )
    out_coefficient, down_coefficient = (
        -row_sums[i : i + 1, :] / row[i : i + 1, :] for i in range(2)
    )
    out_left = 0.0
    for t in range(received.shape[0]):
        through = received[t, tokens : tokens + RANK, 0:tokens]
        out_left += dot(through, attended[t, 0:tokens, :])
    first.append(FACTOR * (out_left + dot_nt(out_right[...] * out_coefficient, out_weight[...])))
    first.append(jnp.zeros((RANK, SPLIT_LANES), F32))
    put(slice(0, SPLIT_LANES), jnp.concatenate(first, axis=0))
    at = slice(2 * RANK, 3 * RANK)
    wait_all(copies)
    down_left = FACTOR * (
        parts[at, :] + dot_nt(down_right[...] * down_coefficient, down_weight[0])
    )
    hidden = down_left.shape[1]
    padded = (hidden + SPLIT_LANES - 1) // SPLIT_LANES * SPLIT_LANES
    down_left = jnp.concatenate([down_left, jnp.zeros((RANK, padded - hidden), F32)], axis=1)
    second = [
        down_left[:, j * SPLIT_LANES : (j + 1) * SPLIT_LANES] for j in range(padded // SPLIT_LANES)
    ]
    second += [
        row_sums[i : i + 1, j * SPLIT_LANES : (j + 1) * SPLIT_LANES]
        for i in range(2)
        for j in range(width // SPLIT_LANES)
    ]
    second += [heads_sums[0:1, i * columns : (i + 1) * columns] for i in range(3)]
    used = sum(r.shape[0] for r in second)
    second.append(jnp.zeros((5 * RANK - used, SPLIT_LANES), F32))
    put(slice(SPLIT_LANES, 2 * SPLIT_LANES), jnp.concatenate(second, axis=0))


def tail_kernel(*refs):
    inputs, (weight, *rest) = refs[:16], refs[16:]
    outs, (split_ref, dz, buffer, sems, down_weight, down_sems) = rest[:-6], rest[-6:]
    heads_back_kernel(inputs[3], weight, *outs, dz, buffer, sems)
    split_grads_kernel(*inputs, split_ref, down_weight, down_sems)


def tail(arrays, weight):
    half, width = arrays[1].shape[1:]
    above, lanes = 3 * RANK, (2 * half + LANES - 1) // LANES * LANES
    blocks, rows, columns = arrays[3].shape
    chunks = 4
    return pl.pallas_call(
        tail_kernel,
        out_shape=(
            *(shape((rows, width), BF16),) * blocks,
            shape((above + 5 * RANK, lanes), BF16),
        ),
        in_specs=[SMEM, ANY, ANY] + [VMEM] * (len(arrays) - 3) + [ANY],
        out_specs=(VMEM,) * (blocks + 1),
        scratch_shapes=[
            pltpu.VMEM((blocks * rows, columns), BF16),
            pltpu.VMEM((chunks, width // chunks, columns), BF16),
            pltpu.SemaphoreType.DMA((chunks,)),
            pltpu.VMEM((1, 2 * half, width), BF16),
            pltpu.SemaphoreType.DMA((2,)),
        ],
        compiler_params=PARAMS,
        cost_estimate=cost(13),
        name="tail",
    )(*arrays, weight)


def unpack_kernel(total, *outs):
    lane_blocks = outs[0].shape[1] // LANES
    for group, out in enumerate(outs):
        for i in range(lane_blocks):
            out[:, i * LANES : (i + 1) * LANES] = total[group * lane_blocks + i].astype(F32)


def unpack(total, count, width):
    return pl.pallas_call(
        unpack_kernel,
        out_shape=(shape((RANK, width)),) * count,
        in_specs=[VMEM],
        out_specs=(VMEM,) * count,
        compiler_params=PARAMS,
        cost_estimate=cost(2),
        name="unpack",
    )(total)


def shared_grads_kernel(
    grads, heads_weight, heads_stats, heads_sums, qr, kr, vr, left, down, row, received,
    row_cross, arrived, out_dz, *refs,
):
    *blocks, terms_ref = refs
    tokens, width = out_dz.shape
    row_sums = gathered_sums(received, tokens)

    def put(group, rows):
        rows = rows.astype(BF16)
        lane_blocks = width // LANES
        for i in range(lane_blocks):
            terms_ref[group * lane_blocks + i] = rows[:, i * LANES : (i + 1) * LANES]

    columns = heads_weight.shape[1] // 3
    coefficient = -heads_sums[0:1, :] / heads_stats[0:1, :]
    throughs, norms = [], []
    for i, right in enumerate((qr, kr, vr)):
        at = slice(i * columns, (i + 1) * columns)
        dz = jnp.concatenate([grads[s, :, at] for s in range(len(blocks))], axis=0)
        throughs.append(dot_nt(right[...], dz))
        norms.append(right[...] * coefficient[:, at])
    through = jnp.concatenate(throughs, axis=0).astype(BF16)
    total = 0.0
    for s in range(0, len(blocks), 2):
        pair = jnp.concatenate([blocks[s][...], blocks[s + 1][...]], axis=0)
        total += jnp.dot(
            through[:, s * tokens : (s + 2) * tokens], pair, preferred_element_type=F32
        )
    for i in range(3):
        at = slice(i * columns, (i + 1) * columns)
        rows = total[i * RANK : (i + 1) * RANK]
        put(i, FACTOR * (rows + dot_nt(norms[i], heads_weight[:, at])))
    put(3, left[0:RANK, :])
    put(4, left[RANK : 2 * RANK, :])
    out_coefficient, down_coefficient = (
        -row_sums[i : i + 1, :] / row[i : i + 1, :] for i in range(2)
    )
    low = 0.0
    for t in range(arrived.shape[0]):
        low += dot_nt(arrived[t, tokens : tokens + RANK, :], arrived[t, 0:tokens, :])
    put(5, FACTOR * (dot(low, out_dz[...]) + row_cross[0] * out_coefficient))
    put(6, FACTOR * (down[...] + row_cross[1] * down_coefficient))
    put(7, jnp.zeros((RANK, width), F32))


def shared_grads(arrays, blocks):
    width = blocks[0].shape[1]
    return pl.pallas_call(
        shared_grads_kernel,
        out_shape=shape((8 * width // LANES, RANK, LANES), BF16),
        in_specs=[VMEM] * (len(arrays) + len(blocks)),
        out_specs=VMEM,
        compiler_params=PARAMS,
        cost_estimate=cost(8),
        name="shared_grads",
    )(*arrays, *blocks)


def on_device(
    hidden_in,
    segment_ids,
    attention_gain,
    mlp_gain,
    query_base,
    query_left,
    query_right,
    query_magnitude,
    key_base,
    key_left,
    key_right,
    key_magnitude,
    value_base,
    value_left,
    value_right,
    value_magnitude,
    output_base,
    output_left,
    output_right,
    output_magnitude,
    gate_base,
    gate_left,
    gate_right,
    gate_magnitude,
    up_base,
    up_left,
    up_right,
    up_magnitude,
    down_base,
    down_left,
    down_right,
    down_magnitude,
    cotangent,
):
    resid = hidden_in[0]
    cot = cotangent[0]
    rows, width = resid.shape
    segments = segment_ids[0]
    length = segments.shape[0]
    heads_width = query_base.shape[1]
    hidden = gate_base.shape[1]
    mlp_row = mlp_gain[None]
    zero_count = jnp.sum((segments == 0).astype(jnp.int32))
    one_count = jnp.sum((segments <= 1).astype(jnp.int32))
    place = jnp.stack(
        [lax.axis_index(a).astype(jnp.int32) for a in ("z", "xl", "y", "core")]
        + [zero_count, one_count]
    )

    _, _, normed_one = rms_forward(resid.astype(F32), attention_gain)
    other, below, above = x_swap(normed_one), z_up(normed_one), z_down(normed_one)

    piece = output_piece(after(place, normed_one), output_base, output_left.T, output_right)
    received = all_to_all(piece, TENSOR)

    hidden_bases = (gate_base.T, up_base.T, down_base)
    hidden_lefts = (gate_left.T, up_left.T, down_left.T)
    hidden_rights = (gate_right, up_right, down_right)
    heads_magnitude = jnp.concatenate([query_magnitude, key_magnitude, value_magnitude])[None]
    hidden_send, *hidden_sent = prepare_send(
        after(place, piece), hidden_bases, hidden_lefts, hidden_rights
    )
    other, below, above, hidden_send = lax.optimization_barrier((other, below, above, hidden_send))

    other_below, other_above = z_up(other), z_down(other)
    pulled = from_x_neighbour(hidden_send)
    starts = jnp.where(segments == 0, 0, jnp.where(segments == 1, zero_count, one_count))
    positions = (jnp.arange(length, dtype=jnp.int32) - after(starts, other)).astype(F32)
    frequency = 10000.0 ** (-jnp.arange(0, HEAD_DIM, 2, dtype=F32) / HEAD_DIM)
    angles = positions[:, None] * frequency[None, :]
    cosine, sine = jnp.cos(angles), jnp.sin(angles)
    cosine = jnp.concatenate([cosine, cosine], axis=-1)
    sine = jnp.concatenate([-sine, sine], axis=-1)

    received = after(received, cosine, sine)
    heads_weight, heads_stats, heads_cross = prepare_heads(
        (query_base, key_base, value_base),
        (query_left.T, key_left.T, value_left.T),
        (query_right, key_right, value_right),
        after(heads_magnitude, received, other),
    )
    out_mine = of_everyone(received.reshape(width, piece.shape[2]), "y")
    other_below, other_above, below, second_place, _ = lax.optimization_barrier(
        (other_below, other_above, below, place, heads_stats)
    )
    other_far, far_one = z_down(other_above), z_up(below)
    hidden_magnitude = jnp.stack([gate_magnitude, up_magnitude])
    hidden_keep, out_weight, extra, row_cross, row_terms, near = prepare_second(
        second_place,
        hidden_bases,
        hidden_lefts,
        hidden_rights,
        (output_base, output_left.T, output_right),
        hidden_magnitude,
        hidden_sent,
        (normed_one, other, below, above, heads_weight, heads_stats, cosine, sine),
    )
    other_far, far_one, far_place, cot_held, extra = lax.optimization_barrier(
        (other_far, far_one, place, cot, extra)
    )
    extra_other = x_swap(extra)
    cot_near = (z_up(cot_held), z_down(cot_held))
    row_blocks = [
        normed_one, other, below, above, other_below, other_above, far_one, other_far
    ]
    far = project_heads(4, far_place, row_blocks[4:], heads_weight, heads_stats, cosine, sine)
    *cot_near, extra_other, attend_place, _ = lax.optimization_barrier(
        (*cot_near, extra_other, place, far)
    )
    half_rows = rows // 2
    cot_all = (
        cot,
        *cot_near,
        z_up(cot_near[0][:half_rows]),
        z_down(cot_near[1][half_rows:]),
    )
    attended, logs = attend(attend_place, near, far, row_terms)
    attended, *cot_ends = lax.optimization_barrier((attended, *cot_all[3:]))
    cot_all = (*cot_all[:3], *cot_ends)
    row_magnitude = jnp.stack([output_magnitude, down_magnitude])
    out_mine = after(out_mine, attended)
    out_columns = (out_mine, core_swap(out_mine))
    arrived = all_to_all(attended, TENSOR)
    swapped = core_swap(after(pulled, attended))

    out_raw, resid_two, normed_two, row = output_forward(
        place, arrived, resid, row_magnitude, mlp_row, out_columns
    )
    hidden_weights = (hidden_send, hidden_keep, pulled, swapped)
    grad_activated, down_dz = hidden_start(place, cot_all, row, hidden_weights)
    heads_lows = low_terms(
        (after(query_left.T, grad_activated), key_left.T, value_left.T), row_blocks
    )
    tokens = gather_z(normed_two, lambda: grad_activated)
    tokens = (*tokens[:3], *lax.optimization_barrier((*tokens[3:], heads_lows))[:2])
    *forward, act, gate_back, up_back, hidden_sums = hidden_middle(
        place, tokens, grad_activated, extra, extra_other, hidden_weights
    )
    far_parts = hidden_back(
        True, after(place, forward[0]), gate_back, up_back, hidden_weights, rows
    )
    forward = scatter_z(*forward, lambda: far_parts[0])
    near_parts = hidden_back(
        False, after(place, far_parts[0], forward[3]), gate_back, up_back, hidden_weights, rows
    )
    back = scatter_z(*near_parts, *far_parts, lambda: (near_parts[0], forward[1], forward[2]))
    hidden_terms = hidden_grads(
        tokens,
        after(down_dz, back[3]),
        act,
        gate_back,
        up_back,
        hidden_sums,
        extra,
        extra_other,
        gate_left.T,
        up_left.T,
        down_right,
    )
    gate_up_left, down_right_part, mine, sent = hidden_terms
    grad_two, out_dz, head_part, layer = output_back(
        after(place, mine),
        back[:3],
        forward[:3],
        cot,
        out_raw,
        resid_two,
        row,
        mlp_row,
        output_right,
        out_columns,
        8,
    )
    gate_up_left, mine, sent = hidden_norms(
        after(place, head_part),
        gate_up_left,
        mine,
        sent,
        extra,
        extra_other,
        gate_left.T,
        up_left.T,
        hidden_weights,
    )
    given = x_swap(sent)
    received = after(all_to_all(head_part, TENSOR), gate_up_left)

    heads_dz, heads_sums = attend_back(
        place, near, far, logs, received, cosine, sine, heads_stats
    )
    *parts, split = tail(
        (
            place,
            hidden_send,
            hidden_keep,
            heads_dz,
            heads_lows,
            heads_stats,
            heads_sums,
            heads_cross,
            mine,
            given,
            row,
            received,
            output_right,
            down_right,
            out_weight,
            attended,
        ),
        heads_weight,
    )
    terms = shared_grads(
        (
            after(heads_dz, parts[0]),
            heads_weight,
            heads_stats,
            heads_sums,
            query_right,
            key_right,
            value_right,
            gate_up_left,
            down_right_part,
            row,
            received,
            row_cross,
            arrived,
            out_dz,
        ),
        row_blocks,
    )
    hop, other_hop = z_up(parts[6]), z_down(parts[7])
    other_from_below = z_up(parts[5])
    from_above = z_down(parts[2])
    hop, other_hop, other_from_below, from_above, _ = lax.optimization_barrier(
        (hop, other_hop, other_from_below, from_above, terms)
    )
    other_part = add(parts[4], other_hop).astype(BF16)
    other_from_above = z_down(other_part)
    from_below = z_up(add(parts[3], hop).astype(BF16))
    split = add(split, core_swap(split)).astype(BF16)
    split = add(split, lax.ppermute(split, "xh", SWAP)).astype(BF16)
    split = add(split, lax.ppermute(split, "y", ((0, 1), (1, 0), (2, 3), (3, 2)))).astype(BF16)
    total = after(all_to_all(terms, ALL), other_part, split).astype(F32).sum(axis=0).astype(BF16)
    split_other = lax.ppermute(split, "y", ((0, 2), (2, 0), (1, 3), (3, 1)))
    other_from_above, split_other = lax.optimization_barrier((other_from_above, split_other))
    split = add(split, split_other)
    across = add(parts[1], other_from_below, other_from_above).astype(BF16)
    grad_normed_one = add(parts[0], from_below, from_above, x_swap(across))
    resid = resid.astype(F32)
    inverse = lax.rsqrt(jnp.mean(resid * resid, axis=-1, keepdims=True) + EPSILON)
    input_grad = grad_two + rms_backward(grad_normed_one, resid * inverse, inverse, attention_gain)
    hidden_split, split = split[: 3 * RANK, :hidden], split[3 * RANK :]
    total = unpack(after(of_everyone(total, ALL), other_from_above).reshape(-1, RANK, LANES), 7, width)
    hidden_magnitude_grad = hidden_split[2 * RANK : 2 * RANK + 2] / hidden_magnitude
    heads, rest = split[:, :SPLIT_LANES], split[:, SPLIT_LANES : 2 * SPLIT_LANES]
    parts = (hidden + SPLIT_LANES - 1) // SPLIT_LANES
    down_left_grad = jnp.concatenate([rest[i * RANK : (i + 1) * RANK] for i in range(parts)], axis=1)
    at = parts * RANK
    row_magnitude_grad = rest[at : at + 2 * width // SPLIT_LANES].reshape(2, width) / row_magnitude
    at += 2 * width // SPLIT_LANES
    heads_magnitude_grad = rest[at : at + 3] / heads_magnitude.reshape(3, -1)
    return (
        layer[None],
        input_grad[None],
        total[0].T,
        heads[:RANK],
        heads_magnitude_grad[0],
        total[1].T,
        heads[RANK : 2 * RANK],
        heads_magnitude_grad[1],
        total[2].T,
        heads[2 * RANK : 3 * RANK],
        heads_magnitude_grad[2],
        heads[3 * RANK : 4 * RANK].T,
        total[5],
        row_magnitude_grad[0],
        total[3].T,
        hidden_split[:RANK],
        hidden_magnitude_grad[0],
        total[4].T,
        hidden_split[RANK : 2 * RANK],
        hidden_magnitude_grad[1],
        down_left_grad[:, :hidden].T,
        total[6],
        row_magnitude_grad[1],
    )


def solution(mesh):
    torus = Mesh(mesh.devices.reshape(4, 2, 2, 4, 2), ("y", "xh", "core", "z", "xl"))
    column = (P(None, TENSOR), P(), P(None, TENSOR), P(TENSOR))
    row = (P(TENSOR, None), P(TENSOR, None), P(), P())
    column_out, row_out = column[1:], row[1:]
    tokens = P(DP, TENSOR, None)
    return jax.shard_map(
        on_device,
        mesh=torus,
        in_specs=(
            tokens,
            P(DP, None),
            P(),
            P(),
            *column,
            *column,
            *column,
            *row,
            *column,
            *column,
            *row,
            tokens,
        ),
        out_specs=(
            tokens,
            tokens,
            *column_out,
            *column_out,
            *column_out,
            *row_out,
            *column_out,
            *column_out,
            *row_out,
        ),
        check_vma=False,
    )
```

```python
import functools

import jax
import jax.numpy as jnp
from jax import lax
from jax.experimental import pallas as pl
from jax.experimental.pallas import tpu as pltpu
from jax.sharding import Mesh
from jax.sharding import PartitionSpec as P

HEAD_DIM = 128
RANK = 16
ALPHA = 32
FACTOR = ALPHA / RANK
EPSILON = 1e-05
MASKED_SCORE = -1e30
DP = ("y", "xh", "core")
TENSOR = ("z", "xl")
ALL = DP + TENSOR
BF16 = jnp.bfloat16
F32 = jnp.float32

SWAP = ((0, 1), (1, 0))
UP = tuple((i, (i + 1) % 4) for i in range(4))
DOWN = tuple((i, (i + 3) % 4) for i in range(4))
SLOTS = ((0, 0), (0, 1), (-1, 0), (1, 0), (-1, 1), (1, 1), (2, 0), (2, 1))
SLOT_AT = ((0, 1), (3, 5), (6, 7), (2, 4))


def z_up(array):
    return lax.ppermute(array, "z", UP)


def z_down(array):
    return lax.ppermute(array, "z", DOWN)


def y_up(array):
    return lax.ppermute(array, "y", UP)


def y_down(array):
    return lax.ppermute(array, "y", DOWN)


def x_swap(array):
    return lax.ppermute(array, "xl", SWAP)


def core_swap(array):
    return lax.ppermute(array, "core", SWAP)


def from_x_neighbour(array):
    pairs = []
    for x in range(4):
        for core in range(2):
            source = (x ^ 1) if core else (x + 3 if x % 2 == 0 else x + 1) % 4
            pairs.append(
                ((source // 2) * 4 + core * 2 + source % 2, (x // 2) * 4 + core * 2 + x % 2)
            )
    return lax.ppermute(array, ("xh", "core", "xl"), tuple(pairs))


def add(*terms):
    total = terms[0].astype(F32)
    for term in terms[1:]:
        total = total + term.astype(F32)
    return total


def gather_z(own, meanwhile):
    half = own.shape[0] // 2
    below, above, _ = lax.optimization_barrier((z_up(own), z_down(own), meanwhile()))
    return own, below, above, z_up(below[:half]), z_down(above[half:])


def halves_kernel(above, below, low, high, above_ref, below_ref):
    half = low.shape[0]
    above_ref[0:half, :] = (above[0:half, :].astype(F32) + low[...].astype(F32)).astype(BF16)
    above_ref[half:, :] = above[half:, :]
    below_ref[0:half, :] = below[0:half, :]
    below_ref[half:, :] = (below[half:, :].astype(F32) + high[...].astype(F32)).astype(BF16)


def add_halves(above, below, low, high):
    vmem = pl.BlockSpec(memory_space=pltpu.VMEM)
    return pl.pallas_call(
        halves_kernel,
        out_shape=(jax.ShapeDtypeStruct(above.shape, BF16),) * 2,
        in_specs=[vmem] * 4,
        out_specs=(vmem,) * 2,
        name="add_halves",
    )(above, below, low, high)


def scatter_z(own, below, above, far_low, far_high, meanwhile):
    low = z_up(far_low)
    high = z_down(far_high)
    low, high = lax.optimization_barrier((low, high, meanwhile()))[:2]
    above_sum, below_sum = add_halves(above, below, low, high)
    return own, z_up(above_sum), z_down(below_sum), above_sum


def all_to_all(array, axes):
    return lax.all_to_all(array, axes, 0, 0, tiled=True)


def of_everyone(array, axes):
    count = lax.axis_size(axes)
    return all_to_all(jnp.broadcast_to(array[None], (count, *array.shape)), axes)


def dot(left, right):
    return jnp.dot(left.astype(BF16), right.astype(BF16), preferred_element_type=F32)


def dot_nt(left, right):
    return lax.dot_general(
        left.astype(BF16), right.astype(BF16), (((1,), (1,)), ((), ())), preferred_element_type=F32
    )


def dot_tn(left, right):
    return lax.dot_general(
        left.astype(BF16), right.astype(BF16), (((0,), (0,)), ((), ())), preferred_element_type=F32
    )


def after_all(*arrays):
    return lax.optimization_barrier(arrays)[:-1]


def rms_forward(resid, gain):
    inverse = lax.rsqrt(jnp.mean(resid * resid, axis=-1, keepdims=True) + EPSILON)
    normal = resid * inverse
    return normal, inverse, (normal * gain.astype(F32)).astype(BF16)


def rms_backward(grad_normed, normal, inverse, gain):
    scaled = grad_normed * gain.astype(F32)
    return inverse * (scaled - normal * jnp.mean(scaled * normal, axis=-1, keepdims=True))


VMEM = pl.BlockSpec(memory_space=pltpu.VMEM)
SMEM = pl.BlockSpec(memory_space=pltpu.SMEM)
ANY = pl.BlockSpec(memory_space=pl.ANY)
QUERY_ROWS = 512
SCORE_SCALE = HEAD_DIM ** (-0.5)
EXPONENT_SCALE = SCORE_SCALE * 1.4426950408889634
MIB = 1024 * 1024
LANES = 128
COST = 1.0
SQUARES, SCALE = RANK, RANK + 1
EXTRA_ROWS = 24


def shape(dims, dtype=F32):
    return jax.ShapeDtypeStruct(dims, dtype)


PARAMS = pltpu.CompilerParams(vmem_limit_bytes=60 * MIB)


def cost(micros):
    return pl.CostEstimate(
        flops=0, bytes_accessed=int(micros * COST * 3.69e6), transcendentals=0
    )


def after(array, *earlier):
    return lax.optimization_barrier((array, *earlier))[0]


def whole_spec(dims):
    return pl.BlockSpec(dims, lambda *_: (0,) * len(dims))


def prepare_heads_kernel(q, k, v, al, bl, cl, ar, br, cr, mag, weight_ref, stats_ref, cross_ref):
    step = pl.program_id(0)
    columns = q.shape[1]

    @pl.when(step == 0)
    def _():
        stats_ref[...] = jnp.zeros_like(stats_ref)
        cross_ref[...] = jnp.zeros_like(cross_ref)

    for i, (base, left, right) in enumerate(((q, al, ar), (k, bl, br), (v, cl, cr))):
        at_columns = slice(i * columns, (i + 1) * columns)
        factor = left[...].astype(BF16)
        weight = base[...].astype(F32) + dot_tn(FACTOR * factor, right[...])
        low = weight.astype(BF16)
        weight_ref[:, at_columns] = low
        stats_ref[0:1, at_columns] += jnp.sum(weight * weight, axis=0, keepdims=True)
        cross_ref[:, at_columns] += dot(factor, low)

    @pl.when(step == pl.num_programs(0) - 1)
    def _():
        stats_ref[1:2, :] = mag[...] * lax.rsqrt(stats_ref[0:1, :])


def output_piece_kernel(place, base, left, right, piece_ref):
    weight = (base[...].astype(F32) + FACTOR * dot_tn(left[...], right[...])).astype(BF16)
    for t in range(piece_ref.shape[0]):
        piece_ref[t] = weight


def output_piece(place, base, left, right):
    rows, width = base.shape
    columns = width // 8

    def column(i, place):
        return 0, 2 * place[2] + place[3]

    return pl.pallas_call(
        output_piece_kernel,
        grid_spec=pltpu.PrefetchScalarGridSpec(
            num_scalar_prefetch=1,
            grid=(1,),
            in_specs=[
                pl.BlockSpec((rows, columns), column),
                pl.BlockSpec((RANK, rows), lambda i, place: (0, 0)),
                pl.BlockSpec((RANK, columns), column),
            ],
            out_specs=pl.BlockSpec((8, rows, columns), lambda i, place: (0, 0, 0)),
        ),
        out_shape=shape((8, rows, columns), BF16),
        compiler_params=PARAMS,
        cost_estimate=cost(2.5),
        name="output_piece",
    )(place, base, left, right)


def halves(which):
    def index(place):
        return place[3] if which == 0 else 1 - place[3]

    return index


def adapted_rows(step, bases, factors, squares, sums, cross):
    rows, width = bases[0].shape
    lows = []
    for i, (base, (left, right)) in enumerate(zip(bases, factors)):
        weight = base[...].astype(F32) + dot(left, FACTOR * right)
        low = weight.astype(BF16)
        lows.append(low)
        if i < 2:
            square = weight * weight
            at = pl.ds(pl.multiple_of(step * rows, rows), rows)
            squares[i, at, :] = sum(square[:, j : j + LANES] for j in range(0, width, LANES))
        else:
            sums[...] += jnp.sum(weight * weight, axis=0, keepdims=True)
            cross[...] += dot_tn(left, low)
    return lows


def down_sublanes(factor):
    unit = (
        lax.broadcasted_iota(jnp.int32, (RANK, LANES), 0)
        == lax.broadcasted_iota(jnp.int32, (RANK, LANES), 1)
    ).astype(BF16)
    return dot_tn(factor, unit)


def prepare_send_kernel(
    place, g, u, d, gl, ul, dl, gr, ur, dr, send_ref, squares_ref, sums_ref, cross_ref, columns
):
    step = pl.program_id(0)
    rows = g.shape[0]

    @pl.when(step == 0)
    def _():
        for i, factor in enumerate((gr, ur, dl)):
            columns[i] = down_sublanes(factor[...])
        cross_ref[...] = jnp.zeros_like(cross_ref)
        sums_ref[...] = jnp.zeros_like(sums_ref)

    at = pl.ds(pl.multiple_of((pl.num_programs(0) * place[3] + step) * rows, rows), rows)
    factors = [(columns[i, at, 0:RANK], right[...]) for i, right in enumerate((gl, ul, dr))]
    lows = adapted_rows(step, (g, u, d), factors, squares_ref, sums_ref, cross_ref)
    for i, low in enumerate(lows):
        send_ref[i] = low


def prepare_keep_kernel(
    place, g, u, d, gl, ul, dl, gr, ur, dr, o, ol, orr, mag, squares_in, sums_in, cross_in,
    keep_ref, out_ref, extra_ref, cross_ref, terms_ref, squares, squares_all, columns, sums,
):
    step = pl.program_id(0)
    steps = pl.num_programs(0)
    rows = g.shape[0]
    out_rows, width = o.shape

    @pl.when(step == 0)
    def _():
        for i, factor in enumerate((gr, ur, dl)):
            columns[i] = down_sublanes(factor[...])
        columns[3, 0 : ol.shape[1], :] = down_sublanes(ol[...])
        cross_ref[0] = jnp.zeros_like(cross_in)
        cross_ref[1] = cross_in[...]
        sums[0:1, :] = jnp.zeros_like(sums_in)
        sums[1:2, :] = sums_in[...]

    at = pl.ds(pl.multiple_of((steps * (1 - place[3]) + step) * rows, rows), rows)
    factors = [(columns[i, at, 0:RANK], right[...]) for i, right in enumerate((gl, ul, dr))]
    lows = adapted_rows(step, (g, u, d), factors, squares, sums.at[1:2], cross_ref.at[1])
    for i, low in enumerate(lows):
        keep_ref[i] = low
    left = columns[3, pl.ds(pl.multiple_of(step * out_rows, out_rows), out_rows), 0:RANK]
    weight = o[...].astype(F32) + dot(left, FACTOR * orr[...])
    low = weight.astype(BF16)
    out_ref[...] = low
    cross_ref[0] += dot_tn(left, low)
    sums[0:1, :] += jnp.sum(weight * weight, axis=0, keepdims=True)

    @pl.when(step == steps - 1)
    def _():
        half = squares.shape[1]
        for core, part in ((place[3], squares_in), (1 - place[3], squares)):
            squares_all[:, pl.ds(pl.multiple_of(core * half, half), half), :] = part[...]
        extra_ref[...] = jnp.zeros_like(extra_ref)
        for i, right in enumerate((gr, ur)):
            extra_ref[i, 0:RANK, :] = right[...]
            total = lax.dot_general(
                jnp.ones((8, LANES), F32),
                squares_all[i],
                (((1,), (1,)), ((), ())),
                precision=lax.Precision.HIGHEST,
                preferred_element_type=F32,
            )
            extra_ref[i, SQUARES : SQUARES + 1, :] = total[0:1]
            extra_ref[i, SCALE : SCALE + 1, :] = mag[i : i + 1, :] * lax.rsqrt(total[0:1])
        extra_ref[2, 0:RANK, :] = dl[...]
        lanes = terms_ref.shape[2]
        total = jnp.concatenate(
            [sums[i : i + 1, j : j + lanes] for i in range(2) for j in range(0, width, lanes)], axis=0
        )
        high = total.astype(BF16)
        rest = (total - high.astype(F32)).astype(BF16)
        for t in range(terms_ref.shape[0]):
            terms_ref[t, 0:RANK, :] = ol[...].astype(BF16)
            terms_ref[t, RANK : RANK + 16, :] = high
            terms_ref[t, RANK + 16 :, :] = rest


HALF_STEPS = 2


def half_specs(which, hidden, width):
    rows = hidden // 2 // HALF_STEPS
    half = halves(which)

    def whole(*dims):
        return pl.BlockSpec(dims, lambda i, place: (0,) * len(dims))

    base = pl.BlockSpec((rows, width), lambda i, place: (HALF_STEPS * half(place) + i, 0))
    specs = [base] * 3 + [whole(RANK, width)] * 2 + [whole(RANK, hidden)] * 3 + [whole(RANK, width)]
    return specs, whole, pl.BlockSpec((3, rows, width), lambda i, place: (0, i, 0))


def prepare_send(place, bases, lefts, rights):
    hidden, width = bases[0].shape
    specs, whole, block = half_specs(0, hidden, width)
    return pl.pallas_call(
        prepare_send_kernel,
        grid_spec=pltpu.PrefetchScalarGridSpec(
            num_scalar_prefetch=1,
            grid=(HALF_STEPS,),
            in_specs=specs,
            out_specs=(block, whole(2, hidden // 2, LANES), whole(1, width), whole(RANK, width)),
            scratch_shapes=[pltpu.VMEM((3, hidden, LANES), F32)],
        ),
        out_shape=(
            shape((3, hidden // 2, width), BF16),
            shape((2, hidden // 2, LANES)),
            shape((1, width)),
            shape((RANK, width)),
        ),
        compiler_params=PARAMS,
        cost_estimate=cost(6),
        name="prepare_send",
    )(place, *bases, *lefts, *rights)


def prepare_heads(bases, lefts, rights, magnitude):
    width, columns = bases[0].shape
    rows = width // HALF_STEPS
    return pl.pallas_call(
        prepare_heads_kernel,
        grid=(HALF_STEPS,),
        out_shape=(
            shape((width, 3 * columns), BF16),
            shape((8, 3 * columns)),
            shape((RANK, 3 * columns)),
        ),
        in_specs=[pl.BlockSpec((rows, columns), lambda i: (i, 0))] * 3
        + [pl.BlockSpec((RANK, rows), lambda i: (0, i))] * 3
        + [whole_spec((RANK, columns))] * 3
        + [whole_spec((1, 3 * columns))],
        out_specs=(
            pl.BlockSpec((rows, 3 * columns), lambda i: (i, 0)),
            whole_spec((8, 3 * columns)),
            whole_spec((RANK, 3 * columns)),
        ),
        compiler_params=PARAMS,
        cost_estimate=cost(6),
        name="prepare_heads",
    )(*bases, *lefts, *rights, magnitude)


def prepare_second_kernel(place, *refs):
    inputs, near_inputs, outputs = refs[:16], refs[16:24], refs[24:]
    prepare_keep_kernel(place, *inputs, *outputs[:5], *outputs[6:])

    @pl.when(pl.program_id(0) == 0)
    def _():
        project_heads_kernel(0, place, *near_inputs, outputs[5])


def prepare_second(place, bases, lefts, rights, out, magnitude, sent, near):
    hidden, width = bases[0].shape
    out_rows = out[0].shape[0]
    specs, whole, block = half_specs(1, hidden, width)
    out_block = pl.BlockSpec((out_rows // HALF_STEPS, width), lambda i, place: (i, 0))
    rows, heads_width = near[0].shape[0], near[4].shape[1]
    return pl.pallas_call(
        prepare_second_kernel,
        grid_spec=pltpu.PrefetchScalarGridSpec(
            num_scalar_prefetch=1,
            grid=(HALF_STEPS,),
            in_specs=specs
            + [
                out_block,
                whole(RANK, out_rows),
                whole(RANK, width),
                whole(2, hidden),
                whole(2, hidden // 2, LANES),
                whole(1, width),
                whole(RANK, width),
            ]
            + [whole(*a.shape) for a in near],
            out_specs=(
                block,
                out_block,
                whole(3, EXTRA_ROWS, hidden),
                whole(2, RANK, width),
                whole(8, 3 * RANK, width // 8),
                whole(4, rows, heads_width),
            ),
            scratch_shapes=[
                pltpu.VMEM((2, hidden // 2, LANES), F32),
                pltpu.VMEM((2, hidden, LANES), F32),
                pltpu.VMEM((4, hidden, LANES), F32),
                pltpu.VMEM((8, width), F32),
            ],
        ),
        out_shape=(
            shape((3, hidden // 2, width), BF16),
            shape((out_rows, width), BF16),
            shape((3, EXTRA_ROWS, hidden)),
            shape((2, RANK, width)),
            shape((8, 3 * RANK, width // 8), BF16),
            shape((4, rows, heads_width), BF16),
        ),
        compiler_params=PARAMS,
        cost_estimate=cost(14),
        name="prepare_second",
    )(place, *bases, *lefts, *rights, *out, magnitude, *sent, *near)


def slot_of(place, block):
    away = lax.rem(block // 2 - place[0] + 4, 4)
    other = jnp.where(place[1] == block % 2, 0, 1)
    return jnp.where(
        away == 0, other, jnp.where(away == 1, 3 + 2 * other, jnp.where(away == 2, 6 + other, 2 + 2 * other))
    )


def block_of(place, slot):
    dz, dx = SLOTS[slot]
    return 2 * lax.rem(place[0] + dz + 4, 4) + (place[1] if dx == 0 else 1 - place[1])


def turned(values, cosine, sine):
    return values * cosine + pltpu.roll(values, HEAD_DIM // 2, 1) * sine


def turned_back(grads, cosine, sine):
    return grads * cosine - pltpu.roll(grads, HEAD_DIM // 2, 1) * sine


def project_heads_kernel(first_slot, place, b0, b1, b2, b3, weight, stats, cosine, sine, out_ref):
    blocks = jnp.concatenate([b[...] for b in (b0, b1, b2, b3)], axis=0)
    rows = b0.shape[0]
    width = weight.shape[1]
    values = jnp.dot(blocks, weight[...], preferred_element_type=F32) * stats[1:2, :]
    for s in range(4):
        at = pl.ds(pl.multiple_of(block_of(place, first_slot + s) * rows, rows), rows)
        cos, sin = cosine[at, :], sine[at, :]
        for head in range(width // HEAD_DIM):
            head_at = slice(head * HEAD_DIM, (head + 1) * HEAD_DIM)
            part = values[s * rows : (s + 1) * rows, head_at]
            if head < 2 * width // HEAD_DIM // 3:
                part = turned(part, cos, sin)
            out_ref[s, :, head_at] = part.astype(BF16)


def project_heads(first_slot, place, blocks, weight, stats, cosine, sine):
    rows = blocks[0].shape[0]
    return pl.pallas_call(
        functools.partial(project_heads_kernel, first_slot),
        out_shape=shape((4, rows, weight.shape[1]), BF16),
        in_specs=[SMEM] + [VMEM] * 8,
        out_specs=VMEM,
        compiler_params=PARAMS,
        cost_estimate=cost(5.5),
        name="project_heads",
    )(place, *blocks, weight, stats, cosine, sine)


def low_kernel(ql, kl, vl, *refs):
    *blocks, out_ref = refs
    rows = blocks[0].shape[0]
    lefts = jnp.concatenate([ql[...], kl[...], vl[...]], axis=0)
    for s, block in enumerate(blocks):
        out_ref[:, s * rows : (s + 1) * rows] = dot_nt(lefts, block[...]).astype(BF16)


def low_terms(lefts, blocks):
    rows = blocks[0].shape[0]
    return pl.pallas_call(
        low_kernel,
        out_shape=shape((3 * RANK, rows * len(blocks)), BF16),
        in_specs=[VMEM] * (3 + len(blocks)),
        out_specs=VMEM,
        compiler_params=PARAMS,
        cost_estimate=cost(4.5),
        name="low_terms",
    )(*lefts, *blocks)


def masked_scores(place, query, key, first_row):
    scores = dot_nt(query, key)
    row = first_row + lax.broadcasted_iota(jnp.int32, (query.shape[0], 1), 0)
    start = jnp.where(row < place[4], 0, jnp.where(row < place[5], place[4], place[5]))
    column = lax.broadcasted_iota(jnp.int32, scores.shape, 1)
    return jnp.where((column <= row) & (column >= start), scores, MASKED_SCORE)


def place_blocks(place, near, far, held):
    rows = near.shape[1]
    for block in range(2 * near.shape[0]):
        slot = slot_of(place, block)
        at = slice(block * rows, (block + 1) * rows)

        @pl.when(slot < 4)
        def _():
            held[at, :] = near[jnp.minimum(slot, 3)]

        @pl.when(slot >= 4)
        def _():
            held[at, :] = far[jnp.maximum(slot - 4, 0)]


def attend_kernel(place, near, far, terms, out_ref, log_ref, held):
    length = held.shape[0]
    width = out_ref.shape[2]
    rows = near.shape[1]
    out_ref[:, rows:, :] = terms[...]
    place_blocks(place, near, far, held)
    for first in range(0, length, QUERY_ROWS):
        last = first + QUERY_ROWS
        for head in range(width // HEAD_DIM):
            at = slice(head * HEAD_DIM, (head + 1) * HEAD_DIM)
            key_at = slice(width + head * HEAD_DIM, width + (head + 1) * HEAD_DIM)
            value_at = slice(2 * width + head * HEAD_DIM, 2 * width + (head + 1) * HEAD_DIM)
            scores = masked_scores(place, held[first:last, at], held[:last, key_at], first)
            largest = jnp.max(scores, axis=-1, keepdims=True)
            weights = jnp.exp2((scores - largest) * EXPONENT_SCALE)
            totals = jnp.sum(weights, axis=-1, keepdims=True)
            probs = (weights * (1.0 / totals)).astype(BF16)
            out = jnp.dot(probs, held[:last, value_at], preferred_element_type=F32)
            for i in range(QUERY_ROWS // rows):
                out_ref[first // rows + i, 0:rows, at] = out[i * rows : (i + 1) * rows].astype(BF16)
            log_ref[first:last, at] = jnp.broadcast_to(
                largest * EXPONENT_SCALE + jnp.log2(totals), (QUERY_ROWS, HEAD_DIM)
            )


def attend(place, near, far, terms):
    blocks, rows, width = near.shape
    length = 2 * blocks * rows
    groups = terms.shape[0]
    return pl.pallas_call(
        attend_kernel,
        out_shape=(
            shape((groups, length // groups + terms.shape[1], width // 3), BF16),
            shape((length, width // 3)),
        ),
        in_specs=[SMEM] + [VMEM] * 3,
        out_specs=(VMEM, VMEM),
        scratch_shapes=[pltpu.VMEM((length, width), BF16)],
        compiler_params=PARAMS,
        cost_estimate=cost(7.5),
        name="attend",
    )(place, near, far, terms)


def attend_back_kernel(
    place, near, far, log_ref, grad_ref, cosine, sine, stats,
    out_ref, sum_ref, held, total,
):
    length = held.shape[0]
    width = grad_ref.shape[2]
    rows = near.shape[1]
    place_blocks(place, near, far, held)
    for first in reversed(range(0, length, QUERY_ROWS)):
        last = first + QUERY_ROWS
        for head in range(width // HEAD_DIM):
            at = slice(head * HEAD_DIM, (head + 1) * HEAD_DIM)
            key_at = slice(width + head * HEAD_DIM, width + (head + 1) * HEAD_DIM)
            value_at = slice(2 * width + head * HEAD_DIM, 2 * width + (head + 1) * HEAD_DIM)
            query = held[first:last, at]
            key = held[:last, key_at]
            scores = masked_scores(place, query, key, first)
            logs = log_ref[first:last, head * HEAD_DIM : head * HEAD_DIM + 1]
            probs = jnp.exp2(scores * EXPONENT_SCALE - logs)
            grad = jnp.concatenate(
                [grad_ref[i, 0:rows, at] for i in range(first // rows, last // rows)], axis=0
            )
            grad_probs = dot_nt(grad, held[:last, value_at])
            inner = jnp.sum(grad_probs * probs, axis=-1, keepdims=True)
            grad_scores = (probs * (grad_probs - inner)).astype(BF16)
            total[first:last, at] = (
                jnp.dot(grad_scores, key, preferred_element_type=F32) * SCORE_SCALE
            )
            grad_key = dot_tn(grad_scores, query) * SCORE_SCALE
            grad_value = dot_tn(probs, grad)
            if last == length:
                total[:, key_at] = grad_key
                total[:, value_at] = grad_value
            else:
                total[:last, key_at] += grad_key
                total[:last, value_at] += grad_value
    heads = 3 * width // HEAD_DIM
    for head in range(heads):
        at = slice(head * HEAD_DIM, (head + 1) * HEAD_DIM)
        sums = jnp.zeros((1, HEAD_DIM), F32)
        for block in range(length // rows):
            block_at = slice(block * rows, (block + 1) * rows)
            grads = total[block_at, at]
            values = held[block_at, at].astype(F32)
            if head < 2 * heads // 3:
                cos, sin = cosine[block_at, :], sine[block_at, :]
                grads = turned_back(grads, cos, sin)
                values = turned_back(values, cos, sin)
            sums += jnp.sum(grads * values, axis=0, keepdims=True)
            out_ref[slot_of(place, block), :, at] = (grads * stats[1:2, at]).astype(BF16)
        sum_ref[:, at] = jnp.broadcast_to(sums, (8, HEAD_DIM))


def attend_back(place, near, far, logs, grad, cosine, sine, stats):
    blocks, rows, width = near.shape
    length = 2 * blocks * rows
    return pl.pallas_call(
        attend_back_kernel,
        out_shape=(shape((2 * blocks, rows, width), BF16), shape((8, width))),
        in_specs=[SMEM] + [VMEM] * 7,
        out_specs=(VMEM, VMEM),
        scratch_shapes=[pltpu.VMEM((length, width), BF16), pltpu.VMEM((length, width), F32)],
        compiler_params=PARAMS,
        cost_estimate=cost(10.5),
        name="attend_back",
    )(place, near, far, logs, grad, cosine, sine, stats)


def heads_back_kernel(grads, source, *refs):
    *outs, dz, weight, sems = refs
    rows = grads.shape[1]
    chunks = weight.shape[0]
    columns = weight.shape[1]
    copies = [
        pltpu.make_async_copy(source.at[pl.ds(i * columns, columns)], weight.at[i], sems.at[i])
        for i in range(chunks)
    ]
    start_all([copies])
    for s in range(len(outs)):
        dz[s * rows : (s + 1) * rows, :] = grads[s]
    for i in range(chunks):
        copies[i].wait()
        part = dot_nt(dz[...], weight[i]).astype(BF16)
        for s, out in enumerate(outs):
            out[:, i * columns : (i + 1) * columns] = part[s * rows : (s + 1) * rows]


def weight_copies(mine, others, buffer, sems):
    return [
        pltpu.make_async_copy(source.at[i], buffer.at[2 * i + j], sems.at[2 * i + j])
        for i in range(mine.shape[0])
        for j, source in enumerate((mine, others))
    ]


def start_all(copies):
    for group in copies:
        for copy in group:
            copy.start()


def wait_all(group):
    for copy in group:
        copy.wait()


def column_of(place, i, lanes):
    core = place[3] if i % 2 == 0 else 1 - place[3]
    return pl.ds(pl.multiple_of((2 * (i // 2) + core) * lanes, lanes), lanes)


def output_kernel(
    place, arrived, resid, magnitude, gain, mine, others, raw_ref, resid_ref, normed_ref, row_ref, buffer, sems
):
    copies = weight_copies(mine, others, buffer, sems)
    start_all([copies])
    rows = resid.shape[0]
    groups, lanes = arrived.shape[0], arrived.shape[2]
    tokens = jnp.concatenate([arrived[t, 0:rows, :] for t in range(groups)], axis=1)
    squares = 0.0
    for t in range(groups):
        parts = arrived[t, rows + RANK : rows + 3 * RANK, :].astype(F32)
        squares += parts[0:RANK] + parts[RANK : 2 * RANK]
    squares = jnp.concatenate(
        [
            jnp.concatenate([squares[i * 8 + j : i * 8 + j + 1] for j in range(8)], axis=1)
            for i in range(2)
        ],
        axis=0,
    )
    scales = magnitude[...] * lax.rsqrt(squares)
    row_ref[0:2, :] = squares
    row_ref[2:4, :] = scales
    row_ref[4:8, :] = jnp.zeros((4, squares.shape[1]), F32)
    for i, copy in enumerate(copies):
        copy.wait()
        raw_ref[:, column_of(place, i, lanes)] = jnp.dot(
            tokens, buffer[i], preferred_element_type=F32
        )
    resid_two = resid[...].astype(F32) + raw_ref[...] * scales[0:1]
    resid_ref[...] = resid_two
    _, _, normed_ref[...] = rms_forward(resid_two, gain[...])


def output_forward(place, arrived, resid, magnitude, gain, columns):
    rows, width = resid.shape
    return pl.pallas_call(
        output_kernel,
        out_shape=(
            shape((rows, width)),
            shape((rows, width)),
            shape((rows, width), BF16),
            shape((8, width)),
        ),
        in_specs=[SMEM] + [VMEM] * 4 + [ANY] * len(columns),
        out_specs=(VMEM,) * 4,
        scratch_shapes=[
            pltpu.VMEM((8, *columns[0].shape[1:]), BF16),
            pltpu.SemaphoreType.DMA((8,)),
        ],
        compiler_params=PARAMS,
        cost_estimate=cost(7.5),
        name="output_forward",
    )(place, arrived, resid, magnitude, gain, *columns)


def output_back_kernel(
    place, own, below, above, down_own, down_below, down_above, cot, raw, resid, row, gain, right, mine,
    others, grad_ref, dz_ref, head_ref, layer_ref, buffer, total, sems,
):
    copies = weight_copies(mine, others, buffer, sems)
    start_all([copies])
    scales = row[2:4, :]
    grad_normed = own[...].astype(F32) + below[...].astype(F32) + above[...].astype(F32)
    resid_two = resid[...]
    cotangent = cot[...].astype(F32)
    inverse = lax.rsqrt(jnp.mean(resid_two * resid_two, axis=-1, keepdims=True) + EPSILON)
    grad = cotangent + rms_backward(grad_normed, resid_two * inverse, inverse, gain[...])
    grad_ref[...] = grad
    dz = (grad * scales[0:1]).astype(BF16)
    dz_ref[...] = dz
    down = (
        down_own[...].astype(F32) + down_below[...].astype(F32) + down_above[...].astype(F32)
    ) * scales[1:2]
    layer_ref[...] = (resid_two + down).astype(BF16)
    sums = (
        jnp.sum(grad * raw[...], axis=0, keepdims=True) * scales[0:1],
        jnp.sum(cotangent * down, axis=0, keepdims=True),
    )
    rows, lanes = dz.shape[0], buffer.shape[2]
    through = dot_nt(right[...], dz)
    terms = jnp.concatenate(
        [jnp.concatenate([through, jnp.zeros((RANK, lanes - rows), F32)], axis=1)]
        + [s[:, j * lanes : (j + 1) * lanes] for s in sums for j in range(8)],
        axis=0,
    ).astype(BF16)
    for i, copy in enumerate(copies):
        copy.wait()
        part = dot_nt(dz_ref[:, column_of(place, i, lanes)], buffer[i])
        if i == 0:
            total[...] = part
        else:
            total[...] += part
    for t in range(head_ref.shape[0]):
        head_ref[t, 0:rows, :] = total[:, t * lanes : (t + 1) * lanes].astype(BF16)
        head_ref[t, rows:, :] = terms


def output_back(place, back, forward, cot, raw, resid, row, gain, right, columns, groups):
    rows, width = resid.shape
    return pl.pallas_call(
        output_back_kernel,
        out_shape=(
            shape((rows, width)),
            shape((rows, width), BF16),
            shape((groups, rows + 2 * RANK, width // groups), BF16),
            shape((rows, width), BF16),
        ),
        in_specs=[SMEM] + [VMEM] * 12 + [ANY] * len(columns),
        out_specs=(VMEM,) * 4,
        scratch_shapes=[
            pltpu.VMEM((8, *columns[0].shape[1:]), BF16),
            pltpu.VMEM((rows, width), F32),
            pltpu.SemaphoreType.DMA((8,)),
        ],
        compiler_params=PARAMS,
        cost_estimate=cost(8),
        name="output_back",
    )(place, *back, *forward, cot, raw, resid, row, gain, right, *columns)


def hidden_copies(place, halves_of, planes, buffer, sems):
    half = buffer.shape[2] // 2
    copies = []
    for c in range(2):
        for k, plane in enumerate(planes):
            for j, which in enumerate((place[3], 1 - place[3])):
                rows = pl.ds(pl.multiple_of(which * half, half), half)
                copies.append(
                    pltpu.make_async_copy(
                        halves_of[2 * c + j].at[plane],
                        buffer.at[c, k, rows],
                        sems.at[2 * len(planes) * c + 2 * k + j],
                    )
                )
    return copies


def ends_of(rows):
    return (0, rows, 2 * rows, 3 * rows, 3 * rows + rows // 2, 4 * rows)


def hidden_start_kernel(
    place, cot_own, cot_below, cot_above, cot_low, cot_high, row, send, keep, pulled, swapped,
    grad_ref, dz_ref, buffer, sems,
):
    copies = hidden_copies(place, (send, keep, pulled, swapped), (2,), buffer, sems)
    start_all([copies])
    ends = ends_of(cot_own.shape[0])
    for i, block in enumerate((cot_own, cot_below, cot_above, cot_low, cot_high)):
        dz_ref[ends[i] : ends[i + 1], :] = (block[...].astype(F32) * row[3:4, :]).astype(BF16)
    for c in range(2):
        wait_all(copies[2 * c : 2 * c + 2])
        grad_ref[c] = dot_nt(dz_ref[...], buffer[c, 0]).astype(BF16)


def hidden_start(place, cot, row, weights):
    rows, width = cot[0].shape
    hidden = 2 * weights[0].shape[1]
    return pl.pallas_call(
        hidden_start_kernel,
        out_shape=(shape((2, 4 * rows, hidden), BF16), shape((4 * rows, width), BF16)),
        in_specs=[SMEM] + [VMEM] * 6 + [ANY] * 4,
        out_specs=(VMEM,) * 2,
        scratch_shapes=[pltpu.VMEM((2, 1, hidden, width), BF16), pltpu.SemaphoreType.DMA((4,))],
        compiler_params=PARAMS,
        cost_estimate=cost(7),
        name="hidden_start",
    )(place, *cot, row, *weights)


def hidden_middle_kernel(
    place, own, below, above, far_low, far_high, grads, extra, extra_other, send, keep, pulled, swapped,
    f0, f1, f2, f3, f4, act_ref, gate_ref, up_ref, sum_ref, tokens, buffer, sems,
):
    copies = hidden_copies(place, (send, keep, pulled, swapped), (0, 1, 2), buffer, sems)
    start_all([copies])
    ends = ends_of(own.shape[0])
    for i, block in enumerate((own, below, above, far_low, far_high)):
        tokens[ends[i] : ends[i + 1], :] = block[...]
    sum_ref[...] = jnp.zeros_like(sum_ref)
    for c in range(2):
        factors = (extra, extra_other)[c]
        gate_scale = factors[0, SCALE : SCALE + 1, :]
        up_scale = factors[1, SCALE : SCALE + 1, :]
        wait_all(copies[6 * c : 6 * c + 2])
        gate = dot_nt(tokens[...], buffer[c, 0]) * gate_scale
        wait_all(copies[6 * c + 2 : 6 * c + 4])
        upper = dot_nt(tokens[...], buffer[c, 1]) * up_scale
        grad = grads[c].astype(F32)
        sigmoid = 0.5 + 0.5 * jnp.tanh(0.5 * gate)
        silu = gate * sigmoid
        act_ref[c] = (silu * upper).astype(BF16)
        grad_up = grad * silu
        grad_gate = grad * upper * (sigmoid + silu * (1.0 - sigmoid))
        sum_ref[c, 0:1, :] = jnp.sum(grad_gate * gate, axis=0, keepdims=True)
        sum_ref[c, 1:2, :] = jnp.sum(grad_up * upper, axis=0, keepdims=True)
        gate_ref[c] = (grad_gate * gate_scale).astype(BF16)
        up_ref[c] = (grad_up * up_scale).astype(BF16)
        wait_all(copies[6 * c + 4 : 6 * c + 6])
    columns = 512
    outs = (f0, f1, f2, f3, f4)
    for at in range(0, tokens.shape[1], columns):
        part = dot(act_ref[0], buffer[0, 2, :, at : at + columns])
        part = (part + dot(act_ref[1], buffer[1, 2, :, at : at + columns])).astype(BF16)
        for i, out in enumerate(outs):
            out[:, at : at + columns] = part[ends[i] : ends[i + 1]]


def hidden_middle(place, tokens, grads, extra, extra_other, weights):
    rows, width = tokens[0].shape
    hidden = extra.shape[2]
    total = 4 * rows
    return pl.pallas_call(
        hidden_middle_kernel,
        out_shape=(
            *(shape((n, width), BF16) for n in (rows, rows, rows, rows // 2, rows // 2)),
            *(shape((2, total, hidden), BF16),) * 3,
            shape((2, 8, hidden)),
        ),
        in_specs=[SMEM] + [VMEM] * 8 + [ANY] * 4,
        out_specs=(VMEM,) * 9,
        scratch_shapes=[
            pltpu.VMEM((total, width), BF16),
            pltpu.VMEM((2, 3, hidden, width), BF16),
            pltpu.SemaphoreType.DMA((12,)),
        ],
        compiler_params=PARAMS,
        cost_estimate=cost(20),
        name="hidden_middle",
    )(place, *tokens, grads, extra, extra_other, *weights)


def hidden_back_kernel(first, place, gate, upper, send, keep, pulled, swapped, *refs):
    *outs, total, backs, buffer, sems, back_sems = refs
    copies = hidden_copies(place, (send, keep, pulled, swapped), (0, 1), buffer, sems)
    rows = total.shape[0]
    back_copies = [
        pltpu.make_async_copy(
            source.at[c, pl.ds(first, rows)], backs.at[c, k], back_sems.at[2 * c + k]
        )
        for c in range(2)
        for k, source in enumerate((gate, upper))
    ]
    for i, copy in enumerate(back_copies):
        start_all([[copy], copies[2 * i : 2 * i + 2]])
    columns = 512
    for i, copy in enumerate(back_copies):
        wait_all([copy, *copies[2 * i : 2 * i + 2]])
        c, k = i // 2, i % 2
        for lanes in range(0, total.shape[1], columns):
            lane_at = slice(lanes, lanes + columns)
            part = dot(backs[c, k], buffer[c, k, :, lane_at])
            if i == 0:
                total[:, lane_at] = part
            elif i < 3:
                total[:, lane_at] += part
            else:
                part = (part + total[:, lane_at]).astype(BF16)
                at = 0
                for out in outs:
                    out[:, lane_at] = part[at : at + out.shape[0], :]
                    at += out.shape[0]


def hidden_back(far, place, gate, upper, weights, rows):
    width = weights[0].shape[2]
    hidden = gate.shape[2]
    counts = (rows // 2, rows // 2) if far else (rows, rows, rows)
    return pl.pallas_call(
        functools.partial(hidden_back_kernel, 3 * rows if far else 0),
        out_shape=tuple(shape((n, width), BF16) for n in counts),
        in_specs=[SMEM] + [ANY] * 6,
        out_specs=(VMEM,) * len(counts),
        scratch_shapes=[
            pltpu.VMEM((sum(counts), width), F32),
            pltpu.VMEM((2, 2, sum(counts), hidden), BF16),
            pltpu.VMEM((2, 2, hidden, width), BF16),
            pltpu.SemaphoreType.DMA((8,)),
            pltpu.SemaphoreType.DMA((4,)),
        ],
        compiler_params=PARAMS,
        cost_estimate=cost(8),
        name="hidden_back",
    )(place, gate, upper, *weights)


def hidden_grads_kernel(
    own, below, above, far_low, far_high, dz, act_in, gate_in, upper_in, sums, extra, extra_other, lefts_t,
    lefts_u, down_right, left_ref, down_ref, mine_ref, sent_ref, gate, upper, act, sems,
):
    copies = [
        pltpu.make_async_copy(source.at[c], target.at[c], sems.at[3 * c + i])
        for c in range(2)
        for i, (source, target) in enumerate(((gate_in, gate), (upper_in, upper), (act_in, act)))
    ]
    start_all([copies])
    tokens = jnp.concatenate([r[...] for r in (own, below, above, far_low, far_high)], axis=0)
    lows = dot_nt(jnp.concatenate([lefts_t[...], lefts_u[...]], axis=0), tokens)
    down_through = dot_nt(down_right[...], dz[...])
    throughs = [0.0, 0.0]
    low_down = 0.0
    for c, (factors, out) in enumerate(((extra, mine_ref), (extra_other, sent_ref))):
        for i, back in enumerate((gate, upper)):
            copies[3 * c + i].wait()
            throughs[i] += dot_nt(factors[i, 0:RANK, :], back[c])
            out[i * RANK : (i + 1) * RANK, :] = dot(lows[i * RANK : (i + 1) * RANK], back[c]).astype(
                out.dtype
            )
        copies[3 * c + 2].wait()
        low_down += dot_nt(factors[2, 0:RANK, :], act[c])
        out[2 * RANK : 3 * RANK, :] = dot(down_through, act[c]).astype(out.dtype)
        out[3 * RANK :, :] = jnp.concatenate(
            [sums[c], jnp.zeros_like(sums[c])], axis=0
        ).astype(out.dtype)
    through = jnp.concatenate(throughs, axis=0)
    left_ref[...] = dot(through, tokens)
    down_ref[...] = dot(low_down, dz[...])


def hidden_grads(tokens, dz, act, gate, upper, sums, extra, extra_other, lefts_t, lefts_u, down_right):
    width = dz.shape[1]
    hidden = act.shape[2]
    return pl.pallas_call(
        hidden_grads_kernel,
        out_shape=(
            shape((2 * RANK, width)),
            shape((RANK, width)),
            shape((4 * RANK, hidden)),
            shape((4 * RANK, hidden), BF16),
        ),
        in_specs=[VMEM] * 6 + [ANY] * 3 + [VMEM] * 6,
        out_specs=(VMEM,) * 4,
        scratch_shapes=[*(pltpu.VMEM(act.shape, BF16),) * 3, pltpu.SemaphoreType.DMA((6,))],
        compiler_params=PARAMS,
        cost_estimate=cost(8.4),
        name="hidden_grads",
    )(*tokens, dz, act, gate, upper, sums, extra, extra_other, lefts_t, lefts_u, down_right)


def half_copies(place, send, keep, planes, buffer, sems):
    half = buffer.shape[1] // 2
    copies = []
    for j, (source, which) in enumerate(((send, place[3]), (keep, 1 - place[3]))):
        rows = pl.ds(pl.multiple_of(which * half, half), half)
        copies.append(
            pltpu.make_async_copy(source.at[planes], buffer.at[:, rows], sems.at[j])
        )
    return copies


def hidden_norms_kernel(
    place, left, mine, other, extra, extra_other, lefts_t, lefts_u, send, keep, pulled, swapped,
    left_ref, cross_ref, weight, sems,
):
    copies = hidden_copies(place, (send, keep, pulled, swapped), (0, 1), weight, sems)
    start_all([copies])
    totals = [left[0:RANK, :], left[RANK : 2 * RANK, :]]
    for c, (factors, parts) in enumerate(((extra, mine), (extra_other, other))):
        for i, left_t in enumerate((lefts_t, lefts_u)):
            sums = parts[3 * RANK + i : 3 * RANK + i + 1, :].astype(F32)
            coefficient = -sums / factors[i, SQUARES : SQUARES + 1, :]
            wait_all(copies[4 * c + 2 * i : 4 * c + 2 * i + 2])
            totals[i] += dot(factors[i, 0:RANK, :] * coefficient, weight[c, i])
            if c == 0:
                cross_ref[i] = dot_nt(left_t[...], weight[c, i])
    left_ref[...] = FACTOR * jnp.concatenate(totals, axis=0)


def hidden_norms(place, left, mine, other, extra, extra_other, lefts_t, lefts_u, weights):
    width, hidden = left.shape[1], mine.shape[1]
    return pl.pallas_call(
        hidden_norms_kernel,
        out_shape=(shape((2 * RANK, width)), shape((2, RANK, hidden))),
        in_specs=[SMEM] + [VMEM] * 7 + [ANY] * 4,
        out_specs=(VMEM,) * 2,
        scratch_shapes=[
            pltpu.VMEM((2, 2, hidden, width), BF16),
            pltpu.SemaphoreType.DMA((8,)),
        ],
        compiler_params=PARAMS,
        cost_estimate=cost(9),
        name="hidden_norms",
    )(place, left, mine, other, extra, extra_other, lefts_t, lefts_u, *weights)


SPLIT_LANES = 256


def gathered_sums(received, tokens):
    sums = 0.0
    for t in range(received.shape[0]):
        sums += received[t, tokens + RANK : tokens + 2 * RANK, :].astype(F32)
    return jnp.concatenate(
        [
            jnp.concatenate([sums[8 * i + j : 8 * i + j + 1] for j in range(8)], axis=1)
            for i in range(2)
        ],
        axis=0,
    )


def split_grads_kernel(
    place, send, keep, grads, lows, heads_stats, heads_sums, heads_cross, mine, given, row, received,
    out_right, down_right, out_weight, attended, extra, cross, split_ref, down_weight, sems,
):
    copies = half_copies(place, send, keep, slice(2, 3), down_weight, sems)
    start_all([copies])
    width = row.shape[1]
    columns = heads_sums.shape[1] // 3
    slots, tokens = grads.shape[:2]
    row_sums = gathered_sums(received, tokens)
    above = 3 * RANK
    hidden = mine.shape[1]
    parts = mine[...] + given[...].astype(F32)
    hidden_rows = []
    for i in range(2):
        coefficient = -parts[3 * RANK + i : 3 * RANK + i + 1] / extra[i, SQUARES : SQUARES + 1, :]
        hidden_rows.append(
            FACTOR * (parts[i * RANK : (i + 1) * RANK] + cross[i] * coefficient)
        )
    split_ref[0:above, 0:hidden] = jnp.concatenate(
        [*hidden_rows, parts[3 * RANK :]], axis=0
    ).astype(BF16)
    split_ref[0:above, hidden:] = jnp.zeros((above, split_ref.shape[1] - hidden), BF16)
    split_ref[above:, 2 * SPLIT_LANES :] = jnp.zeros(
        (split_ref.shape[0] - above, split_ref.shape[1] - 2 * SPLIT_LANES), BF16
    )

    def put(lanes, values):
        split_ref[above:, lanes] = values.astype(BF16)

    coefficient = -heads_sums[0:1, :] / heads_stats[0:1, :]
    first = []
    for i in range(3):
        at = slice(i * columns, (i + 1) * columns)
        dz = jnp.concatenate([grads[s, :, at] for s in range(slots)], axis=0)
        first.append(
            FACTOR
            * (
                jnp.dot(lows[i * RANK : (i + 1) * RANK, :], dz, preferred_element_type=F32)
                + heads_cross[:, at] * coefficient[:, at]
            )
        )
    out_coefficient, down_coefficient = (
        -row_sums[i : i + 1, :] / row[i : i + 1, :] for i in range(2)
    )
    out_left = 0.0
    for t in range(received.shape[0]):
        through = received[t, tokens : tokens + RANK, 0:tokens]
        out_left += dot(through, attended[t, 0:tokens, :])
    first.append(FACTOR * (out_left + dot_nt(out_right[...] * out_coefficient, out_weight[...])))
    first.append(jnp.zeros((RANK, SPLIT_LANES), F32))
    put(slice(0, SPLIT_LANES), jnp.concatenate(first, axis=0))
    at = slice(2 * RANK, 3 * RANK)
    wait_all(copies)
    down_left = FACTOR * (
        parts[at, :] + dot_nt(down_right[...] * down_coefficient, down_weight[0])
    )
    hidden = down_left.shape[1]
    padded = (hidden + SPLIT_LANES - 1) // SPLIT_LANES * SPLIT_LANES
    down_left = jnp.concatenate([down_left, jnp.zeros((RANK, padded - hidden), F32)], axis=1)
    second = [
        down_left[:, j * SPLIT_LANES : (j + 1) * SPLIT_LANES] for j in range(padded // SPLIT_LANES)
    ]
    second += [
        row_sums[i : i + 1, j * SPLIT_LANES : (j + 1) * SPLIT_LANES]
        for i in range(2)
        for j in range(width // SPLIT_LANES)
    ]
    second += [heads_sums[0:1, i * columns : (i + 1) * columns] for i in range(3)]
    used = sum(r.shape[0] for r in second)
    second.append(jnp.zeros((5 * RANK - used, SPLIT_LANES), F32))
    put(slice(SPLIT_LANES, 2 * SPLIT_LANES), jnp.concatenate(second, axis=0))


def tail_kernel(*refs):
    inputs, (weight, *rest) = refs[:18], refs[18:]
    outs, (split_ref, dz, buffer, sems, down_weight, down_sems) = rest[:-6], rest[-6:]
    heads_back_kernel(inputs[3], weight, *outs, dz, buffer, sems)
    split_grads_kernel(*inputs, split_ref, down_weight, down_sems)


def tail(arrays, weight):
    half, width = arrays[1].shape[1:]
    above, lanes = 3 * RANK, (2 * half + LANES - 1) // LANES * LANES
    blocks, rows, columns = arrays[3].shape
    chunks = 4
    return pl.pallas_call(
        tail_kernel,
        out_shape=(
            *(shape((rows, width), BF16),) * blocks,
            shape((above + 5 * RANK, lanes), BF16),
        ),
        in_specs=[SMEM, ANY, ANY] + [VMEM] * (len(arrays) - 3) + [ANY],
        out_specs=(VMEM,) * (blocks + 1),
        scratch_shapes=[
            pltpu.VMEM((blocks * rows, columns), BF16),
            pltpu.VMEM((chunks, width // chunks, columns), BF16),
            pltpu.SemaphoreType.DMA((chunks,)),
            pltpu.VMEM((1, 2 * half, width), BF16),
            pltpu.SemaphoreType.DMA((2,)),
        ],
        compiler_params=PARAMS,
        cost_estimate=cost(13),
        name="tail",
    )(*arrays, weight)


def unpack_kernel(total, *outs):
    lane_blocks = outs[0].shape[1] // LANES
    for group, out in enumerate(outs):
        for i in range(lane_blocks):
            out[:, i * LANES : (i + 1) * LANES] = total[group * lane_blocks + i].astype(F32)


def unpack(total, count, width):
    return pl.pallas_call(
        unpack_kernel,
        out_shape=(shape((RANK, width)),) * count,
        in_specs=[VMEM],
        out_specs=(VMEM,) * count,
        compiler_params=PARAMS,
        cost_estimate=cost(2),
        name="unpack",
    )(total)


def shared_grads_kernel(
    grads, heads_weight, heads_stats, heads_sums, qr, kr, vr, left, down, row, received,
    row_cross, arrived, out_dz, *refs,
):
    *blocks, terms_ref = refs
    tokens, width = out_dz.shape
    row_sums = gathered_sums(received, tokens)

    def put(group, rows):
        rows = rows.astype(BF16)
        lane_blocks = width // LANES
        for i in range(lane_blocks):
            terms_ref[group * lane_blocks + i] = rows[:, i * LANES : (i + 1) * LANES]

    columns = heads_weight.shape[1] // 3
    coefficient = -heads_sums[0:1, :] / heads_stats[0:1, :]
    throughs, norms = [], []
    for i, right in enumerate((qr, kr, vr)):
        at = slice(i * columns, (i + 1) * columns)
        dz = jnp.concatenate([grads[s, :, at] for s in range(len(blocks))], axis=0)
        throughs.append(dot_nt(right[...], dz))
        norms.append(right[...] * coefficient[:, at])
    through = jnp.concatenate(throughs, axis=0).astype(BF16)
    total = 0.0
    for s in range(0, len(blocks), 2):
        pair = jnp.concatenate([blocks[s][...], blocks[s + 1][...]], axis=0)
        total += jnp.dot(
            through[:, s * tokens : (s + 2) * tokens], pair, preferred_element_type=F32
        )
    for i in range(3):
        at = slice(i * columns, (i + 1) * columns)
        rows = total[i * RANK : (i + 1) * RANK]
        put(i, FACTOR * (rows + dot_nt(norms[i], heads_weight[:, at])))
    put(3, left[0:RANK, :])
    put(4, left[RANK : 2 * RANK, :])
    out_coefficient, down_coefficient = (
        -row_sums[i : i + 1, :] / row[i : i + 1, :] for i in range(2)
    )
    low = 0.0
    for t in range(arrived.shape[0]):
        low += dot_nt(arrived[t, tokens : tokens + RANK, :], arrived[t, 0:tokens, :])
    put(5, FACTOR * (dot(low, out_dz[...]) + row_cross[0] * out_coefficient))
    put(6, FACTOR * (down[...] + row_cross[1] * down_coefficient))
    put(7, jnp.zeros((RANK, width), F32))


def shared_grads(arrays, blocks):
    width = blocks[0].shape[1]
    return pl.pallas_call(
        shared_grads_kernel,
        out_shape=shape((8 * width // LANES, RANK, LANES), BF16),
        in_specs=[VMEM] * (len(arrays) + len(blocks)),
        out_specs=VMEM,
        compiler_params=PARAMS,
        cost_estimate=cost(8),
        name="shared_grads",
    )(*arrays, *blocks)


def on_device(
    hidden_in,
    segment_ids,
    attention_gain,
    mlp_gain,
    query_base,
    query_left,
    query_right,
    query_magnitude,
    key_base,
    key_left,
    key_right,
    key_magnitude,
    value_base,
    value_left,
    value_right,
    value_magnitude,
    output_base,
    output_left,
    output_right,
    output_magnitude,
    gate_base,
    gate_left,
    gate_right,
    gate_magnitude,
    up_base,
    up_left,
    up_right,
    up_magnitude,
    down_base,
    down_left,
    down_right,
    down_magnitude,
    cotangent,
):
    resid = hidden_in[0]
    cot = cotangent[0]
    rows, width = resid.shape
    segments = segment_ids[0]
    length = segments.shape[0]
    heads_width = query_base.shape[1]
    hidden = gate_base.shape[1]
    mlp_row = mlp_gain[None]
    zero_count = jnp.sum((segments == 0).astype(jnp.int32))
    one_count = jnp.sum((segments <= 1).astype(jnp.int32))
    place = jnp.stack(
        [lax.axis_index(a).astype(jnp.int32) for a in ("z", "xl", "y", "core")]
        + [zero_count, one_count]
    )

    _, _, normed_one = rms_forward(resid.astype(F32), attention_gain)
    other, below, above = x_swap(normed_one), z_up(normed_one), z_down(normed_one)

    piece = output_piece(after(place, normed_one), output_base, output_left.T, output_right)
    received = all_to_all(piece, TENSOR)

    hidden_bases = (gate_base.T, up_base.T, down_base)
    hidden_lefts = (gate_left.T, up_left.T, down_left.T)
    hidden_rights = (gate_right, up_right, down_right)
    heads_magnitude = jnp.concatenate([query_magnitude, key_magnitude, value_magnitude])[None]
    hidden_send, *hidden_sent = prepare_send(
        after(place, piece), hidden_bases, hidden_lefts, hidden_rights
    )
    other, below, above, hidden_send = lax.optimization_barrier((other, below, above, hidden_send))

    other_below, other_above = z_up(other), z_down(other)
    pulled = from_x_neighbour(hidden_send)
    starts = jnp.where(segments == 0, 0, jnp.where(segments == 1, zero_count, one_count))
    positions = (jnp.arange(length, dtype=jnp.int32) - after(starts, other)).astype(F32)
    frequency = 10000.0 ** (-jnp.arange(0, HEAD_DIM, 2, dtype=F32) / HEAD_DIM)
    angles = positions[:, None] * frequency[None, :]
    cosine, sine = jnp.cos(angles), jnp.sin(angles)
    cosine = jnp.concatenate([cosine, cosine], axis=-1)
    sine = jnp.concatenate([-sine, sine], axis=-1)

    received = after(received, cosine, sine)
    heads_weight, heads_stats, heads_cross = prepare_heads(
        (query_base, key_base, value_base),
        (query_left.T, key_left.T, value_left.T),
        (query_right, key_right, value_right),
        after(heads_magnitude, received, other),
    )
    out_mine = of_everyone(received.reshape(width, piece.shape[2]), "y")
    other_below, other_above, below, second_place, _ = lax.optimization_barrier(
        (other_below, other_above, below, place, heads_stats)
    )
    other_far, far_one = z_down(other_above), z_up(below)
    hidden_magnitude = jnp.stack([gate_magnitude, up_magnitude])
    hidden_keep, out_weight, extra, row_cross, row_terms, near = prepare_second(
        second_place,
        hidden_bases,
        hidden_lefts,
        hidden_rights,
        (output_base, output_left.T, output_right),
        hidden_magnitude,
        hidden_sent,
        (normed_one, other, below, above, heads_weight, heads_stats, cosine, sine),
    )
    other_far, far_one, far_place, cot_held, extra = lax.optimization_barrier(
        (other_far, far_one, place, cot, extra)
    )
    extra_other = x_swap(extra)
    cot_near = (z_up(cot_held), z_down(cot_held))
    row_blocks = [
        normed_one, other, below, above, other_below, other_above, far_one, other_far
    ]
    far = project_heads(4, far_place, row_blocks[4:], heads_weight, heads_stats, cosine, sine)
    *cot_near, extra_other, attend_place, _ = lax.optimization_barrier(
        (*cot_near, extra_other, place, far)
    )
    half_rows = rows // 2
    cot_all = (
        cot,
        *cot_near,
        z_up(cot_near[0][:half_rows]),
        z_down(cot_near[1][half_rows:]),
    )
    attended, logs = attend(attend_place, near, far, row_terms)
    attended, *cot_ends = lax.optimization_barrier((attended, *cot_all[3:]))
    cot_all = (*cot_all[:3], *cot_ends)
    row_magnitude = jnp.stack([output_magnitude, down_magnitude])
    out_mine = after(out_mine, attended)
    out_columns = (out_mine, core_swap(out_mine))
    arrived = all_to_all(attended, TENSOR)
    swapped = core_swap(after(pulled, attended))

    out_raw, resid_two, normed_two, row = output_forward(
        place, arrived, resid, row_magnitude, mlp_row, out_columns
    )
    hidden_weights = (hidden_send, hidden_keep, pulled, swapped)
    grad_activated, down_dz = hidden_start(place, cot_all, row, hidden_weights)
    heads_lows = low_terms(
        (after(query_left.T, grad_activated), key_left.T, value_left.T), row_blocks
    )
    tokens = gather_z(normed_two, lambda: grad_activated)
    tokens = (*tokens[:3], *lax.optimization_barrier((*tokens[3:], heads_lows))[:2])
    *forward, act, gate_back, up_back, hidden_sums = hidden_middle(
        place, tokens, grad_activated, extra, extra_other, hidden_weights
    )
    far_parts = hidden_back(
        True, after(place, forward[0]), gate_back, up_back, hidden_weights, rows
    )
    forward = scatter_z(*forward, lambda: far_parts[0])
    near_parts = hidden_back(
        False, after(place, far_parts[0], forward[3]), gate_back, up_back, hidden_weights, rows
    )
    back = scatter_z(*near_parts, *far_parts, lambda: (near_parts[0], forward[1], forward[2]))
    hidden_terms = hidden_grads(
        tokens,
        after(down_dz, back[3]),
        act,
        gate_back,
        up_back,
        hidden_sums,
        extra,
        extra_other,
        gate_left.T,
        up_left.T,
        down_right,
    )
    gate_up_left, down_right_part, mine, sent = hidden_terms
    grad_two, out_dz, head_part, layer = output_back(
        after(place, mine),
        back[:3],
        forward[:3],
        cot,
        out_raw,
        resid_two,
        row,
        mlp_row,
        output_right,
        out_columns,
        8,
    )
    given = x_swap(sent)
    gate_up_left, hidden_cross = hidden_norms(
        after(place, head_part),
        gate_up_left,
        mine,
        sent,
        extra,
        extra_other,
        gate_left.T,
        up_left.T,
        hidden_weights,
    )
    received = after(all_to_all(head_part, TENSOR), gate_up_left, given)

    heads_dz, heads_sums = attend_back(
        place, near, far, logs, received, cosine, sine, heads_stats
    )
    *parts, split = tail(
        (
            place,
            hidden_send,
            hidden_keep,
            heads_dz,
            heads_lows,
            heads_stats,
            heads_sums,
            heads_cross,
            mine,
            given,
            row,
            received,
            output_right,
            down_right,
            out_weight,
            attended,
            extra,
            hidden_cross,
        ),
        heads_weight,
    )
    terms = shared_grads(
        (
            after(heads_dz, parts[0]),
            heads_weight,
            heads_stats,
            heads_sums,
            query_right,
            key_right,
            value_right,
            gate_up_left,
            down_right_part,
            row,
            received,
            row_cross,
            arrived,
            out_dz,
        ),
        row_blocks,
    )
    hop, other_hop = z_up(parts[6]), z_down(parts[7])
    other_from_below = z_up(parts[5])
    from_above = z_down(parts[2])
    hop, other_hop, other_from_below, from_above, _ = lax.optimization_barrier(
        (hop, other_hop, other_from_below, from_above, terms)
    )
    other_part = add(parts[4], other_hop).astype(BF16)
    other_from_above = z_down(other_part)
    from_below = z_up(add(parts[3], hop).astype(BF16))
    split = add(split, core_swap(split)).astype(BF16)
    split = add(split, lax.ppermute(split, "xh", SWAP)).astype(BF16)
    split = add(split, lax.ppermute(split, "y", ((0, 1), (1, 0), (2, 3), (3, 2)))).astype(BF16)
    total = after(all_to_all(terms, ALL), other_part, split).astype(F32).sum(axis=0).astype(BF16)
    split_other = lax.ppermute(split, "y", ((0, 2), (2, 0), (1, 3), (3, 1)))
    other_from_above, split_other = lax.optimization_barrier((other_from_above, split_other))
    split = add(split, split_other)
    across = add(parts[1], other_from_below, other_from_above).astype(BF16)
    grad_normed_one = add(parts[0], from_below, from_above, x_swap(across))
    resid = resid.astype(F32)
    inverse = lax.rsqrt(jnp.mean(resid * resid, axis=-1, keepdims=True) + EPSILON)
    input_grad = grad_two + rms_backward(grad_normed_one, resid * inverse, inverse, attention_gain)
    hidden_split, split = split[: 3 * RANK, :hidden], split[3 * RANK :]
    total = unpack(after(of_everyone(total, ALL), other_from_above).reshape(-1, RANK, LANES), 7, width)
    hidden_magnitude_grad = hidden_split[2 * RANK : 2 * RANK + 2] / hidden_magnitude
    heads, rest = split[:, :SPLIT_LANES], split[:, SPLIT_LANES : 2 * SPLIT_LANES]
    parts = (hidden + SPLIT_LANES - 1) // SPLIT_LANES
    down_left_grad = jnp.concatenate([rest[i * RANK : (i + 1) * RANK] for i in range(parts)], axis=1)
    at = parts * RANK
    row_magnitude_grad = rest[at : at + 2 * width // SPLIT_LANES].reshape(2, width) / row_magnitude
    at += 2 * width // SPLIT_LANES
    heads_magnitude_grad = rest[at : at + 3] / heads_magnitude.reshape(3, -1)
    return (
        layer[None],
        input_grad[None],
        total[0].T,
        heads[:RANK],
        heads_magnitude_grad[0],
        total[1].T,
        heads[RANK : 2 * RANK],
        heads_magnitude_grad[1],
        total[2].T,
        heads[2 * RANK : 3 * RANK],
        heads_magnitude_grad[2],
        heads[3 * RANK : 4 * RANK].T,
        total[5],
        row_magnitude_grad[0],
        total[3].T,
        hidden_split[:RANK],
        hidden_magnitude_grad[0],
        total[4].T,
        hidden_split[RANK : 2 * RANK],
        hidden_magnitude_grad[1],
        down_left_grad[:, :hidden].T,
        total[6],
        row_magnitude_grad[1],
    )


def solution(mesh):
    torus = Mesh(mesh.devices.reshape(4, 2, 2, 4, 2), ("y", "xh", "core", "z", "xl"))
    column = (P(None, TENSOR), P(), P(None, TENSOR), P(TENSOR))
    row = (P(TENSOR, None), P(TENSOR, None), P(), P())
    column_out, row_out = column[1:], row[1:]
    tokens = P(DP, TENSOR, None)
    return jax.shard_map(
        on_device,
        mesh=torus,
        in_specs=(
            tokens,
            P(DP, None),
            P(),
            P(),
            *column,
            *column,
            *column,
            *row,
            *column,
            *column,
            *row,
            tokens,
        ),
        out_specs=(
            tokens,
            tokens,
            *column_out,
            *column_out,
            *column_out,
            *row_out,
            *column_out,
            *column_out,
            *row_out,
        ),
        check_vma=False,
    )
```

```python
import functools

import jax
import jax.numpy as jnp
from jax import lax
from jax.experimental import pallas as pl
from jax.experimental.pallas import tpu as pltpu
from jax.sharding import Mesh
from jax.sharding import PartitionSpec as P

HEAD_DIM = 128
RANK = 16
ALPHA = 32
FACTOR = ALPHA / RANK
EPSILON = 1e-05
MASKED_SCORE = -1e30
DP = ("y", "xh", "core")
TENSOR = ("z", "xl")
ALL = DP + TENSOR
BF16 = jnp.bfloat16
F32 = jnp.float32

SWAP = ((0, 1), (1, 0))
UP = tuple((i, (i + 1) % 4) for i in range(4))
DOWN = tuple((i, (i + 3) % 4) for i in range(4))
SLOTS = ((0, 0), (0, 1), (-1, 0), (1, 0), (-1, 1), (1, 1), (2, 0), (2, 1))
SLOT_AT = ((0, 1), (3, 5), (6, 7), (2, 4))


def z_up(array):
    return lax.ppermute(array, "z", UP)


def z_down(array):
    return lax.ppermute(array, "z", DOWN)


def y_up(array):
    return lax.ppermute(array, "y", UP)


def y_down(array):
    return lax.ppermute(array, "y", DOWN)


def x_swap(array):
    return lax.ppermute(array, "xl", SWAP)


def core_swap(array):
    return lax.ppermute(array, "core", SWAP)


def from_x_neighbour(array):
    pairs = []
    for x in range(4):
        for core in range(2):
            source = (x ^ 1) if core else (x + 3 if x % 2 == 0 else x + 1) % 4
            pairs.append(
                ((source // 2) * 4 + core * 2 + source % 2, (x // 2) * 4 + core * 2 + x % 2)
            )
    return lax.ppermute(array, ("xh", "core", "xl"), tuple(pairs))


def add(*terms):
    total = terms[0].astype(F32)
    for term in terms[1:]:
        total = total + term.astype(F32)
    return total


def gather_z(own, meanwhile):
    half = own.shape[0] // 2
    below, above, _ = lax.optimization_barrier((z_up(own), z_down(own), meanwhile()))
    return own, below, above, z_up(below[:half]), z_down(above[half:])


def halves_kernel(above, below, low, high, above_ref, below_ref):
    half = low.shape[0]
    above_ref[0:half, :] = (above[0:half, :].astype(F32) + low[...].astype(F32)).astype(BF16)
    above_ref[half:, :] = above[half:, :]
    below_ref[0:half, :] = below[0:half, :]
    below_ref[half:, :] = (below[half:, :].astype(F32) + high[...].astype(F32)).astype(BF16)


def add_halves(above, below, low, high):
    vmem = pl.BlockSpec(memory_space=pltpu.VMEM)
    return pl.pallas_call(
        halves_kernel,
        out_shape=(jax.ShapeDtypeStruct(above.shape, BF16),) * 2,
        in_specs=[vmem] * 4,
        out_specs=(vmem,) * 2,
        name="add_halves",
    )(above, below, low, high)


def scatter_z(own, below, above, far_low, far_high, meanwhile):
    low = z_up(far_low)
    high = z_down(far_high)
    low, high = lax.optimization_barrier((low, high, meanwhile()))[:2]
    above_sum, below_sum = add_halves(above, below, low, high)
    return own, z_up(above_sum), z_down(below_sum), above_sum


def all_to_all(array, axes):
    return lax.all_to_all(array, axes, 0, 0, tiled=True)


def of_everyone(array, axes):
    count = lax.axis_size(axes)
    return all_to_all(jnp.broadcast_to(array[None], (count, *array.shape)), axes)


def dot(left, right):
    return jnp.dot(left.astype(BF16), right.astype(BF16), preferred_element_type=F32)


def dot_nt(left, right):
    return lax.dot_general(
        left.astype(BF16), right.astype(BF16), (((1,), (1,)), ((), ())), preferred_element_type=F32
    )


def dot_tn(left, right):
    return lax.dot_general(
        left.astype(BF16), right.astype(BF16), (((0,), (0,)), ((), ())), preferred_element_type=F32
    )


def after_all(*arrays):
    return lax.optimization_barrier(arrays)[:-1]


def rms_forward(resid, gain):
    inverse = lax.rsqrt(jnp.mean(resid * resid, axis=-1, keepdims=True) + EPSILON)
    normal = resid * inverse
    return normal, inverse, (normal * gain.astype(F32)).astype(BF16)


def rms_backward(grad_normed, normal, inverse, gain):
    scaled = grad_normed * gain.astype(F32)
    return inverse * (scaled - normal * jnp.mean(scaled * normal, axis=-1, keepdims=True))


VMEM = pl.BlockSpec(memory_space=pltpu.VMEM)
SMEM = pl.BlockSpec(memory_space=pltpu.SMEM)
ANY = pl.BlockSpec(memory_space=pl.ANY)
QUERY_ROWS = 512
SCORE_SCALE = HEAD_DIM ** (-0.5)
EXPONENT_SCALE = SCORE_SCALE * 1.4426950408889634
MIB = 1024 * 1024
LANES = 128
COST = 1.0
SQUARES, SCALE = RANK, RANK + 1
EXTRA_ROWS = 24


def shape(dims, dtype=F32):
    return jax.ShapeDtypeStruct(dims, dtype)


PARAMS = pltpu.CompilerParams(vmem_limit_bytes=60 * MIB)


def cost(micros):
    return pl.CostEstimate(
        flops=0, bytes_accessed=int(micros * COST * 3.69e6), transcendentals=0
    )


def after(array, *earlier):
    return lax.optimization_barrier((array, *earlier))[0]


def whole_spec(dims):
    return pl.BlockSpec(dims, lambda *_: (0,) * len(dims))


def prepare_heads_kernel(q, k, v, al, bl, cl, ar, br, cr, mag, weight_ref, stats_ref, cross_ref):
    step = pl.program_id(0)
    columns = q.shape[1]

    @pl.when(step == 0)
    def _():
        stats_ref[...] = jnp.zeros_like(stats_ref)
        cross_ref[...] = jnp.zeros_like(cross_ref)

    for i, (base, left, right) in enumerate(((q, al, ar), (k, bl, br), (v, cl, cr))):
        at_columns = slice(i * columns, (i + 1) * columns)
        factor = left[...].astype(BF16)
        weight = base[...].astype(F32) + dot_tn(FACTOR * factor, right[...])
        low = weight.astype(BF16)
        weight_ref[:, at_columns] = low
        stats_ref[0:1, at_columns] += jnp.sum(weight * weight, axis=0, keepdims=True)
        cross_ref[:, at_columns] += dot(factor, low)

    @pl.when(step == pl.num_programs(0) - 1)
    def _():
        stats_ref[1:2, :] = mag[...] * lax.rsqrt(stats_ref[0:1, :])


def output_piece_kernel(place, base, left, right, piece_ref):
    weight = (base[...].astype(F32) + FACTOR * dot_tn(left[...], right[...])).astype(BF16)
    for t in range(piece_ref.shape[0]):
        piece_ref[t] = weight


def output_piece(place, base, left, right):
    rows, width = base.shape
    columns = width // 8

    def column(i, place):
        return 0, 2 * place[2] + place[3]

    return pl.pallas_call(
        output_piece_kernel,
        grid_spec=pltpu.PrefetchScalarGridSpec(
            num_scalar_prefetch=1,
            grid=(1,),
            in_specs=[
                pl.BlockSpec((rows, columns), column),
                pl.BlockSpec((RANK, rows), lambda i, place: (0, 0)),
                pl.BlockSpec((RANK, columns), column),
            ],
            out_specs=pl.BlockSpec((8, rows, columns), lambda i, place: (0, 0, 0)),
        ),
        out_shape=shape((8, rows, columns), BF16),
        compiler_params=PARAMS,
        cost_estimate=cost(2.5),
        name="output_piece",
    )(place, base, left, right)


def halves(which):
    def index(place):
        return place[3] if which == 0 else 1 - place[3]

    return index


def adapted_rows(step, bases, factors, squares, sums, cross):
    rows, width = bases[0].shape
    lows = []
    for i, (base, (left, right)) in enumerate(zip(bases, factors)):
        weight = base[...].astype(F32) + dot(left, FACTOR * right)
        low = weight.astype(BF16)
        lows.append(low)
        if i < 2:
            square = weight * weight
            at = pl.ds(pl.multiple_of(step * rows, rows), rows)
            squares[i, at, :] = sum(square[:, j : j + LANES] for j in range(0, width, LANES))
        else:
            sums[...] += jnp.sum(weight * weight, axis=0, keepdims=True)
            cross[...] += dot_tn(left, low)
    return lows


def down_sublanes(factor):
    unit = (
        lax.broadcasted_iota(jnp.int32, (RANK, LANES), 0)
        == lax.broadcasted_iota(jnp.int32, (RANK, LANES), 1)
    ).astype(BF16)
    return dot_tn(factor, unit)


def prepare_send_kernel(
    place, g, u, d, gl, ul, dl, gr, ur, dr, send_ref, squares_ref, sums_ref, cross_ref, columns
):
    step = pl.program_id(0)
    rows = g.shape[0]

    @pl.when(step == 0)
    def _():
        for i, factor in enumerate((gr, ur, dl)):
            columns[i] = down_sublanes(factor[...])
        cross_ref[...] = jnp.zeros_like(cross_ref)
        sums_ref[...] = jnp.zeros_like(sums_ref)

    at = pl.ds(pl.multiple_of((pl.num_programs(0) * place[3] + step) * rows, rows), rows)
    factors = [(columns[i, at, 0:RANK], right[...]) for i, right in enumerate((gl, ul, dr))]
    lows = adapted_rows(step, (g, u, d), factors, squares_ref, sums_ref, cross_ref)
    for i, low in enumerate(lows):
        send_ref[i] = low


def prepare_keep_kernel(
    place, g, u, d, gl, ul, dl, gr, ur, dr, o, ol, orr, mag, squares_in, sums_in, cross_in,
    keep_ref, out_ref, extra_ref, cross_ref, terms_ref, squares, squares_all, columns, sums,
):
    step = pl.program_id(0)
    steps = pl.num_programs(0)
    rows = g.shape[0]
    out_rows, width = o.shape

    @pl.when(step == 0)
    def _():
        for i, factor in enumerate((gr, ur, dl)):
            columns[i] = down_sublanes(factor[...])
        columns[3, 0 : ol.shape[1], :] = down_sublanes(ol[...])
        cross_ref[0] = jnp.zeros_like(cross_in)
        cross_ref[1] = cross_in[...]
        sums[0:1, :] = jnp.zeros_like(sums_in)
        sums[1:2, :] = sums_in[...]

    at = pl.ds(pl.multiple_of((steps * (1 - place[3]) + step) * rows, rows), rows)
    factors = [(columns[i, at, 0:RANK], right[...]) for i, right in enumerate((gl, ul, dr))]
    lows = adapted_rows(step, (g, u, d), factors, squares, sums.at[1:2], cross_ref.at[1])
    for i, low in enumerate(lows):
        keep_ref[i] = low
    left = columns[3, pl.ds(pl.multiple_of(step * out_rows, out_rows), out_rows), 0:RANK]
    weight = o[...].astype(F32) + dot(left, FACTOR * orr[...])
    low = weight.astype(BF16)
    out_ref[...] = low
    cross_ref[0] += dot_tn(left, low)
    sums[0:1, :] += jnp.sum(weight * weight, axis=0, keepdims=True)

    @pl.when(step == steps - 1)
    def _():
        half = squares.shape[1]
        for core, part in ((place[3], squares_in), (1 - place[3], squares)):
            squares_all[:, pl.ds(pl.multiple_of(core * half, half), half), :] = part[...]
        extra_ref[...] = jnp.zeros_like(extra_ref)
        for i, right in enumerate((gr, ur)):
            extra_ref[i, 0:RANK, :] = right[...]
            total = lax.dot_general(
                jnp.ones((8, LANES), F32),
                squares_all[i],
                (((1,), (1,)), ((), ())),
                precision=lax.Precision.HIGHEST,
                preferred_element_type=F32,
            )
            extra_ref[i, SQUARES : SQUARES + 1, :] = total[0:1]
            extra_ref[i, SCALE : SCALE + 1, :] = mag[i : i + 1, :] * lax.rsqrt(total[0:1])
        extra_ref[2, 0:RANK, :] = dl[...]
        lanes = terms_ref.shape[2]
        total = jnp.concatenate(
            [sums[i : i + 1, j : j + lanes] for i in range(2) for j in range(0, width, lanes)], axis=0
        )
        high = total.astype(BF16)
        rest = (total - high.astype(F32)).astype(BF16)
        for t in range(terms_ref.shape[0]):
            terms_ref[t, 0:RANK, :] = ol[...].astype(BF16)
            terms_ref[t, RANK : RANK + 16, :] = high
            terms_ref[t, RANK + 16 :, :] = rest


HALF_STEPS = 2


def half_specs(which, hidden, width):
    rows = hidden // 2 // HALF_STEPS
    half = halves(which)

    def whole(*dims):
        return pl.BlockSpec(dims, lambda i, place: (0,) * len(dims))

    base = pl.BlockSpec((rows, width), lambda i, place: (HALF_STEPS * half(place) + i, 0))
    specs = [base] * 3 + [whole(RANK, width)] * 2 + [whole(RANK, hidden)] * 3 + [whole(RANK, width)]
    return specs, whole, pl.BlockSpec((3, rows, width), lambda i, place: (0, i, 0))


def prepare_send(place, bases, lefts, rights):
    hidden, width = bases[0].shape
    specs, whole, block = half_specs(0, hidden, width)
    return pl.pallas_call(
        prepare_send_kernel,
        grid_spec=pltpu.PrefetchScalarGridSpec(
            num_scalar_prefetch=1,
            grid=(HALF_STEPS,),
            in_specs=specs,
            out_specs=(block, whole(2, hidden // 2, LANES), whole(1, width), whole(RANK, width)),
            scratch_shapes=[pltpu.VMEM((3, hidden, LANES), F32)],
        ),
        out_shape=(
            shape((3, hidden // 2, width), BF16),
            shape((2, hidden // 2, LANES)),
            shape((1, width)),
            shape((RANK, width)),
        ),
        compiler_params=PARAMS,
        cost_estimate=cost(6),
        name="prepare_send",
    )(place, *bases, *lefts, *rights)


def prepare_heads(bases, lefts, rights, magnitude):
    width, columns = bases[0].shape
    rows = width // HALF_STEPS
    return pl.pallas_call(
        prepare_heads_kernel,
        grid=(HALF_STEPS,),
        out_shape=(
            shape((width, 3 * columns), BF16),
            shape((8, 3 * columns)),
            shape((RANK, 3 * columns)),
        ),
        in_specs=[pl.BlockSpec((rows, columns), lambda i: (i, 0))] * 3
        + [pl.BlockSpec((RANK, rows), lambda i: (0, i))] * 3
        + [whole_spec((RANK, columns))] * 3
        + [whole_spec((1, 3 * columns))],
        out_specs=(
            pl.BlockSpec((rows, 3 * columns), lambda i: (i, 0)),
            whole_spec((8, 3 * columns)),
            whole_spec((RANK, 3 * columns)),
        ),
        compiler_params=PARAMS,
        cost_estimate=cost(6),
        name="prepare_heads",
    )(*bases, *lefts, *rights, magnitude)


def prepare_second_kernel(place, *refs):
    inputs, near_inputs, outputs = refs[:16], refs[16:24], refs[24:]
    prepare_keep_kernel(place, *inputs, *outputs[:5], *outputs[6:])

    @pl.when(pl.program_id(0) == 0)
    def _():
        project_heads_kernel(0, place, *near_inputs, outputs[5])


def prepare_second(place, bases, lefts, rights, out, magnitude, sent, near):
    hidden, width = bases[0].shape
    out_rows = out[0].shape[0]
    specs, whole, block = half_specs(1, hidden, width)
    out_block = pl.BlockSpec((out_rows // HALF_STEPS, width), lambda i, place: (i, 0))
    rows, heads_width = near[0].shape[0], near[4].shape[1]
    return pl.pallas_call(
        prepare_second_kernel,
        grid_spec=pltpu.PrefetchScalarGridSpec(
            num_scalar_prefetch=1,
            grid=(HALF_STEPS,),
            in_specs=specs
            + [
                out_block,
                whole(RANK, out_rows),
                whole(RANK, width),
                whole(2, hidden),
                whole(2, hidden // 2, LANES),
                whole(1, width),
                whole(RANK, width),
            ]
            + [whole(*a.shape) for a in near],
            out_specs=(
                block,
                out_block,
                whole(3, EXTRA_ROWS, hidden),
                whole(2, RANK, width),
                whole(8, 3 * RANK, width // 8),
                whole(4, rows, heads_width),
            ),
            scratch_shapes=[
                pltpu.VMEM((2, hidden // 2, LANES), F32),
                pltpu.VMEM((2, hidden, LANES), F32),
                pltpu.VMEM((4, hidden, LANES), F32),
                pltpu.VMEM((8, width), F32),
            ],
        ),
        out_shape=(
            shape((3, hidden // 2, width), BF16),
            shape((out_rows, width), BF16),
            shape((3, EXTRA_ROWS, hidden)),
            shape((2, RANK, width)),
            shape((8, 3 * RANK, width // 8), BF16),
            shape((4, rows, heads_width), BF16),
        ),
        compiler_params=PARAMS,
        cost_estimate=cost(14),
        name="prepare_second",
    )(place, *bases, *lefts, *rights, *out, magnitude, *sent, *near)


def slot_of(place, block):
    away = lax.rem(block // 2 - place[0] + 4, 4)
    other = jnp.where(place[1] == block % 2, 0, 1)
    return jnp.where(
        away == 0, other, jnp.where(away == 1, 3 + 2 * other, jnp.where(away == 2, 6 + other, 2 + 2 * other))
    )


def block_of(place, slot):
    dz, dx = SLOTS[slot]
    return 2 * lax.rem(place[0] + dz + 4, 4) + (place[1] if dx == 0 else 1 - place[1])


def turned(values, cosine, sine):
    return values * cosine + pltpu.roll(values, HEAD_DIM // 2, 1) * sine


def turned_back(grads, cosine, sine):
    return grads * cosine - pltpu.roll(grads, HEAD_DIM // 2, 1) * sine


def project_heads_kernel(first_slot, place, b0, b1, b2, b3, weight, stats, cosine, sine, out_ref):
    blocks = jnp.concatenate([b[...] for b in (b0, b1, b2, b3)], axis=0)
    rows = b0.shape[0]
    width = weight.shape[1]
    values = jnp.dot(blocks, weight[...], preferred_element_type=F32) * stats[1:2, :]
    for s in range(4):
        at = pl.ds(pl.multiple_of(block_of(place, first_slot + s) * rows, rows), rows)
        cos, sin = cosine[at, :], sine[at, :]
        for head in range(width // HEAD_DIM):
            head_at = slice(head * HEAD_DIM, (head + 1) * HEAD_DIM)
            part = values[s * rows : (s + 1) * rows, head_at]
            if head < 2 * width // HEAD_DIM // 3:
                part = turned(part, cos, sin)
            out_ref[s, :, head_at] = part.astype(BF16)


def project_heads(first_slot, place, blocks, weight, stats, cosine, sine):
    rows = blocks[0].shape[0]
    return pl.pallas_call(
        functools.partial(project_heads_kernel, first_slot),
        out_shape=shape((4, rows, weight.shape[1]), BF16),
        in_specs=[SMEM] + [VMEM] * 8,
        out_specs=VMEM,
        compiler_params=PARAMS,
        cost_estimate=cost(5.5),
        name="project_heads",
    )(place, *blocks, weight, stats, cosine, sine)


def low_kernel(ql, kl, vl, *refs):
    *blocks, out_ref = refs
    rows = blocks[0].shape[0]
    lefts = jnp.concatenate([ql[...], kl[...], vl[...]], axis=0)
    for s, block in enumerate(blocks):
        out_ref[:, s * rows : (s + 1) * rows] = dot_nt(lefts, block[...]).astype(BF16)


def low_terms(lefts, blocks):
    rows = blocks[0].shape[0]
    return pl.pallas_call(
        low_kernel,
        out_shape=shape((3 * RANK, rows * len(blocks)), BF16),
        in_specs=[VMEM] * (3 + len(blocks)),
        out_specs=VMEM,
        compiler_params=PARAMS,
        cost_estimate=cost(4.5),
        name="low_terms",
    )(*lefts, *blocks)


def masked_scores(place, query, key, first_row):
    scores = dot_nt(query, key)
    row = first_row + lax.broadcasted_iota(jnp.int32, (query.shape[0], 1), 0)
    start = jnp.where(row < place[4], 0, jnp.where(row < place[5], place[4], place[5]))
    column = lax.broadcasted_iota(jnp.int32, scores.shape, 1)
    return jnp.where((column <= row) & (column >= start), scores, MASKED_SCORE)


def place_blocks(place, near, far, held):
    rows = near.shape[1]
    for block in range(2 * near.shape[0]):
        slot = slot_of(place, block)
        at = slice(block * rows, (block + 1) * rows)

        @pl.when(slot < 4)
        def _():
            held[at, :] = near[jnp.minimum(slot, 3)]

        @pl.when(slot >= 4)
        def _():
            held[at, :] = far[jnp.maximum(slot - 4, 0)]


def attend_kernel(place, near, far, terms, out_ref, log_ref, held):
    length = held.shape[0]
    width = out_ref.shape[2]
    rows = near.shape[1]
    out_ref[:, rows:, :] = terms[...]
    place_blocks(place, near, far, held)
    for first in range(0, length, QUERY_ROWS):
        last = first + QUERY_ROWS
        for head in range(width // HEAD_DIM):
            at = slice(head * HEAD_DIM, (head + 1) * HEAD_DIM)
            key_at = slice(width + head * HEAD_DIM, width + (head + 1) * HEAD_DIM)
            value_at = slice(2 * width + head * HEAD_DIM, 2 * width + (head + 1) * HEAD_DIM)
            scores = masked_scores(place, held[first:last, at], held[:last, key_at], first)
            largest = jnp.max(scores, axis=-1, keepdims=True)
            weights = jnp.exp2((scores - largest) * EXPONENT_SCALE)
            totals = jnp.sum(weights, axis=-1, keepdims=True)
            probs = (weights * (1.0 / totals)).astype(BF16)
            out = jnp.dot(probs, held[:last, value_at], preferred_element_type=F32)
            for i in range(QUERY_ROWS // rows):
                out_ref[first // rows + i, 0:rows, at] = out[i * rows : (i + 1) * rows].astype(BF16)
            log_ref[first:last, at] = jnp.broadcast_to(
                largest * EXPONENT_SCALE + jnp.log2(totals), (QUERY_ROWS, HEAD_DIM)
            )


def attend(place, near, far, terms):
    blocks, rows, width = near.shape
    length = 2 * blocks * rows
    groups = terms.shape[0]
    return pl.pallas_call(
        attend_kernel,
        out_shape=(
            shape((groups, length // groups + terms.shape[1], width // 3), BF16),
            shape((length, width // 3)),
        ),
        in_specs=[SMEM] + [VMEM] * 3,
        out_specs=(VMEM, VMEM),
        scratch_shapes=[pltpu.VMEM((length, width), BF16)],
        compiler_params=PARAMS,
        cost_estimate=cost(7.5),
        name="attend",
    )(place, near, far, terms)


def attend_back_kernel(
    place, near, far, log_ref, grad_ref, cosine, sine, stats,
    out_ref, sum_ref, held, total,
):
    length = held.shape[0]
    width = grad_ref.shape[2]
    rows = near.shape[1]
    place_blocks(place, near, far, held)
    for first in reversed(range(0, length, QUERY_ROWS)):
        last = first + QUERY_ROWS
        for head in range(width // HEAD_DIM):
            at = slice(head * HEAD_DIM, (head + 1) * HEAD_DIM)
            key_at = slice(width + head * HEAD_DIM, width + (head + 1) * HEAD_DIM)
            value_at = slice(2 * width + head * HEAD_DIM, 2 * width + (head + 1) * HEAD_DIM)
            query = held[first:last, at]
            key = held[:last, key_at]
            scores = masked_scores(place, query, key, first)
            logs = log_ref[first:last, head * HEAD_DIM : head * HEAD_DIM + 1]
            probs = jnp.exp2(scores * EXPONENT_SCALE - logs)
            grad = jnp.concatenate(
                [grad_ref[i, 0:rows, at] for i in range(first // rows, last // rows)], axis=0
            )
            grad_probs = dot_nt(grad, held[:last, value_at])
            inner = jnp.sum(grad_probs * probs, axis=-1, keepdims=True)
            grad_scores = (probs * (grad_probs - inner)).astype(BF16)
            total[first:last, at] = (
                jnp.dot(grad_scores, key, preferred_element_type=F32) * SCORE_SCALE
            )
            grad_key = dot_tn(grad_scores, query) * SCORE_SCALE
            grad_value = dot_tn(probs, grad)
            if last == length:
                total[:, key_at] = grad_key
                total[:, value_at] = grad_value
            else:
                total[:last, key_at] += grad_key
                total[:last, value_at] += grad_value
    heads = 3 * width // HEAD_DIM
    for head in range(heads):
        at = slice(head * HEAD_DIM, (head + 1) * HEAD_DIM)
        sums = jnp.zeros((1, HEAD_DIM), F32)
        for block in range(length // rows):
            block_at = slice(block * rows, (block + 1) * rows)
            grads = total[block_at, at]
            values = held[block_at, at].astype(F32)
            if head < 2 * heads // 3:
                cos, sin = cosine[block_at, :], sine[block_at, :]
                grads = turned_back(grads, cos, sin)
                values = turned_back(values, cos, sin)
            sums += jnp.sum(grads * values, axis=0, keepdims=True)
            out_ref[slot_of(place, block), :, at] = (grads * stats[1:2, at]).astype(BF16)
        sum_ref[:, at] = jnp.broadcast_to(sums, (8, HEAD_DIM))


def attend_back(place, near, far, logs, grad, cosine, sine, stats):
    blocks, rows, width = near.shape
    length = 2 * blocks * rows
    return pl.pallas_call(
        attend_back_kernel,
        out_shape=(shape((2 * blocks, rows, width), BF16), shape((8, width))),
        in_specs=[SMEM] + [VMEM] * 7,
        out_specs=(VMEM, VMEM),
        scratch_shapes=[pltpu.VMEM((length, width), BF16), pltpu.VMEM((length, width), F32)],
        compiler_params=PARAMS,
        cost_estimate=cost(10.5),
        name="attend_back",
    )(place, near, far, logs, grad, cosine, sine, stats)


def heads_back_kernel(grads, source, *refs):
    *outs, dz, weight, sems = refs
    rows = grads.shape[1]
    chunks = weight.shape[0]
    columns = weight.shape[1]
    copies = [
        pltpu.make_async_copy(source.at[pl.ds(i * columns, columns)], weight.at[i], sems.at[i])
        for i in range(chunks)
    ]
    start_all([copies])
    for s in range(len(outs)):
        dz[s * rows : (s + 1) * rows, :] = grads[s]
    for i in range(chunks):
        copies[i].wait()
        part = dot_nt(dz[...], weight[i]).astype(BF16)
        for s, out in enumerate(outs):
            out[:, i * columns : (i + 1) * columns] = part[s * rows : (s + 1) * rows]


def weight_copies(mine, others, buffer, sems):
    return [
        pltpu.make_async_copy(source.at[i], buffer.at[2 * i + j], sems.at[2 * i + j])
        for i in range(mine.shape[0])
        for j, source in enumerate((mine, others))
    ]


def start_all(copies):
    for group in copies:
        for copy in group:
            copy.start()


def wait_all(group):
    for copy in group:
        copy.wait()


def column_of(place, i, lanes):
    core = place[3] if i % 2 == 0 else 1 - place[3]
    return pl.ds(pl.multiple_of((2 * (i // 2) + core) * lanes, lanes), lanes)


def output_kernel(
    place, arrived, resid, magnitude, gain, mine, others, raw_ref, resid_ref, normed_ref, row_ref, buffer, sems
):
    copies = weight_copies(mine, others, buffer, sems)
    start_all([copies])
    rows = resid.shape[0]
    groups, lanes = arrived.shape[0], arrived.shape[2]
    tokens = jnp.concatenate([arrived[t, 0:rows, :] for t in range(groups)], axis=1)
    squares = 0.0
    for t in range(groups):
        parts = arrived[t, rows + RANK : rows + 3 * RANK, :].astype(F32)
        squares += parts[0:RANK] + parts[RANK : 2 * RANK]
    squares = jnp.concatenate(
        [
            jnp.concatenate([squares[i * 8 + j : i * 8 + j + 1] for j in range(8)], axis=1)
            for i in range(2)
        ],
        axis=0,
    )
    scales = magnitude[...] * lax.rsqrt(squares)
    row_ref[0:2, :] = squares
    row_ref[2:4, :] = scales
    row_ref[4:8, :] = jnp.zeros((4, squares.shape[1]), F32)
    for i, copy in enumerate(copies):
        copy.wait()
        raw_ref[:, column_of(place, i, lanes)] = jnp.dot(
            tokens, buffer[i], preferred_element_type=F32
        )
    resid_two = resid[...].astype(F32) + raw_ref[...] * scales[0:1]
    resid_ref[...] = resid_two
    _, _, normed_ref[...] = rms_forward(resid_two, gain[...])


def output_forward(place, arrived, resid, magnitude, gain, columns):
    rows, width = resid.shape
    return pl.pallas_call(
        output_kernel,
        out_shape=(
            shape((rows, width)),
            shape((rows, width)),
            shape((rows, width), BF16),
            shape((8, width)),
        ),
        in_specs=[SMEM] + [VMEM] * 4 + [ANY] * len(columns),
        out_specs=(VMEM,) * 4,
        scratch_shapes=[
            pltpu.VMEM((8, *columns[0].shape[1:]), BF16),
            pltpu.SemaphoreType.DMA((8,)),
        ],
        compiler_params=PARAMS,
        cost_estimate=cost(7.5),
        name="output_forward",
    )(place, arrived, resid, magnitude, gain, *columns)


def output_back_kernel(
    place, own, below, above, down_own, down_below, down_above, cot, raw, resid, row, gain, right, mine,
    others, grad_ref, dz_ref, head_ref, layer_ref, buffer, total, sems,
):
    copies = weight_copies(mine, others, buffer, sems)
    start_all([copies])
    scales = row[2:4, :]
    grad_normed = own[...].astype(F32) + below[...].astype(F32) + above[...].astype(F32)
    resid_two = resid[...]
    cotangent = cot[...].astype(F32)
    inverse = lax.rsqrt(jnp.mean(resid_two * resid_two, axis=-1, keepdims=True) + EPSILON)
    grad = cotangent + rms_backward(grad_normed, resid_two * inverse, inverse, gain[...])
    grad_ref[...] = grad
    dz = (grad * scales[0:1]).astype(BF16)
    dz_ref[...] = dz
    down = (
        down_own[...].astype(F32) + down_below[...].astype(F32) + down_above[...].astype(F32)
    ) * scales[1:2]
    layer_ref[...] = (resid_two + down).astype(BF16)
    sums = (
        jnp.sum(grad * raw[...], axis=0, keepdims=True) * scales[0:1],
        jnp.sum(cotangent * down, axis=0, keepdims=True),
    )
    rows, lanes = dz.shape[0], buffer.shape[2]
    through = dot_nt(right[...], dz)
    terms = jnp.concatenate(
        [jnp.concatenate([through, jnp.zeros((RANK, lanes - rows), F32)], axis=1)]
        + [s[:, j * lanes : (j + 1) * lanes] for s in sums for j in range(8)],
        axis=0,
    ).astype(BF16)
    for i, copy in enumerate(copies):
        copy.wait()
        part = dot_nt(dz_ref[:, column_of(place, i, lanes)], buffer[i])
        if i == 0:
            total[...] = part
        else:
            total[...] += part
    for t in range(head_ref.shape[0]):
        head_ref[t, 0:rows, :] = total[:, t * lanes : (t + 1) * lanes].astype(BF16)
        head_ref[t, rows:, :] = terms


def output_back(place, back, forward, cot, raw, resid, row, gain, right, columns, groups):
    rows, width = resid.shape
    return pl.pallas_call(
        output_back_kernel,
        out_shape=(
            shape((rows, width)),
            shape((rows, width), BF16),
            shape((groups, rows + 2 * RANK, width // groups), BF16),
            shape((rows, width), BF16),
        ),
        in_specs=[SMEM] + [VMEM] * 12 + [ANY] * len(columns),
        out_specs=(VMEM,) * 4,
        scratch_shapes=[
            pltpu.VMEM((8, *columns[0].shape[1:]), BF16),
            pltpu.VMEM((rows, width), F32),
            pltpu.SemaphoreType.DMA((8,)),
        ],
        compiler_params=PARAMS,
        cost_estimate=cost(8),
        name="output_back",
    )(place, *back, *forward, cot, raw, resid, row, gain, right, *columns)


def hidden_copies(place, halves_of, planes, buffer, sems):
    half = buffer.shape[2] // 2
    copies = []
    for c in range(2):
        for k, plane in enumerate(planes):
            for j, which in enumerate((place[3], 1 - place[3])):
                rows = pl.ds(pl.multiple_of(which * half, half), half)
                copies.append(
                    pltpu.make_async_copy(
                        halves_of[2 * c + j].at[plane],
                        buffer.at[c, k, rows],
                        sems.at[2 * len(planes) * c + 2 * k + j],
                    )
                )
    return copies


def ends_of(rows):
    return (0, rows, 2 * rows, 3 * rows, 3 * rows + rows // 2, 4 * rows)


def hidden_start_kernel(
    place, cot_own, cot_below, cot_above, cot_low, cot_high, row, send, keep, pulled, swapped,
    grad_ref, dz_ref, buffer, sems,
):
    copies = hidden_copies(place, (send, keep, pulled, swapped), (2,), buffer, sems)
    start_all([copies])
    ends = ends_of(cot_own.shape[0])
    for i, block in enumerate((cot_own, cot_below, cot_above, cot_low, cot_high)):
        dz_ref[ends[i] : ends[i + 1], :] = (block[...].astype(F32) * row[3:4, :]).astype(BF16)
    for c in range(2):
        wait_all(copies[2 * c : 2 * c + 2])
        grad_ref[c] = dot_nt(dz_ref[...], buffer[c, 0]).astype(BF16)


def hidden_start(place, cot, row, weights):
    rows, width = cot[0].shape
    hidden = 2 * weights[0].shape[1]
    return pl.pallas_call(
        hidden_start_kernel,
        out_shape=(shape((2, 4 * rows, hidden), BF16), shape((4 * rows, width), BF16)),
        in_specs=[SMEM] + [VMEM] * 6 + [ANY] * 4,
        out_specs=(VMEM,) * 2,
        scratch_shapes=[pltpu.VMEM((2, 1, hidden, width), BF16), pltpu.SemaphoreType.DMA((4,))],
        compiler_params=PARAMS,
        cost_estimate=cost(7),
        name="hidden_start",
    )(place, *cot, row, *weights)


def hidden_middle_kernel(
    place, own, below, above, far_low, far_high, grads, extra, extra_other, send, keep, pulled, swapped,
    f0, f1, f2, f3, f4, act_ref, gate_ref, up_ref, sum_ref, tokens, buffer, sems,
):
    copies = hidden_copies(place, (send, keep, pulled, swapped), (0, 1, 2), buffer, sems)
    start_all([copies])
    ends = ends_of(own.shape[0])
    for i, block in enumerate((own, below, above, far_low, far_high)):
        tokens[ends[i] : ends[i + 1], :] = block[...]
    sum_ref[...] = jnp.zeros_like(sum_ref)
    for c in range(2):
        factors = (extra, extra_other)[c]
        gate_scale = factors[0, SCALE : SCALE + 1, :]
        up_scale = factors[1, SCALE : SCALE + 1, :]
        wait_all(copies[6 * c : 6 * c + 2])
        gate = dot_nt(tokens[...], buffer[c, 0]) * gate_scale
        wait_all(copies[6 * c + 2 : 6 * c + 4])
        upper = dot_nt(tokens[...], buffer[c, 1]) * up_scale
        grad = grads[c].astype(F32)
        sigmoid = 0.5 + 0.5 * jnp.tanh(0.5 * gate)
        silu = gate * sigmoid
        act_ref[c] = (silu * upper).astype(BF16)
        grad_up = grad * silu
        grad_gate = grad * upper * (sigmoid + silu * (1.0 - sigmoid))
        sum_ref[c, 0:1, :] = jnp.sum(grad_gate * gate, axis=0, keepdims=True)
        sum_ref[c, 1:2, :] = jnp.sum(grad_up * upper, axis=0, keepdims=True)
        gate_ref[c] = (grad_gate * gate_scale).astype(BF16)
        up_ref[c] = (grad_up * up_scale).astype(BF16)
        wait_all(copies[6 * c + 4 : 6 * c + 6])
    columns = 512
    outs = (f0, f1, f2, f3, f4)
    for at in range(0, tokens.shape[1], columns):
        part = dot(act_ref[0], buffer[0, 2, :, at : at + columns])
        part = (part + dot(act_ref[1], buffer[1, 2, :, at : at + columns])).astype(BF16)
        for i, out in enumerate(outs):
            out[:, at : at + columns] = part[ends[i] : ends[i + 1]]


def hidden_middle(place, tokens, grads, extra, extra_other, weights):
    rows, width = tokens[0].shape
    hidden = extra.shape[2]
    total = 4 * rows
    return pl.pallas_call(
        hidden_middle_kernel,
        out_shape=(
            *(shape((n, width), BF16) for n in (rows, rows, rows, rows // 2, rows // 2)),
            *(shape((2, total, hidden), BF16),) * 3,
            shape((2, 8, hidden)),
        ),
        in_specs=[SMEM] + [VMEM] * 8 + [ANY] * 4,
        out_specs=(VMEM,) * 9,
        scratch_shapes=[
            pltpu.VMEM((total, width), BF16),
            pltpu.VMEM((2, 3, hidden, width), BF16),
            pltpu.SemaphoreType.DMA((12,)),
        ],
        compiler_params=PARAMS,
        cost_estimate=cost(20),
        name="hidden_middle",
    )(place, *tokens, grads, extra, extra_other, *weights)


def hidden_back_kernel(first, place, gate, upper, send, keep, pulled, swapped, *refs):
    *outs, total, backs, buffer, sems, back_sems = refs
    copies = hidden_copies(place, (send, keep, pulled, swapped), (0, 1), buffer, sems)
    rows = total.shape[0]
    back_copies = [
        pltpu.make_async_copy(
            source.at[c, pl.ds(first, rows)], backs.at[c, k], back_sems.at[2 * c + k]
        )
        for c in range(2)
        for k, source in enumerate((gate, upper))
    ]
    for i, copy in enumerate(back_copies):
        start_all([[copy], copies[2 * i : 2 * i + 2]])
    columns = 512
    for i, copy in enumerate(back_copies):
        wait_all([copy, *copies[2 * i : 2 * i + 2]])
        c, k = i // 2, i % 2
        for lanes in range(0, total.shape[1], columns):
            lane_at = slice(lanes, lanes + columns)
            part = dot(backs[c, k], buffer[c, k, :, lane_at])
            if i == 0:
                total[:, lane_at] = part
            elif i < 3:
                total[:, lane_at] += part
            else:
                part = (part + total[:, lane_at]).astype(BF16)
                at = 0
                for out in outs:
                    out[:, lane_at] = part[at : at + out.shape[0], :]
                    at += out.shape[0]


def hidden_back(far, place, gate, upper, weights, rows):
    width = weights[0].shape[2]
    hidden = gate.shape[2]
    counts = (rows // 2, rows // 2) if far else (rows, rows, rows)
    return pl.pallas_call(
        functools.partial(hidden_back_kernel, 3 * rows if far else 0),
        out_shape=tuple(shape((n, width), BF16) for n in counts),
        in_specs=[SMEM] + [ANY] * 6,
        out_specs=(VMEM,) * len(counts),
        scratch_shapes=[
            pltpu.VMEM((sum(counts), width), F32),
            pltpu.VMEM((2, 2, sum(counts), hidden), BF16),
            pltpu.VMEM((2, 2, hidden, width), BF16),
            pltpu.SemaphoreType.DMA((8,)),
            pltpu.SemaphoreType.DMA((4,)),
        ],
        compiler_params=PARAMS,
        cost_estimate=cost(8),
        name="hidden_back",
    )(place, gate, upper, *weights)


def hidden_grads_kernel(
    own, below, above, far_low, far_high, dz, act_in, gate_in, upper_in, sums, extra, extra_other, lefts_t,
    lefts_u, down_right, left_ref, down_ref, mine_ref, sent_ref, gate, upper, act, sems,
):
    copies = [
        pltpu.make_async_copy(source.at[c], target.at[c], sems.at[3 * c + i])
        for c in range(2)
        for i, (source, target) in enumerate(((gate_in, gate), (upper_in, upper), (act_in, act)))
    ]
    start_all([copies])
    tokens = jnp.concatenate([r[...] for r in (own, below, above, far_low, far_high)], axis=0)
    lows = dot_nt(jnp.concatenate([lefts_t[...], lefts_u[...]], axis=0), tokens)
    down_through = dot_nt(down_right[...], dz[...])
    throughs = [0.0, 0.0]
    low_down = 0.0
    for c, (factors, out) in enumerate(((extra, mine_ref), (extra_other, sent_ref))):
        for i, back in enumerate((gate, upper)):
            copies[3 * c + i].wait()
            throughs[i] += dot_nt(factors[i, 0:RANK, :], back[c])
            out[i * RANK : (i + 1) * RANK, :] = dot(lows[i * RANK : (i + 1) * RANK], back[c]).astype(
                out.dtype
            )
        copies[3 * c + 2].wait()
        low_down += dot_nt(factors[2, 0:RANK, :], act[c])
        out[2 * RANK : 3 * RANK, :] = dot(down_through, act[c]).astype(out.dtype)
        out[3 * RANK :, :] = jnp.concatenate(
            [sums[c], jnp.zeros_like(sums[c])], axis=0
        ).astype(out.dtype)
    through = jnp.concatenate(throughs, axis=0)
    left_ref[...] = dot(through, tokens)
    down_ref[...] = dot(low_down, dz[...])


def hidden_grads(tokens, dz, act, gate, upper, sums, extra, extra_other, lefts_t, lefts_u, down_right):
    width = dz.shape[1]
    hidden = act.shape[2]
    return pl.pallas_call(
        hidden_grads_kernel,
        out_shape=(
            shape((2 * RANK, width)),
            shape((RANK, width)),
            shape((4 * RANK, hidden)),
            shape((4 * RANK, hidden), BF16),
        ),
        in_specs=[VMEM] * 6 + [ANY] * 3 + [VMEM] * 6,
        out_specs=(VMEM,) * 4,
        scratch_shapes=[*(pltpu.VMEM(act.shape, BF16),) * 3, pltpu.SemaphoreType.DMA((6,))],
        compiler_params=PARAMS,
        cost_estimate=cost(8.4),
        name="hidden_grads",
    )(*tokens, dz, act, gate, upper, sums, extra, extra_other, lefts_t, lefts_u, down_right)


def half_copies(place, send, keep, planes, buffer, sems):
    half = buffer.shape[1] // 2
    copies = []
    for j, (source, which) in enumerate(((send, place[3]), (keep, 1 - place[3]))):
        rows = pl.ds(pl.multiple_of(which * half, half), half)
        copies.append(
            pltpu.make_async_copy(source.at[planes], buffer.at[:, rows], sems.at[j])
        )
    return copies


def hidden_norms_kernel(
    place, left, mine, other, extra, extra_other, lefts_t, lefts_u, send, keep, pulled, swapped,
    left_ref, cross_ref, weight, sems,
):
    copies = hidden_copies(place, (send, keep, pulled, swapped), (0, 1), weight, sems)
    start_all([copies])
    totals = [left[0:RANK, :], left[RANK : 2 * RANK, :]]
    for c, (factors, parts) in enumerate(((extra, mine), (extra_other, other))):
        for i, left_t in enumerate((lefts_t, lefts_u)):
            sums = parts[3 * RANK + i : 3 * RANK + i + 1, :].astype(F32)
            coefficient = -sums / factors[i, SQUARES : SQUARES + 1, :]
            wait_all(copies[4 * c + 2 * i : 4 * c + 2 * i + 2])
            totals[i] += dot(factors[i, 0:RANK, :] * coefficient, weight[c, i])
            if c == 0:
                cross_ref[i] = dot_nt(left_t[...], weight[c, i])
    left_ref[...] = FACTOR * jnp.concatenate(totals, axis=0)


def hidden_norms(place, left, mine, other, extra, extra_other, lefts_t, lefts_u, weights):
    width, hidden = left.shape[1], mine.shape[1]
    return pl.pallas_call(
        hidden_norms_kernel,
        out_shape=(shape((2 * RANK, width)), shape((2, RANK, hidden))),
        in_specs=[SMEM] + [VMEM] * 7 + [ANY] * 4,
        out_specs=(VMEM,) * 2,
        scratch_shapes=[
            pltpu.VMEM((2, 2, hidden, width), BF16),
            pltpu.SemaphoreType.DMA((8,)),
        ],
        compiler_params=PARAMS,
        cost_estimate=cost(9),
        name="hidden_norms",
    )(place, left, mine, other, extra, extra_other, lefts_t, lefts_u, *weights)


SPLIT_LANES = 256


def gathered_sums(received, tokens):
    sums = 0.0
    for t in range(received.shape[0]):
        sums += received[t, tokens + RANK : tokens + 2 * RANK, :].astype(F32)
    return jnp.concatenate(
        [
            jnp.concatenate([sums[8 * i + j : 8 * i + j + 1] for j in range(8)], axis=1)
            for i in range(2)
        ],
        axis=0,
    )


def split_grads_kernel(
    place, send, keep, grads, lows, heads_stats, heads_sums, heads_cross, mine, given, row, received,
    out_right, down_right, out_weight, attended, extra, cross, split_ref, down_weight, sems,
):
    copies = half_copies(place, send, keep, slice(2, 3), down_weight, sems)
    start_all([copies])
    width = row.shape[1]
    columns = heads_sums.shape[1] // 3
    slots, tokens = grads.shape[:2]
    row_sums = gathered_sums(received, tokens)
    above = 3 * RANK
    hidden = mine.shape[1]
    parts = mine[...] + given[...].astype(F32)
    hidden_rows = []
    for i in range(2):
        coefficient = -parts[3 * RANK + i : 3 * RANK + i + 1] / extra[i, SQUARES : SQUARES + 1, :]
        hidden_rows.append(
            FACTOR * (parts[i * RANK : (i + 1) * RANK] + cross[i] * coefficient)
        )
    split_ref[0:above, 0:hidden] = jnp.concatenate(
        [*hidden_rows, parts[3 * RANK :]], axis=0
    ).astype(BF16)
    split_ref[0:above, hidden:] = jnp.zeros((above, split_ref.shape[1] - hidden), BF16)
    split_ref[above:, 2 * SPLIT_LANES :] = jnp.zeros(
        (split_ref.shape[0] - above, split_ref.shape[1] - 2 * SPLIT_LANES), BF16
    )

    def put(lanes, values):
        split_ref[above:, lanes] = values.astype(BF16)

    coefficient = -heads_sums[0:1, :] / heads_stats[0:1, :]
    first = []
    for i in range(3):
        at = slice(i * columns, (i + 1) * columns)
        dz = jnp.concatenate([grads[s, :, at] for s in range(slots)], axis=0)
        first.append(
            FACTOR
            * (
                jnp.dot(lows[i * RANK : (i + 1) * RANK, :], dz, preferred_element_type=F32)
                + heads_cross[:, at] * coefficient[:, at]
            )
        )
    out_coefficient, down_coefficient = (
        -row_sums[i : i + 1, :] / row[i : i + 1, :] for i in range(2)
    )
    out_left = 0.0
    for t in range(received.shape[0]):
        through = received[t, tokens : tokens + RANK, 0:tokens]
        out_left += dot(through, attended[t, 0:tokens, :])
    first.append(FACTOR * (out_left + dot_nt(out_right[...] * out_coefficient, out_weight[...])))
    first.append(jnp.zeros((RANK, SPLIT_LANES), F32))
    put(slice(0, SPLIT_LANES), jnp.concatenate(first, axis=0))
    at = slice(2 * RANK, 3 * RANK)
    wait_all(copies)
    down_left = FACTOR * (
        parts[at, :] + dot_nt(down_right[...] * down_coefficient, down_weight[0])
    )
    hidden = down_left.shape[1]
    padded = (hidden + SPLIT_LANES - 1) // SPLIT_LANES * SPLIT_LANES
    down_left = jnp.concatenate([down_left, jnp.zeros((RANK, padded - hidden), F32)], axis=1)
    second = [
        down_left[:, j * SPLIT_LANES : (j + 1) * SPLIT_LANES] for j in range(padded // SPLIT_LANES)
    ]
    second += [
        row_sums[i : i + 1, j * SPLIT_LANES : (j + 1) * SPLIT_LANES]
        for i in range(2)
        for j in range(width // SPLIT_LANES)
    ]
    second += [heads_sums[0:1, i * columns : (i + 1) * columns] for i in range(3)]
    used = sum(r.shape[0] for r in second)
    second.append(jnp.zeros((5 * RANK - used, SPLIT_LANES), F32))
    put(slice(SPLIT_LANES, 2 * SPLIT_LANES), jnp.concatenate(second, axis=0))


def tail_kernel(*refs):
    inputs, (weight, *rest) = refs[:18], refs[18:]
    outs, (split_ref, dz, buffer, sems, down_weight, down_sems) = rest[:-6], rest[-6:]
    heads_back_kernel(inputs[3], weight, *outs, dz, buffer, sems)
    split_grads_kernel(*inputs, split_ref, down_weight, down_sems)


def tail(arrays, weight):
    half, width = arrays[1].shape[1:]
    above, lanes = 3 * RANK, (2 * half + LANES - 1) // LANES * LANES
    blocks, rows, columns = arrays[3].shape
    chunks = 4
    return pl.pallas_call(
        tail_kernel,
        out_shape=(
            *(shape((rows, width), BF16),) * blocks,
            shape((above + 5 * RANK, lanes), BF16),
        ),
        in_specs=[SMEM, ANY, ANY] + [VMEM] * (len(arrays) - 3) + [ANY],
        out_specs=(VMEM,) * (blocks + 1),
        scratch_shapes=[
            pltpu.VMEM((blocks * rows, columns), BF16),
            pltpu.VMEM((chunks, width // chunks, columns), BF16),
            pltpu.SemaphoreType.DMA((chunks,)),
            pltpu.VMEM((1, 2 * half, width), BF16),
            pltpu.SemaphoreType.DMA((2,)),
        ],
        compiler_params=PARAMS,
        cost_estimate=cost(13),
        name="tail",
    )(*arrays, weight)


def unpack_kernel(total, *outs):
    lane_blocks = outs[0].shape[1] // LANES
    for group, out in enumerate(outs):
        for i in range(lane_blocks):
            out[:, i * LANES : (i + 1) * LANES] = total[group * lane_blocks + i].astype(F32)


def unpack(total, count, width):
    return pl.pallas_call(
        unpack_kernel,
        out_shape=(shape((RANK, width)),) * count,
        in_specs=[VMEM],
        out_specs=(VMEM,) * count,
        compiler_params=PARAMS,
        cost_estimate=cost(2),
        name="unpack",
    )(total)


def shared_grads_kernel(
    grads, heads_weight, heads_stats, heads_sums, qr, kr, vr, left, down, row, received,
    row_cross, arrived, out_dz, *refs,
):
    *blocks, terms_ref = refs
    tokens, width = out_dz.shape
    row_sums = gathered_sums(received, tokens)

    def put(group, rows):
        rows = rows.astype(BF16)
        lane_blocks = width // LANES
        for i in range(lane_blocks):
            terms_ref[group * lane_blocks + i] = rows[:, i * LANES : (i + 1) * LANES]

    columns = heads_weight.shape[1] // 3
    coefficient = -heads_sums[0:1, :] / heads_stats[0:1, :]
    throughs, norms = [], []
    for i, right in enumerate((qr, kr, vr)):
        at = slice(i * columns, (i + 1) * columns)
        dz = jnp.concatenate([grads[s, :, at] for s in range(len(blocks))], axis=0)
        throughs.append(dot_nt(right[...], dz))
        norms.append(right[...] * coefficient[:, at])
    through = jnp.concatenate(throughs, axis=0).astype(BF16)
    total = 0.0
    for s in range(0, len(blocks), 2):
        pair = jnp.concatenate([blocks[s][...], blocks[s + 1][...]], axis=0)
        total += jnp.dot(
            through[:, s * tokens : (s + 2) * tokens], pair, preferred_element_type=F32
        )
    for i in range(3):
        at = slice(i * columns, (i + 1) * columns)
        rows = total[i * RANK : (i + 1) * RANK]
        put(i, FACTOR * (rows + dot_nt(norms[i], heads_weight[:, at])))
    put(3, left[0:RANK, :])
    put(4, left[RANK : 2 * RANK, :])
    out_coefficient, down_coefficient = (
        -row_sums[i : i + 1, :] / row[i : i + 1, :] for i in range(2)
    )
    low = 0.0
    for t in range(arrived.shape[0]):
        low += dot_nt(arrived[t, tokens : tokens + RANK, :], arrived[t, 0:tokens, :])
    put(5, FACTOR * (dot(low, out_dz[...]) + row_cross[0] * out_coefficient))
    put(6, FACTOR * (down[...] + row_cross[1] * down_coefficient))
    put(7, jnp.zeros((RANK, width), F32))


def shared_grads(arrays, blocks):
    width = blocks[0].shape[1]
    return pl.pallas_call(
        shared_grads_kernel,
        out_shape=shape((8 * width // LANES, RANK, LANES), BF16),
        in_specs=[VMEM] * (len(arrays) + len(blocks)),
        out_specs=VMEM,
        compiler_params=PARAMS,
        cost_estimate=cost(8),
        name="shared_grads",
    )(*arrays, *blocks)


def on_device(
    hidden_in,
    segment_ids,
    attention_gain,
    mlp_gain,
    query_base,
    query_left,
    query_right,
    query_magnitude,
    key_base,
    key_left,
    key_right,
    key_magnitude,
    value_base,
    value_left,
    value_right,
    value_magnitude,
    output_base,
    output_left,
    output_right,
    output_magnitude,
    gate_base,
    gate_left,
    gate_right,
    gate_magnitude,
    up_base,
    up_left,
    up_right,
    up_magnitude,
    down_base,
    down_left,
    down_right,
    down_magnitude,
    cotangent,
):
    resid = hidden_in[0]
    cot = cotangent[0]
    rows, width = resid.shape
    segments = segment_ids[0]
    length = segments.shape[0]
    heads_width = query_base.shape[1]
    hidden = gate_base.shape[1]
    mlp_row = mlp_gain[None]
    zero_count = jnp.sum((segments == 0).astype(jnp.int32))
    one_count = jnp.sum((segments <= 1).astype(jnp.int32))
    place = jnp.stack(
        [lax.axis_index(a).astype(jnp.int32) for a in ("z", "xl", "y", "core")]
        + [zero_count, one_count]
    )

    _, _, normed_one = rms_forward(resid.astype(F32), attention_gain)
    other, below, above = x_swap(normed_one), z_up(normed_one), z_down(normed_one)

    piece = output_piece(after(place, normed_one), output_base, output_left.T, output_right)
    received = all_to_all(piece, TENSOR)

    hidden_bases = (gate_base.T, up_base.T, down_base)
    hidden_lefts = (gate_left.T, up_left.T, down_left.T)
    hidden_rights = (gate_right, up_right, down_right)
    heads_magnitude = jnp.concatenate([query_magnitude, key_magnitude, value_magnitude])[None]
    hidden_send, *hidden_sent = prepare_send(
        after(place, piece), hidden_bases, hidden_lefts, hidden_rights
    )
    other, below, above, hidden_send = lax.optimization_barrier((other, below, above, hidden_send))

    other_below, other_above = z_up(other), z_down(other)
    pulled = from_x_neighbour(hidden_send)
    starts = jnp.where(segments == 0, 0, jnp.where(segments == 1, zero_count, one_count))
    positions = (jnp.arange(length, dtype=jnp.int32) - after(starts, other)).astype(F32)
    frequency = 10000.0 ** (-jnp.arange(0, HEAD_DIM, 2, dtype=F32) / HEAD_DIM)
    angles = positions[:, None] * frequency[None, :]
    cosine, sine = jnp.cos(angles), jnp.sin(angles)
    cosine = jnp.concatenate([cosine, cosine], axis=-1)
    sine = jnp.concatenate([-sine, sine], axis=-1)

    received = after(received, cosine, sine)
    heads_weight, heads_stats, heads_cross = prepare_heads(
        (query_base, key_base, value_base),
        (query_left.T, key_left.T, value_left.T),
        (query_right, key_right, value_right),
        after(heads_magnitude, received, other),
    )
    out_mine = of_everyone(received.reshape(width, piece.shape[2]), "y")
    other_below, other_above, below, second_place, _ = lax.optimization_barrier(
        (other_below, other_above, below, place, heads_stats)
    )
    other_far, far_one = z_down(other_above), z_up(below)
    hidden_magnitude = jnp.stack([gate_magnitude, up_magnitude])
    hidden_keep, out_weight, extra, row_cross, row_terms, near = prepare_second(
        second_place,
        hidden_bases,
        hidden_lefts,
        hidden_rights,
        (output_base, output_left.T, output_right),
        hidden_magnitude,
        hidden_sent,
        (normed_one, other, below, above, heads_weight, heads_stats, cosine, sine),
    )
    other_far, far_one, far_place, cot_held, extra = lax.optimization_barrier(
        (other_far, far_one, place, cot, extra)
    )
    extra_other = x_swap(extra)
    cot_near = (z_up(cot_held), z_down(cot_held))
    row_blocks = [
        normed_one, other, below, above, other_below, other_above, far_one, other_far
    ]
    far = project_heads(4, far_place, row_blocks[4:], heads_weight, heads_stats, cosine, sine)
    *cot_near, extra_other, attend_place, _ = lax.optimization_barrier(
        (*cot_near, extra_other, place, far)
    )
    half_rows = rows // 2
    cot_all = (
        cot,
        *cot_near,
        z_up(cot_near[0][:half_rows]),
        z_down(cot_near[1][half_rows:]),
    )
    attended, logs = attend(attend_place, near, far, row_terms)
    attended, *cot_ends = lax.optimization_barrier((attended, *cot_all[3:]))
    cot_all = (*cot_all[:3], *cot_ends)
    row_magnitude = jnp.stack([output_magnitude, down_magnitude])
    out_mine = after(out_mine, attended)
    out_columns = (out_mine, core_swap(out_mine))
    arrived = all_to_all(attended, TENSOR)
    swapped = core_swap(after(pulled, attended))

    out_raw, resid_two, normed_two, row = output_forward(
        place, arrived, resid, row_magnitude, mlp_row, out_columns
    )
    hidden_weights = (hidden_send, hidden_keep, pulled, swapped)
    grad_activated, down_dz = hidden_start(place, cot_all, row, hidden_weights)
    heads_lows = low_terms(
        (after(query_left.T, grad_activated), key_left.T, value_left.T), row_blocks
    )
    tokens = gather_z(normed_two, lambda: grad_activated)
    tokens = (*tokens[:3], *lax.optimization_barrier((*tokens[3:], heads_lows))[:2])
    *forward, act, gate_back, up_back, hidden_sums = hidden_middle(
        place, tokens, grad_activated, extra, extra_other, hidden_weights
    )
    far_parts = hidden_back(
        True, after(place, forward[0]), gate_back, up_back, hidden_weights, rows
    )
    forward = scatter_z(*forward, lambda: far_parts[0])
    near_parts = hidden_back(
        False, after(place, far_parts[0], forward[3]), gate_back, up_back, hidden_weights, rows
    )
    back = scatter_z(*near_parts, *far_parts, lambda: (near_parts[0], forward[1], forward[2]))
    hidden_terms = hidden_grads(
        tokens,
        after(down_dz, back[3]),
        act,
        gate_back,
        up_back,
        hidden_sums,
        extra,
        extra_other,
        gate_left.T,
        up_left.T,
        down_right,
    )
    gate_up_left, down_right_part, mine, sent = hidden_terms
    grad_two, out_dz, head_part, layer = output_back(
        after(place, mine),
        back[:3],
        forward[:3],
        cot,
        out_raw,
        resid_two,
        row,
        mlp_row,
        output_right,
        out_columns,
        8,
    )
    given = x_swap(sent)
    gate_up_left, hidden_cross = hidden_norms(
        after(place, head_part),
        gate_up_left,
        mine,
        sent,
        extra,
        extra_other,
        gate_left.T,
        up_left.T,
        hidden_weights,
    )
    received = after(all_to_all(head_part, TENSOR), gate_up_left, given)

    heads_dz, heads_sums = attend_back(
        place, near, far, logs, received, cosine, sine, heads_stats
    )
    *parts, split = tail(
        (
            place,
            hidden_send,
            hidden_keep,
            heads_dz,
            heads_lows,
            heads_stats,
            heads_sums,
            heads_cross,
            mine,
            given,
            row,
            received,
            output_right,
            down_right,
            out_weight,
            attended,
            extra,
            hidden_cross,
        ),
        heads_weight,
    )
    terms = shared_grads(
        (
            after(heads_dz, parts[0]),
            heads_weight,
            heads_stats,
            heads_sums,
            query_right,
            key_right,
            value_right,
            gate_up_left,
            down_right_part,
            row,
            received,
            row_cross,
            arrived,
            out_dz,
        ),
        row_blocks,
    )
    hop, other_hop = z_up(parts[6]), z_down(parts[7])
    other_from_below = z_up(parts[5])
    from_above = z_down(parts[2])
    hop, other_hop, other_from_below, from_above, _ = lax.optimization_barrier(
        (hop, other_hop, other_from_below, from_above, terms)
    )
    other_part = add(parts[4], other_hop).astype(BF16)
    other_from_above = z_down(other_part)
    from_below = z_up(add(parts[3], hop).astype(BF16))
    split = add(split, core_swap(split)).astype(BF16)
    split = add(split, lax.ppermute(split, "xh", SWAP)).astype(BF16)
    split = add(split, lax.ppermute(split, "y", ((0, 1), (1, 0), (2, 3), (3, 2)))).astype(BF16)
    total = after(all_to_all(terms, ALL), other_part, split).astype(F32).sum(axis=0).astype(BF16)
    split_other = lax.ppermute(split, "y", ((0, 2), (2, 0), (1, 3), (3, 1)))
    other_from_above, split_other = lax.optimization_barrier((other_from_above, split_other))
    split = add(split, split_other)
    across = add(parts[1], other_from_below, other_from_above).astype(BF16)
    split = after(split, across)
    grad_normed_one = add(parts[0], from_below, from_above, x_swap(across))
    resid = resid.astype(F32)
    inverse = lax.rsqrt(jnp.mean(resid * resid, axis=-1, keepdims=True) + EPSILON)
    input_grad = grad_two + rms_backward(grad_normed_one, resid * inverse, inverse, attention_gain)
    hidden_split, split = split[: 3 * RANK, :hidden], split[3 * RANK :]
    total = unpack(after(of_everyone(total, ALL), other_from_above).reshape(-1, RANK, LANES), 7, width)
    hidden_magnitude_grad = hidden_split[2 * RANK : 2 * RANK + 2] / hidden_magnitude
    heads, rest = split[:, :SPLIT_LANES], split[:, SPLIT_LANES : 2 * SPLIT_LANES]
    parts = (hidden + SPLIT_LANES - 1) // SPLIT_LANES
    down_left_grad = jnp.concatenate([rest[i * RANK : (i + 1) * RANK] for i in range(parts)], axis=1)
    at = parts * RANK
    row_magnitude_grad = rest[at : at + 2 * width // SPLIT_LANES].reshape(2, width) / row_magnitude
    at += 2 * width // SPLIT_LANES
    heads_magnitude_grad = rest[at : at + 3] / heads_magnitude.reshape(3, -1)
    return (
        layer[None],
        input_grad[None],
        total[0].T,
        heads[:RANK],
        heads_magnitude_grad[0],
        total[1].T,
        heads[RANK : 2 * RANK],
        heads_magnitude_grad[1],
        total[2].T,
        heads[2 * RANK : 3 * RANK],
        heads_magnitude_grad[2],
        heads[3 * RANK : 4 * RANK].T,
        total[5],
        row_magnitude_grad[0],
        total[3].T,
        hidden_split[:RANK],
        hidden_magnitude_grad[0],
        total[4].T,
        hidden_split[RANK : 2 * RANK],
        hidden_magnitude_grad[1],
        down_left_grad[:, :hidden].T,
        total[6],
        row_magnitude_grad[1],
    )


def solution(mesh):
    torus = Mesh(mesh.devices.reshape(4, 2, 2, 4, 2), ("y", "xh", "core", "z", "xl"))
    column = (P(None, TENSOR), P(), P(None, TENSOR), P(TENSOR))
    row = (P(TENSOR, None), P(TENSOR, None), P(), P())
    column_out, row_out = column[1:], row[1:]
    tokens = P(DP, TENSOR, None)
    return jax.shard_map(
        on_device,
        mesh=torus,
        in_specs=(
            tokens,
            P(DP, None),
            P(),
            P(),
            *column,
            *column,
            *column,
            *row,
            *column,
            *column,
            *row,
            tokens,
        ),
        out_specs=(
            tokens,
            tokens,
            *column_out,
            *column_out,
            *column_out,
            *row_out,
            *column_out,
            *column_out,
            *row_out,
        ),
        check_vma=False,
    )
```
